32 devices in a mesh: section: 2 (over core), seq: 4 (over y, x), head: 4 (over z).
Axes of the slice: x: 2, y: 2, z: 4, core: 2. Of those that a mesh axis runs over, the one named last changes fastest.
Arguments:
- layer_input: bfloat16 [4, 2048, 1536], P(None, 'seq'), may hold values from -6 to 6
- cotangent: bfloat16 [4, 2048, 1536], P(None, 'seq'), may hold values from -6 to 6
- pre_gain: float32 [2, 1536], P('section'), may hold values from 0.5 to 1.5
- proj_zx: bfloat16 [2, 1536, 2, 3072], P('section', None, None, 'head'), may hold values from -0.15625 to 0.15625
- proj_bc: bfloat16 [2, 1536, 256], P('section'), may hold values from -0.15625 to 0.15625
- proj_dt: bfloat16 [2, 1536, 48], P('section', None, 'head'), may hold values from -0.15625 to 0.15625
- kernel_inner: float32 [2, 4, 3072], P('section', None, 'head'), may hold values from -0.5 to 0.5
- bias_inner: float32 [2, 3072], P('section', 'head'), may hold values from -0.5 to 0.5
- kernel_state: float32 [2, 4, 256], P('section'), may hold values from -0.5 to 0.5
- bias_state: float32 [2, 256], P('section'), may hold values from -0.5 to 0.5
- step_bias: float32 [2, 48], P('section', 'head'), may hold values from -4 to -2
- decay_log: float32 [2, 48], P('section', 'head'), may hold values from -8 to 0
- skip_gain: float32 [2, 48], P('section', 'head'), may hold values from 0.5 to 1.5
- norm_gain: float32 [2, 3072], P('section', 'head'), may hold values from 0.5 to 1.5
- proj_out: bfloat16 [2, 3072, 1536], P('section', 'head'), may hold values from -0.109375 to 0.109375
Outputs:
- layer_out: bfloat16 [2, 4, 2048, 1536], P('section', None, 'seq')
- layer_grad: bfloat16 [2, 4, 2048, 1536], P('section', None, 'seq')
- grad_pre_gain: float32 [2, 1536], P('section', 'seq')
- grad_proj_zx: float32 [2, 1536, 2, 3072], P('section', 'seq', None, 'head')
- grad_proj_bc: float32 [2, 1536, 256], P('section', ('seq', 'head'))
- grad_proj_dt: float32 [2, 1536, 48], P('section', 'seq', 'head')
- grad_kernel_inner: float32 [2, 4, 3072], P('section', None, 'head')
- grad_bias_inner: float32 [2, 3072], P('section', 'head')
- grad_kernel_state: float32 [2, 4, 256], P('section', None, ('seq', 'head'))
- grad_bias_state: float32 [2, 256], P('section', ('seq', 'head'))
- grad_step_bias: float32 [2, 48], P('section', 'head')
- grad_decay_log: float32 [2, 48], P('section', 'head')
- grad_skip_gain: float32 [2, 48], P('section', 'head')
- grad_norm_gain: float32 [2, 3072], P('section', 'head')
- grad_proj_out: float32 [2, 3072, 1536], P('section', 'head', 'seq')
The draws below stay inside these ranges and needn't reach their ends.
All inputs are finite; a program needn't handle non-finite values.
Results may differ from the reference program's by a relative error of at most 0.019.
The reference program's roundings to bfloat16 on the way (of `normed` and `normed_out`) count: a program that leaves them out, or rounds other values in their place, can miss the bound.
Values may be sent and summed in bfloat16 or wider, within the bound.
No kernel may reach another device: no remote copies, remote signals or barrier semaphores. Data moves between devices by JAX's collectives and lax.ppermute only.
A program may use at most 320 MiB of HBM per device.

```python
import math
from functools import partial
import jax
import jax.numpy as jnp
from jax import lax

D = 1536
H = 48
P_SIZE = 64
NS = 128
CONV = 4
GROUP = 256
MICRO = 4
DI = 3072
LAYERS = 2
LENGTH = 2048


def draw_decay_log(key, part):
    key = jax.random.fold_in(key, 7)
    pick_key, fast_key, slow_key = jax.random.split(key, 3)
    share = 0.5
    slow_heads = jax.random.uniform(pick_key, (LAYERS, H), jnp.float32) < share
    fast_values = jax.random.uniform(fast_key, (LAYERS, H), jnp.float32, math.log(0.25), 0.0)
    slow_values = math.log(40.0 / LENGTH) + jax.random.uniform(slow_key, (LAYERS, H), jnp.float32, math.log(0.2), 0.0)
    return jnp.where(slow_heads, slow_values, fast_values).astype(jnp.float32)


def block_levels(own_key, shape, shards, least, top_value):
    gain = 1.0
    for axis_at, blocks in shards:
        steps = jax.random.uniform(jax.random.fold_in(jax.random.fold_in(own_key, 6), axis_at), (blocks,), jnp.float32, least / len(shards), top_value / len(shards))
        gain = gain * jnp.repeat(jnp.exp(steps), shape[axis_at] // blocks).reshape((-1,) + (1,) * (len(shape) - 1 - axis_at))
    return gain


def gaussian(key, shape, spread, limit, cuts=(), dtype=jnp.bfloat16):
    drawn = jax.random.normal(key, shape, jnp.float32) * spread
    if len(cuts) > 0:
        drawn = block_levels(key, shape, cuts, -0.22, 0.18) * drawn
    return jnp.clip(drawn, min=-limit, max=limit).astype(dtype)


def setup_inputs(seed: int = 0) -> dict:
    key_list = jax.random.split(jax.random.key(seed), 16)
    layer_input = gaussian(key_list[0], (MICRO, LENGTH, D), 1.0, 6.0, ((1, 4),))
    cotangent = gaussian(key_list[1], (MICRO, LENGTH, D), 1.0, 6.0, ((1, 4),))
    pre_gain = jnp.clip(1.0 + 0.1 * jax.random.normal(key_list[2], (LAYERS, D), jnp.float32), 0.5, 1.5)
    proj_zx = gaussian(key_list[3], (LAYERS, D, 2, DI), D ** -0.5, 0.15625, ((0, 2), (3, 4)))
    proj_bc = gaussian(key_list[4], (LAYERS, D, 2 * NS), D ** -0.5, 0.15625, ((0, 2),))
    proj_dt = gaussian(key_list[5], (LAYERS, D, H), D ** -0.5, 0.15625, ((0, 2), (2, 4)))
    kernel_inner = jnp.clip(jax.random.uniform(key_list[6], (LAYERS, CONV, DI), jnp.float32, -0.5, 0.5) * block_levels(key_list[6], (LAYERS, CONV, DI), ((0, 2), (2, 4)), -0.4, 0.0), -0.5, 0.5)
    bias_inner = jnp.clip(jax.random.uniform(key_list[7], (LAYERS, DI), jnp.float32, -0.5, 0.5) * block_levels(key_list[7], (LAYERS, DI), ((0, 2), (1, 4)), -0.4, 0.0), -0.5, 0.5)
    kernel_state = jnp.clip(jax.random.uniform(key_list[8], (LAYERS, CONV, 2 * NS), jnp.float32, -0.5, 0.5) * block_levels(key_list[8], (LAYERS, CONV, 2 * NS), ((0, 2),), -0.4, 0.0), -0.5, 0.5)
    bias_state = jnp.clip(jax.random.uniform(key_list[9], (LAYERS, 2 * NS), jnp.float32, -0.5, 0.5) * block_levels(key_list[9], (LAYERS, 2 * NS), ((0, 2),), -0.4, 0.0), -0.5, 0.5)
    step_bias = jnp.clip(-4.0 + 2.0 * jax.random.uniform(key_list[10], (LAYERS, H), jnp.float32) ** block_levels(key_list[10], (LAYERS, H), ((0, 2), (1, 4)), -0.2, 0.2), -4.0, -2.0)
    decay_log = draw_decay_log(jax.random.fold_in(key_list[15], 71), 0)
    skip_gain = jnp.clip(0.5 + 1.0 * jax.random.uniform(key_list[12], (LAYERS, H), jnp.float32) ** block_levels(key_list[12], (LAYERS, H), ((0, 2), (1, 4)), -0.2, 0.2), 0.5, 1.5)
    norm_gain = jnp.clip(1.0 + 0.1 * jax.random.normal(key_list[13], (LAYERS, DI), jnp.float32), 0.5, 1.5)
    proj_out = gaussian(key_list[14], (LAYERS, DI, D), DI ** -0.5, 0.109375, ((0, 2), (1, 4)))
    return {"layer_input": layer_input, "cotangent": cotangent, "pre_gain": pre_gain, "proj_zx": proj_zx, "proj_bc": proj_bc, "proj_dt": proj_dt, "kernel_inner": kernel_inner, "bias_inner": bias_inner, "kernel_state": kernel_state, "bias_state": bias_state, "step_bias": step_bias, "decay_log": decay_log, "skip_gain": skip_gain, "norm_gain": norm_gain, "proj_out": proj_out}


EPS = 1e-05
HIGH = lax.Precision.HIGHEST

@jax.custom_vjp
def low(v):
    return lax.optimization_barrier(v.astype(jnp.bfloat16)).astype(jnp.float32)

@jax.custom_vjp
def low_back(v):
    return v

def low_keep(v):
    return (low(v), None)

def low_pass(kept, grad):
    return (grad,)

def back_keep(v):
    return (v, None)

def back_low(kept, grad):
    return (low(grad),)
low.defvjp(low_keep, low_pass)
low_back.defvjp(back_keep, back_low)

def block_step_fn(decay_log, skip_gain, state_now, element):
    values, keys_state, reads_state, steps = element
    log_rates = -steps * jnp.exp(decay_log)[None, :]
    within = jnp.cumsum(log_rates, axis=0)
    causal = jnp.arange(GROUP)[:, None] >= jnp.arange(GROUP)[None, :]
    gap_sums = jnp.where(causal[:, :, None], within[:, None, :] - within[None, :, :], 0.0)
    decays = jnp.where(causal[:, :, None], jnp.exp(gap_sums), 0.0)
    scores = jnp.dot(reads_state, keys_state.T, precision=HIGH)
    weights = decays * scores[:, :, None] * steps[None, :, :]
    output = jnp.einsum('ijh,jhp->ihp', weights, values, precision=HIGH)
    output = output + jnp.einsum('ih,in,hpn->ihp', jnp.exp(within), reads_state, state_now, precision=HIGH)
    output = output + skip_gain[None, :, None] * values
    tail_decay = jnp.exp(within[-1:, :] - within) * steps
    state_next = jnp.exp(within[-1])[:, None, None] * state_now + jnp.einsum('jh,jhp,jn->hpn', tail_decay, values, keys_state, precision=HIGH)
    return (state_next, output)

def layer(params, rows):
    pre_gain, proj_zx, proj_bc, proj_dt, kernel_inner, bias_inner, kernel_state, bias_state, step_bias, decay_log, skip_gain, norm_gain, proj_out = params
    length_rows = rows.shape[0]
    normed = low(rows * lax.rsqrt(lax.optimization_barrier(jnp.mean(rows * rows, axis=1, keepdims=True)) + EPS) * pre_gain)
    gate_value = jnp.einsum('td,dkc->tkc', normed, proj_zx, precision=HIGH)
    gate_pre = low_back(gate_value[:, 0])
    inner_pre = low_back(gate_value[:, 1])
    state_pre = jnp.dot(normed, proj_bc, precision=HIGH)
    step_raw = low_back(jnp.dot(normed, proj_dt, precision=HIGH))
    mixed_in = jnp.concatenate([inner_pre, state_pre], axis=1)
    kernel = jnp.concatenate([kernel_inner, kernel_state], axis=1)
    padded = jnp.pad(mixed_in, ((CONV - 1, 0), (0, 0)))
    shift_sum = jnp.concatenate([bias_inner, bias_state])[None, :]
    for offset in range(CONV):
        shift_sum = shift_sum + kernel[offset][None, :] * padded[offset:offset + length_rows]
    activated = jax.nn.silu(shift_sum)
    steps = jax.nn.softplus(step_raw + step_bias[None, :])
    blocks = length_rows // GROUP
    values = activated[:, :DI].reshape(blocks, GROUP, H, P_SIZE)
    keys_state = activated[:, DI:DI + NS].reshape(blocks, GROUP, NS)
    reads_state = activated[:, DI + NS:].reshape(blocks, GROUP, NS)
    block_step = jax.checkpoint(partial(block_step_fn, decay_log, skip_gain))
    _, output = lax.scan(block_step, jnp.zeros((H, P_SIZE, NS), jnp.float32), (values, keys_state, reads_state, steps.reshape(blocks, GROUP, H)))
    output = output.reshape(length_rows, DI)
    gated = output * jax.nn.silu(gate_pre)
    normed_out = low(gated * lax.rsqrt(lax.optimization_barrier(jnp.mean(gated * gated, axis=1, keepdims=True)) + EPS) * norm_gain)
    return low_back(low(rows + jnp.dot(normed_out, proj_out, precision=HIGH)))

def run_layer(params, rows_all):
    return lax.map(partial(layer, params), rows_all)

def reference(layer_input, cotangent, pre_gain, proj_zx, proj_bc, proj_dt, kernel_inner, bias_inner, kernel_state, bias_state, step_bias, decay_log, skip_gain, norm_gain, proj_out):
    stacked = (pre_gain, proj_zx, proj_bc, proj_dt, kernel_inner, bias_inner, kernel_state, bias_state, step_bias, decay_log, skip_gain, norm_gain, proj_out)
    current = layer_input.astype(jnp.float32)
    outputs = []
    pullbacks = []
    for layer_index in range(LAYERS):
        params = tuple((weight[layer_index].astype(jnp.float32) for weight in stacked))
        current, pullback = jax.vjp(run_layer, params, current)
        outputs.append(current)
        pullbacks.append(pullback)
    flowing = cotangent.astype(jnp.float32)
    grads = [None] * LAYERS
    inputs_grad = [None] * LAYERS
    for layer_index in reversed(range(LAYERS)):
        grads[layer_index], flowing = pullbacks[layer_index](flowing)
        inputs_grad[layer_index] = flowing
    per_weight = [jnp.stack([grads[layer_index][member] for layer_index in range(LAYERS)]) for member in range(13)]
    return (jnp.stack(outputs).astype(jnp.bfloat16), jnp.stack(inputs_grad).astype(jnp.bfloat16), per_weight[0], per_weight[1], per_weight[2], per_weight[3], per_weight[4], per_weight[5], per_weight[6], per_weight[7], per_weight[8], per_weight[9], per_weight[10], per_weight[11], per_weight[12])
```

```python
from functools import partial

import jax
import jax.numpy as jnp
from jax import lax
from jax.experimental import pallas as pl
from jax.experimental.pallas import tpu as pltpu
from jax.sharding import PartitionSpec as P

P_SIZE = 64
NS = 128
GROUP = 256
LANES = 128
EDGE = 8
PACK = 16
BLOCK = 256

EPS = 1e-05
HIGH = lax.Precision.HIGHEST
F32 = jnp.float32
BF16 = jnp.bfloat16
VMEM_LIMIT = 60 * 1024 * 1024
WIRE = F32
COST = pl.CostEstimate(flops=1_000_000, bytes_accessed=1_000_000, transcendentals=0)

NN = (((1,), (0,)), ((), ()))
NT = (((1,), (1,)), ((), ()))
TN = (((0,), (0,)), ((), ()))


def call(kernel, after, grid, in_specs, out_specs, out_shape, name, scratch_shapes=(), prefetch=0):
    count = prefetch + len(in_specs)

    def body(*refs):
        kernel(*refs[:count], *refs[count + len(after) :])

    return pl.pallas_call(
        body,
        grid_spec=pltpu.PrefetchScalarGridSpec(
            num_scalar_prefetch=prefetch,
            grid=grid,
            in_specs=[*in_specs, *[pl.BlockSpec(memory_space=pl.ANY)] * len(after)],
            out_specs=out_specs,
            scratch_shapes=scratch_shapes,
        ),
        out_shape=out_shape,
        compiler_params=pltpu.CompilerParams(vmem_limit_bytes=VMEM_LIMIT),
        cost_estimate=COST,
        name=name,
    )


def low_dot(a, b, dims):
    return lax.dot_general(a.astype(BF16), b.astype(BF16), dims, preferred_element_type=F32)


def high_dot(a, b, dims):
    return lax.dot_general(a, b, dims, precision=HIGH, preferred_element_type=F32)


def iota(shape, dim):
    return lax.broadcasted_iota(jnp.int32, shape, dim)


def softplus(v):
    return jnp.maximum(v, 0.0) + jnp.log1p(jnp.exp(-jnp.abs(v)))


def sigmoid(v):
    return 1.0 / (1.0 + jnp.exp(-v))


def column(values, lane):
    return jnp.sum(jnp.where(iota(values.shape, 1) == lane, values, 0.0), axis=1, keepdims=True)


def convolve(ext_ref, kernel_ref, bias_ref, rows):
    taps = kernel_ref.shape[0]
    total = bias_ref[...] + kernel_ref[0:1, :] * ext_ref[EDGE - taps + 1 : EDGE - taps + 1 + rows, :]
    for k in range(1, taps):
        at = EDGE - taps + 1 + k
        total = total + kernel_ref[k : k + 1, :] * ext_ref[at : at + rows, :]
    return total


def convolve_back(grad_ref, ext_ref, kernel_ref, grad, rows):
    taps = kernel_ref.shape[0]
    width = grad.shape[1]
    grad_ref[0:EDGE, :] = jnp.zeros((EDGE, width), F32)
    grad_ref[EDGE : EDGE + rows, :] = grad
    grad_ref[EDGE + rows :, :] = jnp.zeros((EDGE, width), F32)
    total = kernel_ref[0:1, :] * grad_ref[taps - 1 : taps - 1 + rows + EDGE, :]
    for k in range(1, taps):
        at = taps - 1 - k
        total = total + kernel_ref[k : k + 1, :] * grad_ref[at : at + rows + EDGE, :]
    small = []
    for k in range(taps):
        at = EDGE - taps + 1 + k
        small.append(jnp.sum(grad * ext_ref[at : at + rows, :], axis=0, keepdims=True))
    small.append(jnp.sum(grad, axis=0, keepdims=True))
    return total, small


def chunk_sums(steps, decay_log, rows):
    rates = -steps * jnp.exp(decay_log)
    lower = jnp.where(iota((GROUP, GROUP), 0) >= iota((GROUP, GROUP), 1), 1.0, 0.0)
    parts = [high_dot(lower, rates[at : at + GROUP], NN) for at in range(0, rows, GROUP)]
    return rates, jnp.concatenate(parts, axis=0)


def pair_select(first, second, shape, dim):
    return jnp.where(iota(shape, dim) < P_SIZE, first, second)


def pack_decay(packed_ref, within_ref, chunks):
    total = within_ref[GROUP - 1 : GROUP, :]
    for c in range(1, chunks):
        total = total + within_ref[(c + 1) * GROUP - 1 : (c + 1) * GROUP, :]
    decay = jnp.exp(total)
    kind = packed_ref.dtype
    high = decay.astype(kind)
    rest = (decay - high.astype(F32)).astype(kind)
    packed_ref[packed_ref.shape[0] - PACK :, :] = jnp.concatenate(
        [high, rest, jnp.zeros((PACK - 2, LANES), kind)], axis=0
    )


def unpack_states(state_refs, decay_rows, first_head):
    count = state_refs[0].shape[0]
    owner = iota((count, LANES), 0) // P_SIZE + first_head
    mine = iota((count, LANES), 1) == owner
    total = jnp.zeros((count, NS), F32)
    for ref, rows in zip(reversed(state_refs), reversed(decay_rows)):
        decay = rows[0:1, :].astype(F32) + rows[1:2, :].astype(F32)
        factor = jnp.sum(jnp.where(mine, decay, 0.0), axis=1, keepdims=True)
        total = factor * total + ref[...].astype(F32)
    return total


def scan_forward_kernel(
    dot,
    inner_ref, state_ref, dt_ref, edge_in_ref, edge_st_ref, ker_in_ref, bias_in_ref,
    ker_st_ref, bias_st_ref, step_bias_ref, decay_ref, skip_ref,
    out_ref, kq_ref, step_ref, within_ref, starts_ref, packed_ref,
    scores_ref, turned_ref, ext_ref, ext_st_ref,
):
    pair = pl.program_id(0)
    rows = inner_ref.shape[0]
    chunks = rows // GROUP

    @pl.when(pair == 0)
    def _():
        ext_st_ref[0:EDGE, :] = edge_st_ref[...]
        ext_st_ref[EDGE:, :] = state_ref[...]
        pre = convolve(ext_st_ref, ker_st_ref, bias_st_ref, rows)
        kq_ref[...] = pre * sigmoid(pre)
        steps = softplus(dt_ref[...] + step_bias_ref[...])
        _, within = chunk_sums(steps, decay_ref[...], rows)
        step_ref[...] = steps
        within_ref[...] = within
        turned_ref[...] = within.T
        pack_decay(packed_ref, within_ref, chunks)
        for c in range(chunks):
            at = slice(c * GROUP, (c + 1) * GROUP)
            scores_ref[c] = high_dot(kq_ref[at, NS:], kq_ref[at, :NS], NT)

    ext_ref[0:EDGE, :] = edge_in_ref[...]
    ext_ref[EDGE:, :] = inner_ref[...]
    pre = convolve(ext_ref, ker_in_ref, bias_in_ref, rows)
    values = pre * sigmoid(pre)
    within_cols = [column(within_ref[...], 2 * pair + k) for k in range(2)]
    step_cols = [column(step_ref[...], 2 * pair + k) for k in range(2)]
    shape = (rows, LANES)
    scaled = values * pair_select(step_cols[0], step_cols[1], shape, 1)
    within_wide = pair_select(within_cols[0], within_cols[1], shape, 1)
    causal = iota((GROUP, GROUP), 0) >= iota((GROUP, GROUP), 1)
    state = jnp.zeros((LANES, NS), F32)
    for c in range(chunks):
        at = slice(c * GROUP, (c + 1) * GROUP)
        scaled_low = scaled[at]
        halves = []
        ends = []
        for k in range(2):
            row = turned_ref[pl.ds(2 * pair + k, 1), at]
            decays = jnp.exp(jnp.where(causal, within_cols[k][at] - row, -1e30))
            halves.append(dot(decays * scores_ref[c], scaled_low, NN))
            ends.append(within_cols[k][(c + 1) * GROUP - 1 : (c + 1) * GROUP])
        result = pair_select(halves[0], halves[1], (GROUP, LANES), 1)
        if c > 0:
            result = result + jnp.exp(within_wide[at]) * dot(kq_ref[at, NS:], state, NT)
        out_ref[at, :] = result + skip_ref[...] * values[at]
        starts_ref[c] = state
        end_wide = pair_select(ends[0], ends[1], (1, LANES), 1)
        tail = jnp.exp(end_wide - within_wide[at])
        piece = dot(scaled[at] * tail, kq_ref[at, :NS], TN)
        state = jnp.exp(pair_select(ends[0], ends[1], (LANES, 1), 0)) * state + piece
    packed_ref[pl.ds(pl.multiple_of(pair * LANES, LANES), LANES), :] = state


def scan_forward(after, dot, pre, pre_st, edge, small):
    rows = pre.shape[0]
    width = small["bias_inner"].shape[1]
    pairs = width // LANES
    chunks = rows // GROUP
    taps = small["kernel_inner"].shape[0]
    block = lambda shape, index: pl.BlockSpec(shape, index)
    const2 = lambda p: (0, 0)
    return call(
        partial(scan_forward_kernel, dot),
        after,
        grid=(pairs,),
        in_specs=[
            block((rows, LANES), lambda p: (0, pairs + p)),
            block((rows, 2 * NS), lambda p: (0, 0)),
            block((rows, LANES), lambda p: (0, 2)),
            block((EDGE, LANES), lambda p: (0, p)),
            block((EDGE, 2 * NS), lambda p: (0, pairs // 2)),
            block((taps, LANES), lambda p: (0, p)),
            block((1, LANES), lambda p: (0, p)),
            block((taps, 2 * NS), const2),
            block((1, 2 * NS), const2),
            block((1, LANES), const2),
            block((1, LANES), const2),
            block((1, LANES), lambda p: (0, p)),
        ],
        out_specs=[
            block((rows, LANES), lambda p: (0, p)),
            block((rows, 2 * NS), const2),
            block((rows, LANES), const2),
            block((rows, LANES), const2),
            block((chunks, LANES, NS), lambda p: (0, p, 0)),
            block((width + PACK, NS), const2),
        ],
        out_shape=[
            jax.ShapeDtypeStruct((rows, width), F32),
            jax.ShapeDtypeStruct((rows, 2 * NS), F32),
            jax.ShapeDtypeStruct((rows, LANES), F32),
            jax.ShapeDtypeStruct((rows, LANES), F32),
            jax.ShapeDtypeStruct((chunks, width, NS), F32),
            jax.ShapeDtypeStruct((width + PACK, NS), F32),
        ],
        scratch_shapes=[
            pltpu.VMEM((chunks, GROUP, GROUP), F32),
            pltpu.VMEM((LANES, rows), F32),
            pltpu.VMEM((rows + EDGE, LANES), F32),
            pltpu.VMEM((rows + EDGE, 2 * NS), F32),
        ],
        name="scan_forward",
    )(
        pre, pre_st, pre_st, edge, edge, small["kernel_inner"], small["bias_inner"],
        small["kernel_state"], small["bias_state"], small["step_bias"], small["decay_log"],
        small["skip_wide"], *after,
    )


def scan_backward_kernel(
    inner_ref, state_ref, dt_ref, edge_in_ref, edge_st_ref, ker_in_ref, bias_in_ref,
    ker_st_ref, bias_st_ref, step_bias_ref, decay_ref, skip_ref,
    kq_ref, step_ref, within_ref, starts_ref, before_ref, grad_ref, *refs,
):
    arrived = len(refs) - 20
    after_refs, decay_refs, refs = refs[: arrived // 2], refs[arrived // 2 : arrived], refs[arrived:]
    (inner_out, edge_in_out, small_in_out, state_out, edge_st_out, small_st_out, raw_out, small_dt_out,
    scores_ref, turned_ref, ext_ref, ext_st_ref, back_ref, back_st_ref,
    grad_scores, grad_kq, grad_within, grad_turned, grad_steps, grad_ends) = refs
    pair = pl.program_id(0)
    rows = inner_ref.shape[0]
    chunks = rows // GROUP
    taps = ker_in_ref.shape[0]

    @pl.when(pair == 0)
    def _():
        turned_ref[...] = within_ref[...].T
        for c in range(chunks):
            at = slice(c * GROUP, (c + 1) * GROUP)
            scores_ref[c] = high_dot(kq_ref[at, NS:], kq_ref[at, :NS], NT)
        for ref in (grad_scores, grad_kq, grad_within, grad_turned, grad_steps, grad_ends):
            ref[...] = jnp.zeros_like(ref)

    ext_ref[0:EDGE, :] = edge_in_ref[...]
    ext_ref[EDGE:, :] = inner_ref[...]
    pre = convolve(ext_ref, ker_in_ref, bias_in_ref, rows)
    sig = sigmoid(pre)
    values = pre * sig
    shape = (rows, LANES)
    within_cols = [column(within_ref[...], 2 * pair + k) for k in range(2)]
    step_cols = [column(step_ref[...], 2 * pair + k) for k in range(2)]
    step_wide = pair_select(step_cols[0], step_cols[1], shape, 1)
    scaled = values * step_wide
    within_wide = pair_select(within_cols[0], within_cols[1], shape, 1)
    causal = iota((GROUP, GROUP), 0) >= iota((GROUP, GROUP), 1)
    first_half = iota((GROUP, LANES), 1) < P_SIZE
    lanes = iota((1, LANES), 1)
    pick = jnp.where(
        iota((LANES, LANES), 1) == 2 * pair + iota((LANES, LANES), 0) // P_SIZE, 1.0, 0.0
    )
    ends = [
        [within_cols[k][(c + 1) * GROUP - 1 : (c + 1) * GROUP] for k in range(2)]
        for c in range(chunks)
    ]
    passed = [[jnp.zeros((1, 1), F32)] * 2]
    for c in range(chunks - 1):
        passed.append([passed[c][k] + ends[c][k] for k in range(2)])
    state_grad = unpack_states(after_refs, [ref[...] for ref in decay_refs], 2 * pair)
    value_grads = [None] * chunks
    for c in reversed(range(chunks)):
        at = slice(c * GROUP, (c + 1) * GROUP)
        start_decay = jnp.exp(pair_select(passed[c][0], passed[c][1], (LANES, 1), 0))
        state = starts_ref[c] + start_decay * before_ref[...]
        grad = grad_ref[at, :]
        grad_low = grad.astype(BF16)
        scaled_low = scaled[at].astype(BF16)
        keys = kq_ref[at, :NS].astype(BF16)
        reads = kq_ref[at, NS:].astype(BF16)
        state_low = state.astype(BF16)
        state_grad_low = state_grad.astype(BF16)
        halves = []
        for k in range(2):
            head = 2 * pair + k
            row = turned_ref[pl.ds(head, 1), at]
            decays = jnp.exp(jnp.where(causal, within_cols[k][at] - row, -1e30))
            weights = decays * scores_ref[c]
            mine = first_half if k == 0 else jnp.logical_not(first_half)
            own = jnp.where(mine, grad, 0.0).astype(BF16)
            weight_grad = lax.dot_general(own, scaled_low, NT, preferred_element_type=F32)
            halves.append(low_dot(weights, grad_low, TN))
            grad_scores[c] += weight_grad * decays
            moved = weight_grad * weights
            grad_within[at, :] += jnp.where(
                lanes == head, jnp.sum(moved, axis=1, keepdims=True), 0.0
            )
            grad_turned[pl.ds(head, 1), at] = jnp.sum(moved, axis=0, keepdims=True)
        scaled_grad = pair_select(halves[0], halves[1], (GROUP, LANES), 1)
        end_wide = pair_select(ends[c][0], ends[c][1], (1, LANES), 1)
        tail = jnp.exp(end_wide - within_wide[at])
        late = tail * lax.dot_general(keys, state_grad_low, NT, preferred_element_type=F32)
        late_sums = high_dot(scaled[at] * late, pick, NN)
        scaled_grad = scaled_grad + late
        grad_kq[at, :NS] += low_dot(scaled[at] * tail, state_grad_low, NN)
        entry = jnp.exp(within_wide[at])
        early = entry * lax.dot_general(reads, state_low, NT, preferred_element_type=F32)
        early_sums = high_dot(grad * early, pick, NN)
        grad_entry = (grad * entry).astype(BF16)
        grad_kq[at, NS:] += lax.dot_general(grad_entry, state_low, NN, preferred_element_type=F32)
        grad_within[at, :] += early_sums - late_sums
        end_decay = jnp.exp(pair_select(ends[c][0], ends[c][1], (LANES, 1), 0))
        kept = end_decay * state_grad * state
        kept_sum = jnp.sum(kept, axis=1, keepdims=True)
        kept_sums = jnp.sum(kept_sum * pick, axis=0, keepdims=True)
        grad_ends[c : c + 1, :] += jnp.sum(late_sums, axis=0, keepdims=True) + kept_sums
        grad_steps[at, :] += high_dot(values[at] * scaled_grad, pick, NN)
        value_grads[c] = step_wide[at] * scaled_grad + skip_ref[...] * grad
        state_grad = end_decay * state_grad + lax.dot_general(
            grad_entry, reads, TN, preferred_element_type=F32
        )
    value_grad = jnp.concatenate(value_grads, axis=0)
    pre_grad = value_grad * sig * (1.0 + pre * (1.0 - sig))
    total, small = convolve_back(back_ref, ext_ref, ker_in_ref, pre_grad, rows)
    edge_in_out[...] = total[0:EDGE]
    inner_out[...] = total[EDGE:]
    small.append(jnp.sum(grad_ref[...] * values, axis=0, keepdims=True))
    small.append(jnp.zeros((8 - len(small), LANES), F32))
    small_in_out[...] = jnp.concatenate(small, axis=0)

    @pl.when(pair == pl.num_programs(0) - 1)
    def _():
        upper = jnp.where(iota((GROUP, GROUP), 0) <= iota((GROUP, GROUP), 1), 1.0, 0.0)
        scale = -jnp.exp(decay_ref[...])
        decay_grad = jnp.zeros((1, LANES), F32)
        back = grad_turned[...].T
        for c in range(chunks):
            at = slice(c * GROUP, (c + 1) * GROUP)
            grad_kq[at, NS:] += high_dot(grad_scores[c], kq_ref[at, :NS], NN)
            grad_kq[at, :NS] += high_dot(grad_scores[c], kq_ref[at, NS:], TN)
            rate_grad = high_dot(upper, grad_within[at, :] - back[at], NN) + grad_ends[c : c + 1, :]
            grad_steps[at, :] += rate_grad * scale
            decay_grad += jnp.sum(rate_grad * scale * step_ref[at, :], axis=0, keepdims=True)
        raw = grad_steps[...] * sigmoid(dt_ref[...] + step_bias_ref[...])
        raw_out[...] = raw
        raw_sum = jnp.sum(raw, axis=0, keepdims=True)
        small_dt_out[...] = jnp.concatenate(
            [raw_sum, decay_grad, jnp.zeros((6, LANES), F32)], axis=0
        )
        ext_st_ref[0:EDGE, :] = edge_st_ref[...]
        ext_st_ref[EDGE:, :] = state_ref[...]
        pre_st = convolve(ext_st_ref, ker_st_ref, bias_st_ref, rows)
        sig_st = sigmoid(pre_st)
        pre_st_grad = grad_kq[...] * sig_st * (1.0 + pre_st * (1.0 - sig_st))
        total_st, small_st = convolve_back(back_st_ref, ext_st_ref, ker_st_ref, pre_st_grad, rows)
        edge_st_out[...] = total_st[0:EDGE]
        state_out[...] = total_st[EDGE:]
        small_st.append(jnp.zeros((8 - len(small_st), 2 * NS), F32))
        small_st_out[...] = jnp.concatenate(small_st, axis=0)


def scan_backward(after, pre, pre_st, edge, small, kq, steps, within, starts, before, later, grad):
    rows = pre.shape[0]
    width = grad.shape[1]
    pairs = width // LANES
    chunks = rows // GROUP
    taps = small["kernel_inner"].shape[0]
    block = lambda shape, index: pl.BlockSpec(shape, index)
    const2 = lambda p: (0, 0)
    lane2 = lambda p: (0, p)
    return call(
        scan_backward_kernel,
        after,
        grid=(pairs,),
        in_specs=[
            block((rows, LANES), lambda p: (0, pairs + p)),
            block((rows, 2 * NS), lambda p: (0, 0)),
            block((rows, LANES), lambda p: (0, 2)),
            block((EDGE, LANES), lane2),
            block((EDGE, 2 * NS), lambda p: (0, pairs // 2)),
            block((taps, LANES), lane2),
            block((1, LANES), lane2),
            block((taps, 2 * NS), const2),
            block((1, 2 * NS), const2),
            block((1, LANES), const2),
            block((1, LANES), const2),
            block((1, LANES), lane2),
            block((rows, 2 * NS), const2),
            block((rows, LANES), const2),
            block((rows, LANES), const2),
            block((chunks, LANES, NS), lambda p: (0, p, 0)),
            block((LANES, NS), lambda p: (p, 0)),
            block((rows, LANES), lane2),
        ]
        + [block((LANES, NS), lambda p: (p, 0))] * len(later)
        + [block((PACK, NS), lambda p: (width // PACK, 0))] * len(later),
        out_specs=[
            block((rows, LANES), lane2),
            block((EDGE, LANES), lane2),
            block((8, LANES), lane2),
            block((rows, 2 * NS), const2),
            block((EDGE, 2 * NS), const2),
            block((8, 2 * NS), const2),
            block((rows, LANES), const2),
            block((8, LANES), const2),
        ],
        out_shape=[
            jax.ShapeDtypeStruct((rows, width), F32),
            jax.ShapeDtypeStruct((EDGE, width), F32),
            jax.ShapeDtypeStruct((8, width), F32),
            jax.ShapeDtypeStruct((rows, 2 * NS), F32),
            jax.ShapeDtypeStruct((EDGE, 2 * NS), F32),
            jax.ShapeDtypeStruct((8, 2 * NS), F32),
            jax.ShapeDtypeStruct((rows, LANES), F32),
            jax.ShapeDtypeStruct((8, LANES), F32),
        ],
        scratch_shapes=[
            pltpu.VMEM((chunks, GROUP, GROUP), F32),
            pltpu.VMEM((LANES, rows), F32),
            pltpu.VMEM((rows + EDGE, LANES), F32),
            pltpu.VMEM((rows + EDGE, 2 * NS), F32),
            pltpu.VMEM((rows + 2 * EDGE, LANES), F32),
            pltpu.VMEM((rows + 2 * EDGE, 2 * NS), F32),
            pltpu.VMEM((chunks, GROUP, GROUP), F32),
            pltpu.VMEM((rows, 2 * NS), F32),
            pltpu.VMEM((rows, LANES), F32),
            pltpu.VMEM((LANES, rows), F32),
            pltpu.VMEM((rows, LANES), F32),
            pltpu.VMEM((8, LANES), F32),
        ],
        name="scan_backward",
    )(
        pre, pre_st, pre_st, edge, edge, small["kernel_inner"], small["bias_inner"],
        small["kernel_state"], small["bias_state"], small["step_bias"], small["decay_log"],
        small["skip_wide"], kq, steps, within, starts, before, grad, *later, *later, *after,
    )


def widen(values, width):
    spread = jnp.where(
        iota((LANES, width), 1) // P_SIZE == iota((LANES, width), 0), 1.0, 0.0
    ).astype(BF16)
    high = values.astype(BF16)
    rest = (values - high.astype(F32)).astype(BF16)
    return lax.dot_general(high, spread, NN, preferred_element_type=F32) + lax.dot_general(
        rest, spread, NN, preferred_element_type=F32
    )


def entry_decay(within_ref, chunk, chunks):
    offset = jnp.zeros((1, LANES), F32)
    for c in range(chunks - 1):
        offset = offset + jnp.where(c < chunk, within_ref[(c + 1) * GROUP - 1 : (c + 1) * GROUP, :], 0.0)
    at = pl.multiple_of(chunk * GROUP, GROUP)
    return jnp.exp(within_ref[pl.ds(at, GROUP), :] + offset)


def stat_columns(stats_ref):
    height, length = stats_ref.shape
    return jnp.concatenate([stats_ref[...], jnp.zeros((LANES - height, length), F32)], axis=0).T


def mix_first_kernel(dot, chunks, arrived, with_grad, *refs):
    local_ref, gate_ref, reads_ref, within_ref, gain_ref = refs[:5]
    arrived_refs = refs[5 : 5 + arrived]
    refs = refs[5 + arrived :]
    if with_grad:
        proj_ref, up_ref, mixer_ref, before_ref, stats_ref, back_ref = refs
    else:
        mixer_ref, before_ref, stats_ref = refs
    width = local_ref.shape[1]
    chunk = pl.program_id(0)

    @pl.when(chunk == 0)
    def _():
        states = [ref.at[0:width, :] for ref in arrived_refs]
        decays = [ref[width:, :] for ref in arrived_refs]
        before_ref[...] = unpack_states(states, decays, 0)

    entry = widen(entry_decay(within_ref, chunk, chunks), width)
    mixer = local_ref[...] + entry * dot(reads_ref[...], before_ref[...], NT)
    mixer_ref[...] = mixer
    gate = gate_ref[...]
    gated = mixer * gate * sigmoid(gate)
    ones = jnp.ones((8, width), F32)
    stats = high_dot(ones, gated * gated, NT)
    if with_grad:
        back = lax.dot_general(up_ref[...], proj_ref[...], NT, preferred_element_type=F32)
        back_ref[...] = back
        other = high_dot(ones, back * gated * gain_ref[...], NT)
        stats = jnp.where(iota(stats.shape, 0) == 1, other, stats)
    stats_ref[...] = stats


def mix_first(after, dot, local, pre, kq, within, gain, arrived, upstream=None, proj_out=None):
    rows, width = local.shape
    chunks = rows // GROUP
    block = lambda shape, index: pl.BlockSpec(shape, index)
    row2 = lambda c: (c, 0)
    const2 = lambda c: (0, 0)
    with_grad = upstream is not None
    in_specs = [
        block((GROUP, width), row2),
        block((GROUP, width), row2),
        block((GROUP, NS), lambda c: (c, 1)),
        block((rows, LANES), const2),
        block((1, width), const2),
    ] + [block((width + PACK, NS), const2)] * len(arrived)
    out_specs = [
        block((GROUP, width), row2),
        block((width, NS), const2),
        block((8, GROUP), lambda c: (0, c)),
    ]
    out_shape = [
        jax.ShapeDtypeStruct((rows, width), F32),
        jax.ShapeDtypeStruct((width, NS), F32),
        jax.ShapeDtypeStruct((8, rows), F32),
    ]
    args = [local, pre, kq, within, gain, *arrived]
    flops = 4 * rows * width * NS
    if with_grad:
        features = upstream.shape[1]
        in_specs += [block((width, features), const2), block((GROUP, features), row2)]
        out_specs.append(block((GROUP, width), row2))
        out_shape.append(jax.ShapeDtypeStruct((rows, width), F32))
        args += [proj_out, upstream]
        flops += 2 * rows * width * features
    return call(
        partial(mix_first_kernel, dot, chunks, len(arrived), with_grad),
        after,
        grid=(chunks,),
        in_specs=in_specs,
        out_specs=out_specs,
        out_shape=out_shape,
        name="mix_first",
    )(*args, *after)


def project_out_kernel(total_width, mixer_ref, gate_ref, gain_ref, stats_ref, proj_ref, normed_ref, part_ref, low_ref):
    scale = lax.rsqrt(stat_columns(stats_ref)[:, 0:1] / total_width + EPS)
    gate = gate_ref[...]
    normed = (mixer_ref[...] * gate * sigmoid(gate) * scale * gain_ref[...]).astype(BF16)
    normed_ref[...] = normed
    part = lax.dot_general(normed, proj_ref[...], NN, preferred_element_type=F32)
    part_ref[...] = part
    low_ref[...] = part.astype(BF16)


def project_out(after, chunk, mixer, pre, gain, stats, proj_out, total_width):
    width = mixer.shape[1]
    features = proj_out.shape[1]
    block = lambda shape, index: pl.BlockSpec(shape, index)
    const2 = lambda c: (0, 0)
    return call(
        partial(project_out_kernel, total_width),
        after,
        grid=(1,),
        in_specs=[
            block((GROUP, width), lambda c: (chunk, 0)),
            block((GROUP, width), lambda c: (chunk, 0)),
            block((1, width), const2),
            block((8, GROUP), lambda c: (0, chunk)),
            block((width, features), const2),
        ],
        out_specs=[block((GROUP, width), const2), block((GROUP, features), const2), block((GROUP, features), const2)],
        out_shape=[
            jax.ShapeDtypeStruct((GROUP, width), BF16),
            jax.ShapeDtypeStruct((GROUP, features), F32),
            jax.ShapeDtypeStruct((GROUP, features), BF16),
        ],
        name="project_out",
    )(mixer, pre, gain, stats, proj_out, *after)


def assemble(place_ref, refs, out_ref):
    half = refs[0].shape[0]
    for chunk in range(len(refs) // 4):
        done, sent, crossed, passed = refs[4 * chunk : 4 * chunk + 4]
        low = slice(2 * chunk * half, (2 * chunk + 1) * half)
        high = slice((2 * chunk + 1) * half, (2 * chunk + 2) * half)
        for place, pair in enumerate(((sent, passed), (done, crossed), (crossed, done), (passed, sent))):

            @pl.when(place_ref[0] == place)
            def _(pair=pair):
                out_ref[low, :] = pair[0][...]
                out_ref[high, :] = pair[1][...]


def gather_kernel(place_ref, *refs):
    assemble(place_ref, refs[:-1], refs[-1])


def gather(after, place, pieces):
    half, features = pieces[0].shape
    rows = half * len(pieces) // 2
    same = lambda i, place_ref: (0, 0)
    return call(
        gather_kernel,
        after,
        grid=(1,),
        in_specs=[pl.BlockSpec((half, features), same)] * len(pieces),
        out_specs=pl.BlockSpec((rows, features), same),
        out_shape=jax.ShapeDtypeStruct((rows, features), BF16),
        name="gather",
        prefetch=1,
    )(place, *pieces, *after)


def project_kernel(assembled, place_ref, *refs):
    if assembled:
        pieces = refs[:assembled]
        gain_ref, wide_ref, bc_ref, dt_ref, normed_ref, pre_ref, state_ref, edge_ref, rows_ref = refs[assembled:]
    else:
        rows_ref, gain_ref, wide_ref, bc_ref, dt_ref, normed_ref, pre_ref, state_ref, edge_ref = refs
    width = wide_ref.shape[1]
    rows = pre_ref.shape[0]

    @pl.when(pl.program_id(0) == 0)
    def _():
        if assembled:
            assemble(place_ref, pieces, rows_ref)
        wide = rows_ref[...].astype(F32)
        scale = lax.rsqrt(jnp.mean(wide * wide, axis=1, keepdims=True) + EPS)
        normed = (wide * scale * gain_ref[...]).astype(BF16)
        normed_ref[...] = normed
        state = lax.dot_general(normed, bc_ref[...], NN, preferred_element_type=F32)
        state_ref[:, 0 : 2 * NS] = state
        state_ref[:, 2 * NS :] = lax.dot_general(normed, dt_ref[...], NN, preferred_element_type=F32)
        edge_ref[:, width:] = state[rows - EDGE :]

    pre = lax.dot_general(normed_ref[...], wide_ref[...], NN, preferred_element_type=F32)
    pre_ref[...] = pre
    edge_ref[:, 0:width] = pre[rows - EDGE :]


def project(after, place, rows_in, gain, w_wide, w_bc, w_dt):
    assembled = len(rows_in) if isinstance(rows_in, (list, tuple)) else 0
    pieces = list(rows_in) if assembled else [rows_in]
    features = w_wide.shape[0]
    width = w_wide.shape[1] // 2
    rows = pieces[0].shape[0] * (assembled // 2 if assembled else 1)
    block = lambda shape, index: pl.BlockSpec(shape, index)
    const2 = lambda f, place_ref: (0, 0)
    out_specs = [
        block((rows, features), const2),
        block((rows, width), lambda f, place_ref: (0, f)),
        block((rows, 2 * NS + LANES), const2),
        block((EDGE, width + 2 * NS), const2),
    ]
    out_shape = [
        jax.ShapeDtypeStruct((rows, features), BF16),
        jax.ShapeDtypeStruct((rows, 2 * width), F32),
        jax.ShapeDtypeStruct((rows, 2 * NS + LANES), F32),
        jax.ShapeDtypeStruct((EDGE, width + 2 * NS), F32),
    ]
    if assembled:
        out_specs.append(block((rows, features), const2))
        out_shape.append(jax.ShapeDtypeStruct((rows, features), BF16))
    return call(
        partial(project_kernel, assembled),
        after,
        grid=(2,),
        in_specs=[block(piece.shape, const2) for piece in pieces]
        + [
            block((1, features), const2),
            block((features, width), lambda f, place_ref: (0, f)),
            block((features, 2 * NS), const2),
            block((features, LANES), const2),
        ],
        out_specs=out_specs,
        out_shape=out_shape,
        name="project",
        prefetch=1,
    )(place, *pieces, gain, w_wide, w_bc, w_dt, *after)


def back_first_kernel(count, place_ref, *refs):
    pieces = refs[:count]
    proj_ref, mixer_ref, gate_ref, gain_ref, up_ref, back_ref, stats_ref = refs[count:]
    chunk = pl.program_id(0)

    @pl.when(chunk == 0)
    def _():
        assemble(place_ref, pieces, up_ref)

    at = pl.multiple_of(chunk * GROUP, GROUP)
    back = lax.dot_general(
        up_ref[pl.ds(at, GROUP), :], proj_ref[...], NT, preferred_element_type=F32
    )
    back_ref[...] = back
    gate = gate_ref[...]
    product = back * mixer_ref[...] * gate * sigmoid(gate) * gain_ref[...]
    stats_ref[...] = high_dot(jnp.ones((8, back.shape[1]), F32), product, NT)


def back_first(after, place, pieces, proj_out, mixer, pre, gain):
    rows, width = mixer.shape
    features = proj_out.shape[1]
    chunks = rows // GROUP
    block = lambda shape, index: pl.BlockSpec(shape, index)
    row2 = lambda c, place_ref: (c, 0)
    const2 = lambda c, place_ref: (0, 0)
    return call(
        partial(back_first_kernel, len(pieces)),
        after,
        grid=(chunks,),
        in_specs=[block(piece.shape, const2) for piece in pieces]
        + [
            block((width, features), const2),
            block((GROUP, width), row2),
            block((GROUP, width), row2),
            block((1, width), const2),
        ],
        out_specs=[
            block((rows, features), const2),
            block((GROUP, width), row2),
            block((8, GROUP), lambda c, place_ref: (0, c)),
        ],
        out_shape=[
            jax.ShapeDtypeStruct((rows, features), BF16),
            jax.ShapeDtypeStruct((rows, width), F32),
            jax.ShapeDtypeStruct((8, rows), F32),
        ],
        name="back_first",
        prefetch=1,
    )(place, *pieces, proj_out, mixer, pre, gain, *after)


def mix_back_kernel(chunks, with_part, total_width, *refs):
    back_ref, mixer_ref, gate_ref, reads_ref, within_ref, gain_ref, square_ref, product_ref = refs[:8]
    refs = refs[8:]
    if with_part:
        proj_ref, grad_ref, gate_grad_ref, gain_grad_ref, packed_ref, normed_ref, *low_refs, total_ref = refs
    else:
        grad_ref, gate_grad_ref, gain_grad_ref, packed_ref, total_ref = refs
    width = mixer_ref.shape[1]
    chunk = pl.program_id(0)
    scale = lax.rsqrt(stat_columns(square_ref)[:, 0:1] / total_width + EPS)
    product = stat_columns(product_ref)[:, 1:2] / total_width
    gate = gate_ref[...]
    sig = sigmoid(gate)
    act = gate * sig
    mixer = mixer_ref[...]
    back = back_ref[...]
    gated = mixer * act
    unit = gated * scale
    if with_part:
        normed = (unit * gain_ref[...]).astype(BF16)
        normed_ref[...] = normed
        low = lax.dot_general(normed, proj_ref[...], NN, preferred_element_type=F32).astype(BF16)
        for c in range(chunks):
            @pl.when(chunk == c)
            def _(c=c):
                low_refs[c][...] = low
    gated_grad = scale * back * gain_ref[...] - gated * (scale * scale * scale * product)
    grad = gated_grad * act
    grad_ref[...] = grad
    gate_grad_ref[...] = (gated_grad * mixer * sig * (1.0 + gate * (1.0 - sig))).astype(BF16)
    entry = widen(entry_decay(within_ref, chunk, chunks), width)
    gain_part = jnp.sum(back * unit, axis=0, keepdims=True)
    state_part = low_dot(grad * entry, reads_ref[...], TN)

    @pl.when(chunk == 0)
    def _():
        gain_grad_ref[...] = gain_part
        total_ref[...] = state_part

    @pl.when(chunk > 0)
    def _():
        gain_grad_ref[...] += gain_part
        total_ref[...] += state_part

    @pl.when(chunk == chunks - 1)
    def _():
        packed_ref[0:width, :] = total_ref[...].astype(BF16)
        pack_decay(packed_ref, within_ref, chunks)


def mix_back(after, back, mixer, pre, kq, within, gain, square, product, total_width, proj_out=None):
    rows, width = mixer.shape
    chunks = rows // GROUP
    block = lambda shape, index: pl.BlockSpec(shape, index)
    row2 = lambda c: (c, 0)
    const2 = lambda c: (0, 0)
    with_part = proj_out is not None
    in_specs = [
        block((GROUP, width), row2),
        block((GROUP, width), row2),
        block((GROUP, width), row2),
        block((GROUP, NS), lambda c: (c, 1)),
        block((rows, LANES), const2),
        block((1, width), const2),
        block((8, GROUP), lambda c: (0, c)),
        block((8, GROUP), lambda c: (0, c)),
    ]
    out_specs = [
        block((GROUP, width), row2),
        block((GROUP, width), row2),
        block((1, width), const2),
        block((width + PACK, NS), const2),
    ]
    out_shape = [
        jax.ShapeDtypeStruct((rows, width), F32),
        jax.ShapeDtypeStruct((rows, width), BF16),
        jax.ShapeDtypeStruct((1, width), F32),
        jax.ShapeDtypeStruct((width + PACK, NS), BF16),
    ]
    args = [back, mixer, pre, kq, within, gain, square, product]
    flops = 2 * rows * width * NS
    if with_part:
        features = proj_out.shape[1]
        in_specs.append(block((width, features), const2))
        out_specs += [block((GROUP, width), row2)] + [block((GROUP, features), const2)] * chunks
        out_shape.append(jax.ShapeDtypeStruct((rows, width), BF16))
        out_shape += [jax.ShapeDtypeStruct((GROUP, features), BF16)] * chunks
        args.append(proj_out)
        flops += 2 * rows * width * features
    return call(
        partial(mix_back_kernel, chunks, with_part, total_width),
        after,
        grid=(chunks,),
        in_specs=in_specs,
        out_specs=out_specs,
        out_shape=out_shape,
        scratch_shapes=[pltpu.VMEM((width, NS), F32)],
        name="mix_back",
    )(*args, *after)


def project_back_kernel(
    gate_ref, inner_ref, state_ref, raw_ref, edge_ref, wide_ref, bc_ref, dt_ref,
    grads_ref, narrow_grads_ref, *part_refs,
):
    width = gate_ref.shape[1]
    rows = gate_ref.shape[0]

    @pl.when(pl.program_id(0) == 0)
    def _():
        grads_ref[:, 0:width] = gate_ref[...]
        added = jnp.concatenate(
            [jnp.zeros((EDGE, width), F32), edge_ref[:, 0:width]], axis=0
        )
        grads_ref[0 : rows - PACK, width:] = inner_ref[0 : rows - PACK, :].astype(BF16)
        grads_ref[rows - PACK :, width:] = (inner_ref[rows - PACK :, :] + added).astype(BF16)
        added = jnp.concatenate(
            [jnp.zeros((EDGE, 2 * NS), F32), edge_ref[:, width:]], axis=0
        )
        narrow_grads_ref[0 : rows - PACK, 0 : 2 * NS] = state_ref[0 : rows - PACK, :].astype(BF16)
        narrow_grads_ref[rows - PACK :, 0 : 2 * NS] = (state_ref[rows - PACK :, :] + added).astype(BF16)
        narrow_grads_ref[:, 2 * NS :] = raw_ref[...].astype(BF16)

    part = lax.dot_general(grads_ref[...], wide_ref[...], NT, preferred_element_type=F32)
    part = part + lax.dot_general(
        narrow_grads_ref[:, 0 : 2 * NS], bc_ref[...], NT, preferred_element_type=F32
    )
    part = part + lax.dot_general(
        narrow_grads_ref[:, 2 * NS :], dt_ref[...], NT, preferred_element_type=F32
    )
    for c, part_ref in enumerate(part_refs):
        part_ref[...] = part[c * GROUP : (c + 1) * GROUP].astype(BF16)


def project_back(after, gate_grad, inner, state, raw, edges, w_wide, w_bc, w_dt):
    rows, width = gate_grad.shape
    features = w_wide.shape[0]
    size = 512 if features % 512 == 0 else features
    block = lambda shape, index: pl.BlockSpec(shape, index)
    const2 = lambda f: (0, 0)
    narrow = 2 * NS + LANES
    return call(
        project_back_kernel,
        after,
        grid=(features // size,),
        in_specs=[
            block((rows, width), const2),
            block((rows, width), const2),
            block((rows, 2 * NS), const2),
            block((rows, LANES), const2),
            block((EDGE, width + 2 * NS), const2),
            block((size, 2 * width), lambda f: (f, 0)),
            block((size, 2 * NS), lambda f: (f, 0)),
            block((size, LANES), lambda f: (f, 0)),
        ],
        out_specs=[
            block((rows, 2 * width), const2),
            block((rows, narrow), const2),
        ]
        + [block((GROUP, size), lambda f: (0, f))] * (rows // GROUP),
        out_shape=[
            jax.ShapeDtypeStruct((rows, 2 * width), BF16),
            jax.ShapeDtypeStruct((rows, narrow), BF16),
        ]
        + [jax.ShapeDtypeStruct((GROUP, features), BF16)] * (rows // GROUP),
        name="project_back",
    )(gate_grad, inner, state, raw, edges, w_wide, w_bc, w_dt, *after)


def add_half_kernel(index_ref, own_ref, first_ref, out_ref):
    out_ref[...] = (own_ref[...].astype(F32) + first_ref[...].astype(F32)).astype(out_ref.dtype)


def add_half(after, index, own, first, kind):
    half = own.shape[0] // 2
    features = own.shape[1]
    pick = pl.BlockSpec((half, features), lambda i, index_ref: (index_ref[0], 0))
    return call(
        add_half_kernel,
        after,
        grid=(1,),
        in_specs=[pick, pick],
        out_specs=pl.BlockSpec((half, features), lambda i, index_ref: (0, 0)),
        out_shape=jax.ShapeDtypeStruct((half, features), kind),
        name="add_half",
        prefetch=1,
    )(index, own, first, *after)


def finish_out_kernel(index_ref, own_ref, first_ref, second_ref, rows_ref, out_ref):
    total = own_ref[...].astype(F32) + first_ref[...].astype(F32) + second_ref[...].astype(F32)
    out_ref[...] = (rows_ref[...].astype(F32) + total).astype(BF16)


def finish_back_kernel(
    index_ref, own_ref, first_ref, second_ref, rows_ref, gain_ref, up_ref, out_ref, gain_grad_ref
):
    total = own_ref[...].astype(F32) + first_ref[...].astype(F32) + second_ref[...].astype(F32)
    wide = rows_ref[...].astype(F32)
    scale = lax.rsqrt(jnp.mean(wide * wide, axis=1, keepdims=True) + EPS)
    unit = wide * scale
    grad_unit = total * gain_ref[...]
    mean = jnp.mean(grad_unit * unit, axis=1, keepdims=True)
    out_ref[...] = (up_ref[...].astype(F32) + scale * (grad_unit - unit * mean)).astype(BF16)
    gain_grad_ref[...] = jnp.sum(total * unit, axis=0, keepdims=True)


def finish_half(after, index, chunk, own, first, second, rows_in, gain=None, upstream=None):
    half, features = second.shape
    pick = pl.BlockSpec((half, features), lambda i, index_ref: (index_ref[0], 0))
    whole = pl.BlockSpec((half, features), lambda i, index_ref: (2 * chunk + index_ref[0], 0))
    same = pl.BlockSpec((half, features), lambda i, index_ref: (0, 0))
    one = pl.BlockSpec((1, features), lambda i, index_ref: (0, 0))
    in_specs = [pick, pick, same, whole]
    out_specs = [same]
    out_shape = [jax.ShapeDtypeStruct((half, features), BF16)]
    args = [own, first, second, rows_in]
    kernel = finish_out_kernel
    if upstream is not None:
        kernel = finish_back_kernel
        in_specs += [one, whole]
        out_specs.append(one)
        out_shape.append(jax.ShapeDtypeStruct((1, features), F32))
        args += [gain, upstream]
    return call(
        kernel,
        after,
        grid=(1,),
        in_specs=in_specs,
        out_specs=out_specs,
        out_shape=out_shape,
        name="finish_half",
        prefetch=1,
    )(index, *args, *after)


def weight_grads_kernel(per, *refs):
    out_ref = refs[-1]
    sums = [None, None, None]
    for m in range(per):
        normed_ref, up_ref, grads_ref, narrow_ref, normed_out_ref = refs[5 * m : 5 * m + 5]
        products = [
            lax.dot_general(left[...], right[...], TN, preferred_element_type=F32)
            for left, right in ((normed_ref, grads_ref), (normed_ref, narrow_ref), (up_ref, normed_out_ref))
        ]
        sums = products if m == 0 else [a + b for a, b in zip(sums, products)]
    at = 0
    for part in sums:
        out_ref[:, at : at + part.shape[1]] = part.astype(BF16)
        at += part.shape[1]


def weight_grads(after, terms):
    rows, features = terms[0][0].shape
    size = 256
    block = lambda shape, index: pl.BlockSpec(shape, index)
    in_specs = []
    args = []
    for normed, up, grads, narrow, normed_out in terms:
        in_specs += [block((rows, size), lambda f: (0, f))] * 2
        in_specs += [block(a.shape, lambda f: (0, 0)) for a in (grads, narrow, normed_out)]
        args += [normed, up, grads, narrow, normed_out]
    total = sum(a.shape[1] for a in terms[0][2:])
    return call(
        partial(weight_grads_kernel, len(terms)),
        after,
        grid=(features // size,),
        in_specs=in_specs,
        out_specs=block((size, total), lambda f: (f, 0)),
        out_shape=jax.ShapeDtypeStruct((features, total), BF16),
        name="weight_grads",
    )(*args, *after)


def neighbor(array, axis, by):
    length = lax.axis_size(axis)
    pairs = [(i, i + by) for i in range(length) if 0 <= i + by < length]
    return lax.ppermute(array, axis, pairs)


def swap(array):
    return lax.ppermute(array, "section", [(0, 1), (1, 0)])


def pass_states(packed, direction):
    return [neighbor(packed, "seq", direction * by) for by in range(1, lax.axis_size("seq"))]


def ring_parts(array, axis):
    length = lax.axis_size(axis)
    return [
        lax.ppermute(array, axis, [(i, (i + by) % length) for i in range(length)])
        for by in range(1, length)
    ]


class Order:
    def __init__(self):
        self.after = ()

    def __call__(self, result):
        self.after = (result[0] if isinstance(result, (list, tuple)) else result,)
        return result


def shards(
    layer_input, cotangent, pre_gain, proj_zx, proj_bc, proj_dt, kernel_inner, bias_inner,
    kernel_state, bias_state, step_bias, decay_log, skip_gain, norm_gain, proj_out,
):
    section = lax.axis_index("section")
    sections = lax.axis_size("section")
    micro, rows, features = layer_input.shape
    per = micro // sections
    width = norm_gain.shape[1]
    heads = step_bias.shape[1]
    total_width = width * lax.axis_size("head")
    taps = kernel_inner.shape[1]
    chunks = rows // GROUP
    assert lax.axis_size("head") == 4
    place = lax.axis_index("head")
    inner_place = (place == 1) | (place == 2)
    lower = place < 2
    keep = jnp.where(lower, 0, 1).astype(jnp.int32)[None]
    give = 1 - keep
    across = [(1, 2), (2, 1)]
    outward = [(1, 0), (2, 3)]
    order = Order()

    own_dt = jnp.pad(proj_dt[0], ((0, 0), (0, LANES - heads)))
    at_place = place.astype(jnp.int32)[None]
    pieces = {
        "pre_gain": pre_gain[0][None],
        "kernel_inner": kernel_inner[0],
        "bias_inner": bias_inner,
        "kernel_state": kernel_state[0],
        "bias_state": bias_state,
        "step_bias": jnp.pad(step_bias, ((0, 0), (0, LANES - heads))),
        "decay_log": jnp.pad(decay_log, ((0, 0), (0, LANES - heads))),
        "skip_wide": jnp.repeat(skip_gain, P_SIZE, axis=1),
        "norm_gain": norm_gain,
    }
    names = list(pieces)
    flat = jnp.concatenate([pieces[name].reshape(-1, LANES) for name in names], axis=0)
    own = (proj_zx[0], proj_bc[0], own_dt, proj_out[0], flat)
    other = tuple(swap(a) for a in own)
    layers = []
    for index in range(sections):
        mine = section == index
        w_zx, w_bc, w_dt, w_out, packed = (jnp.where(mine, a, b) for a, b in zip(own, other))
        small = {}
        at = 0
        for name in names:
            count = pieces[name].size // LANES
            small[name] = packed[at : at + count].reshape(pieces[name].shape)
            at += count
        layers.append((w_zx.reshape(features, 2 * width), w_bc, w_dt, w_out, small))

    span = range(per)
    mine_in = lax.dynamic_slice_in_dim(layer_input, section * per, per, 0)
    mine_back = lax.dynamic_slice_in_dim(cotangent, section * per, per, 0)

    class Micro:
        pass

    def enter(rows_in, layer):
        t = Micro()
        w_wide, w_bc, w_dt, t.w_out, t.small = layer
        t.layer, t.rows_in = layer, rows_in
        t.gain = t.small["norm_gain"]
        t.normed, t.pre, t.pre_st, edge, *rest = order(
            project(order.after, at_place, rows_in, t.small["pre_gain"], w_wide, w_bc, w_dt)
        )
        if rest:
            t.rows_in = rest[0]
        t.edge = neighbor(edge, "seq", 1)
        return t

    def scan(t, dot):
        t.local, t.kq, t.steps, t.within, t.starts, packed = order(
            scan_forward(order.after, dot, t.pre, t.pre_st, t.edge, t.small)
        )
        t.arrived = pass_states(packed, 1)

    def mix(t, dot, upstream=None):
        args = () if upstream is None else (upstream, t.w_out)
        t.mixer, t.before, stats, *t.back = order(
            mix_first(order.after, dot, t.local, t.pre, t.kq, t.within, t.gain, t.arrived, *args)
        )
        t.stats = [stats, *ring_parts(stats, "head")]

    def send_first(t, lows, owns):
        t.owns = owns
        t.firsts = [lax.ppermute(low, "head", [(0, 1), (3, 2)]) for low in lows]

    def out(t, c):
        if c == 0:
            t.stats = sum(t.stats)
            t.normed_out, t.owns, t.firsts = [], [], []
        normed, own, low = order(
            project_out(order.after, c, t.mixer, t.pre, t.gain, t.stats, t.w_out, total_width)
        )
        t.normed_out.append(normed)
        t.owns.append(own)
        t.firsts.append(lax.ppermute(low if WIRE == BF16 else own, "head", [(0, 1), (3, 2)]))
        if c == chunks - 1:
            t.normed_out = jnp.concatenate(t.normed_out, axis=0)

    def pass_half(t, c):
        if c == 0:
            t.seconds = []
        kind = t.firsts[c].dtype
        given = order(add_half(order.after, give, t.owns[c], t.firsts[c], kind))
        t.seconds.append(lax.ppermute(given, "head", across))

    def finish(t, c, upstream=None):
        if c == 0:
            t.pieces, t.gain_parts = [], []
        extra = () if upstream is None else (t.small["pre_gain"], upstream)
        done, *gain_part = order(
            finish_half(
                order.after, keep, c, t.owns[c], t.firsts[c], t.seconds[c], t.rows_in, *extra
            )
        )
        t.gain_parts += [jnp.where(inner_place, g, 0.0) for g in gain_part]
        crossed = lax.ppermute(done, "head", across)
        sent = lax.ppermute(done, "head", outward)
        passed = lax.ppermute(crossed, "head", outward)
        t.pieces += [done, sent, crossed, passed]

    def collect(t):
        return order(gather(order.after, at_place, t.pieces))

    def mix_up(t, with_part):
        square = sum(t.stats) if with_part else t.stats
        product = square if with_part else sum(t.products)
        extra = (t.w_out,) if with_part else ()
        t.grad, t.gate_grad, t.gain_grad, packed, *rest = order(
            mix_back(
                order.after, t.back, t.mixer, t.pre, t.kq, t.within, t.gain, square, product, total_width, *extra
            )
        )
        t.later = pass_states(packed, -1)
        if with_part:
            t.normed_out = rest[0]
            send_first(t, rest[1:], rest[1:])

    def back_start(t, pieces):
        t.upstream, t.back, product = order(
            back_first(order.after, at_place, pieces, t.w_out, t.mixer, t.pre, t.gain)
        )
        t.products = [product, *ring_parts(product, "head")]

    def scan_back(t):
        t.inner, edge_in, t.small_in, t.state, edge_st, t.small_st, t.raw, t.small_dt = order(
            scan_backward(
                order.after, t.pre, t.pre_st, t.edge, t.small, t.kq, t.steps, t.within, t.starts, t.before, t.later, t.grad
            )
        )
        t.edges = neighbor(jnp.concatenate([edge_in, edge_st], axis=1), "seq", -1)

    def back_out(t, upstream):
        r = Micro()
        r.rows_in, r.small = t.rows_in, t.small
        grads, narrow, *parts = order(
            project_back(
                order.after, t.gate_grad, t.inner, t.state, t.raw, t.edges, *t.layer[:3]
            )
        )
        send_first(r, parts, parts)
        t.weights = (t.normed, upstream, grads, narrow, t.normed_out)
        return r

    dot0, dot1 = high_dot, low_dot
    a, b = 0, 1
    f0 = [enter(mine_in[m], layers[0]) for m in span]
    for t in f0:
        scan(t, dot0)
    for t in f0:
        mix(t, dot0)
    for t in f0:
        for c in range(chunks):
            out(t, c)
    jobs = [(t, c) for t in f0 for c in range(chunks)]
    for k in range(len(jobs) + 1):
        if k < len(jobs):
            pass_half(*jobs[k])
        if k > 0:
            finish(*jobs[k - 1])
    f1 = []
    for m in span:
        f1.append(enter(f0[m].pieces, layers[1]))
        scan(f1[m], dot1)
        mix(f1[m], dot1, mine_back[m])
        f1[m].back = f1[m].back[0]
        mix_up(f1[m], True)
    b1 = []
    for m in span:
        scan_back(f1[m])
        b1.append(back_out(f1[m], mine_back[m]))
    jobs = [(b1[m], c, mine_back[m]) for m in span for c in range(chunks)]
    given1 = None
    for k in range(len(jobs) + 1):
        if k < len(jobs):
            pass_half(*jobs[k][:2])
        if k > 0:
            finish(*jobs[k - 1])
        if k == 1:
            given1 = order(weight_grads(order.after, [t.weights for t in f1]))
    for m in span:
        back_start(f0[m], b1[m].pieces)
    for m in span:
        mix_up(f0[m], False)
    for c in range(chunks):
        pass_half(f1[0], c)
    for c in range(chunks):
        finish(f1[0], c)
    b0 = []
    for m in span:
        scan_back(f0[m])
        if m == 0:
            for c in range(chunks):
                pass_half(f1[1], c)
        else:
            for c in range(chunks):
                finish(f1[1], c)
        b0.append(back_out(f0[m], f0[m].upstream))
    outs1 = [collect(t) for t in f1]
    jobs = [(b0[m], c, f0[m].upstream) for m in span for c in range(chunks)]
    for k in range(len(jobs) + 1):
        if k < len(jobs):
            pass_half(*jobs[k][:2])
        if k > 0:
            finish(*jobs[k - 1])
        if k == 1:
            given0 = order(weight_grads(order.after, [t.weights for t in f0]))
    sents0 = [collect(t) for t in b0]
    outs0 = [t.rows_in for t in f1]
    sents1 = [t.upstream for t in f0]

    def place_layers(first_layer, second_layer):
        both = [jnp.stack(first_layer), jnp.stack(second_layer)]
        kept = jnp.where(section == 0, both[0], both[1])
        moved = swap(jnp.where(section == 0, both[1], both[0]))
        return jnp.where(
            section == 0,
            jnp.concatenate([kept, moved], axis=0),
            jnp.concatenate([moved, kept], axis=0),
        )

    layer_out = place_layers(outs0, outs1)
    layer_grad = place_layers(sents0, sents1)

    seqs = lax.axis_size("seq")
    share = features // seqs
    half = share // sections

    def reduce_weights(total):
        total = total.reshape(seqs, sections, half, -1)
        kept = lax.dynamic_index_in_dim(total, section, 1, False)
        given = lax.dynamic_index_in_dim(total, 1 - section, 1, False)
        summed = (kept.astype(F32) + swap(given).astype(F32)).astype(BF16).reshape(seqs * half, -1)
        return lax.psum_scatter(summed, "seq", scatter_dimension=0, tiled=True)

    reduced = [reduce_weights(given0), reduce_weights(given1)]
    kept = jnp.where(section == 0, reduced[0], reduced[1])
    moved = swap(jnp.where(section == 0, reduced[1], reduced[0]))
    weights = jnp.where(
        section == 0,
        jnp.concatenate([kept, moved], axis=0),
        jnp.concatenate([moved, kept], axis=0),
    ).astype(F32)
    grad_zx = weights[:, : 2 * width].reshape(share, 2, width)
    grad_bc = lax.psum_scatter(
        weights[:, 2 * width : 2 * width + 2 * NS], "head", scatter_dimension=0, tiled=True
    )
    grad_dt = weights[:, 2 * width + 2 * NS : 2 * width + 2 * NS + heads]
    grad_out = weights[:, 2 * width + 2 * NS + LANES :].T

    def join(tasks, sums):
        parts = [
            sum(getattr(t, name) for t in tasks).reshape(-1, LANES)
            for name in ("small_in", "gain_grad", "small_dt", "small_st")
        ]
        gains = sum(sum(t.gain_parts) for t in sums)
        return jnp.concatenate([*parts, gains.reshape(-1, LANES)], axis=0)

    smalls = jnp.stack([join(f0, b0), join(f1, b1)])
    smalls = lax.psum(smalls, ("section", "seq"))
    smalls = lax.dynamic_index_in_dim(smalls, section, 0, False)
    inner_rows = 8 * width // LANES
    gain_rows = width // LANES
    at = 0
    small_in = smalls[at : at + inner_rows].reshape(8, width)
    at += inner_rows
    gain_grad = smalls[at : at + gain_rows].reshape(width)
    at += gain_rows
    small_dt = smalls[at : at + 8]
    at += 8
    shared = lax.psum(smalls[at:], "head")
    small_st = shared[: 8 * 2 * NS // LANES].reshape(8, 2 * NS)
    grad_pre = shared[8 * 2 * NS // LANES :].reshape(features)
    grad_pre = lax.dynamic_slice_in_dim(grad_pre, lax.axis_index("seq") * share, share, 0)
    parts = seqs * lax.axis_size("head")
    st_width = 2 * NS // parts
    st_at = (lax.axis_index("seq") * lax.axis_size("head") + lax.axis_index("head")) * st_width
    small_st = lax.dynamic_slice_in_dim(small_st, st_at, st_width, 1)
    return (
        layer_out[None],
        layer_grad[None],
        grad_pre[None],
        grad_zx[None],
        grad_bc[None],
        grad_dt[None],
        small_in[None, :taps],
        small_in[None, taps],
        small_st[None, :taps],
        small_st[None, taps],
        small_dt[None, 0, :heads],
        small_dt[None, 1, :heads],
        small_in[None, taps + 1].reshape(1, heads, P_SIZE).sum(axis=2),
        gain_grad[None],
        grad_out[None],
    )


def solution(mesh):
    return jax.shard_map(
        shards,
        mesh=mesh,
        in_specs=(
            P(None, "seq", None),
            P(None, "seq", None),
            P("section", None),
            P("section", None, None, "head"),
            P("section", None, None),
            P("section", None, "head"),
            P("section", None, "head"),
            P("section", "head"),
            P("section", None, None),
            P("section", None),
            P("section", "head"),
            P("section", "head"),
            P("section", "head"),
            P("section", "head"),
            P("section", "head", None),
        ),
        out_specs=(
            P("section", None, "seq", None),
            P("section", None, "seq", None),
            P("section", "seq"),
            P("section", "seq", None, "head"),
            P("section", ("seq", "head"), None),
            P("section", "seq", "head"),
            P("section", None, "head"),
            P("section", "head"),
            P("section", None, ("seq", "head")),
            P("section", ("seq", "head")),
            P("section", "head"),
            P("section", "head"),
            P("section", "head"),
            P("section", "head"),
            P("section", "head", "seq"),
        ),
        check_vma=False,
    )
```

```python
from functools import partial

import jax
import jax.numpy as jnp
from jax import lax
from jax.experimental import pallas as pl
from jax.experimental.pallas import tpu as pltpu
from jax.sharding import PartitionSpec as P

P_SIZE = 64
NS = 128
GROUP = 256
LANES = 128
EDGE = 8
PACK = 16
BLOCK = 256

EPS = 1e-05
HIGH = lax.Precision.HIGHEST
F32 = jnp.float32
BF16 = jnp.bfloat16
VMEM_LIMIT = 60 * 1024 * 1024
HEAD, SEQ, SECTION = "head", "seq", "section"
WIRE = F32

NN = (((1,), (0,)), ((), ()))
NT = (((1,), (1,)), ((), ()))
TN = (((0,), (0,)), ((), ()))


def call(kernel, after, grid, in_specs, out_specs, out_shape, scratch_shapes=(), prefetch=0):
    count = prefetch + len(in_specs)

    def body(*refs):
        kernel(*refs[:count], *refs[count + len(after) :])

    return pl.pallas_call(
        body,
        grid_spec=pltpu.PrefetchScalarGridSpec(
            num_scalar_prefetch=prefetch,
            grid=grid,
            in_specs=[*in_specs, *[pl.BlockSpec(memory_space=pl.ANY)] * len(after)],
            out_specs=out_specs,
            scratch_shapes=scratch_shapes,
        ),
        out_shape=out_shape,
        compiler_params=pltpu.CompilerParams(vmem_limit_bytes=VMEM_LIMIT),
        name=getattr(kernel, "func", kernel).__name__,
    )


def low_dot(a, b, dims):
    return lax.dot_general(a.astype(BF16), b.astype(BF16), dims, preferred_element_type=F32)


def high_dot(a, b, dims):
    return lax.dot_general(a, b, dims, precision=HIGH, preferred_element_type=F32)


def split_dot(a, b, dims):
    a_high, b_high = a.astype(BF16), b.astype(BF16)
    a_low = (a - a_high.astype(F32)).astype(BF16)
    b_low = (b - b_high.astype(F32)).astype(BF16)
    dot = partial(lax.dot_general, dimension_numbers=dims, preferred_element_type=F32)
    return dot(a_high, b_high) + (dot(a_high, b_low) + dot(a_low, b_high))


def iota(shape, dim):
    return lax.broadcasted_iota(jnp.int32, shape, dim)


def softplus(v):
    return jnp.maximum(v, 0.0) + jnp.log1p(jnp.exp(-jnp.abs(v)))


def sigmoid(v):
    return 1.0 / (1.0 + jnp.exp(-v))


def column(values, lane):
    return jnp.sum(jnp.where(iota(values.shape, 1) == lane, values, 0.0), axis=1, keepdims=True)


def convolve(ext_ref, kernel_ref, bias_ref, rows):
    taps = kernel_ref.shape[0]
    total = bias_ref[...] + kernel_ref[0:1, :] * ext_ref[EDGE - taps + 1 : EDGE - taps + 1 + rows, :]
    for k in range(1, taps):
        at = EDGE - taps + 1 + k
        total = total + kernel_ref[k : k + 1, :] * ext_ref[at : at + rows, :]
    return total


def convolve_back(grad_ref, ext_ref, kernel_ref, grad, rows):
    taps = kernel_ref.shape[0]
    width = grad.shape[1]
    grad_ref[0:EDGE, :] = jnp.zeros((EDGE, width), F32)
    grad_ref[EDGE : EDGE + rows, :] = grad
    grad_ref[EDGE + rows :, :] = jnp.zeros((EDGE, width), F32)
    total = kernel_ref[0:1, :] * grad_ref[taps - 1 : taps - 1 + rows + EDGE, :]
    for k in range(1, taps):
        at = taps - 1 - k
        total = total + kernel_ref[k : k + 1, :] * grad_ref[at : at + rows + EDGE, :]
    small = []
    for k in range(taps):
        at = EDGE - taps + 1 + k
        small.append(jnp.sum(grad * ext_ref[at : at + rows, :], axis=0, keepdims=True))
    small.append(jnp.sum(grad, axis=0, keepdims=True))
    return total, small


def chunk_sums(steps, decay_log, rows):
    rates = -steps * jnp.exp(decay_log)
    lower = jnp.where(iota((GROUP, GROUP), 0) >= iota((GROUP, GROUP), 1), 1.0, 0.0)
    parts = [high_dot(lower, rates[at : at + GROUP], NN) for at in range(0, rows, GROUP)]
    return rates, jnp.concatenate(parts, axis=0)


def pair_select(first, second, shape, dim):
    return jnp.where(iota(shape, dim) < P_SIZE, first, second)


def pack_decay(packed_ref, within_ref, chunks):
    total = within_ref[GROUP - 1 : GROUP, :]
    for c in range(1, chunks):
        total = total + within_ref[(c + 1) * GROUP - 1 : (c + 1) * GROUP, :]
    decay = jnp.exp(total)
    kind = packed_ref.dtype
    high = decay.astype(kind)
    rest = (decay - high.astype(F32)).astype(kind)
    packed_ref[packed_ref.shape[0] - PACK :, :] = jnp.concatenate(
        [high, rest, jnp.zeros((PACK - 2, LANES), kind)], axis=0
    )


def head_factors(decay, count, first_head):
    owner = iota((count, LANES), 0) // P_SIZE + first_head
    return jnp.sum(jnp.where(iota((count, LANES), 1) == owner, decay, 0.0), axis=1, keepdims=True)


def decay_of(rows):
    return rows[0:1, :].astype(F32) + rows[1:2, :].astype(F32)


def unpack_states(seq, forward, state_refs, decay_rows, first_head):
    count = state_refs[0].shape[0]
    total = jnp.zeros((count, NS), F32)
    passed = jnp.ones((1, LANES), F32)
    for level, (ref, rows) in enumerate(zip(state_refs, decay_rows)):
        used = (lax.shift_right_logical(seq, level) & 1) == (1 if forward else 0)
        part = head_factors(passed, count, first_head) * ref[...].astype(F32)
        total = total + jnp.where(used, part, 0.0)
        passed = jnp.where(used, passed * decay_of(rows), passed)
    return total


def merge_kernel(forward, level, seq_ref, own_ref, got_ref, out_ref):
    width = own_ref.shape[0] - PACK
    right = (lax.shift_right_logical(seq_ref[0], level) & 1) == 1
    own_late = right if forward else jnp.logical_not(right)
    own, got = own_ref[0:width, :].astype(F32), got_ref[0:width, :].astype(F32)
    own_decay, got_decay = decay_of(own_ref[width:, :]), decay_of(got_ref[width:, :])
    decay = jnp.where(own_late, own_decay, got_decay)
    factors = head_factors(decay, width, 0)
    out_ref[0:width, :] = (
        factors * jnp.where(own_late, got, own) + jnp.where(own_late, own, got)
    ).astype(out_ref.dtype)
    both = own_decay * got_decay
    high = both.astype(out_ref.dtype)
    rest = (both - high.astype(F32)).astype(out_ref.dtype)
    out_ref[width:, :] = jnp.concatenate(
        [high, rest, jnp.zeros((PACK - 2, LANES), out_ref.dtype)], axis=0
    )


def merge(after, seq, forward, level, own, got):
    spec = pl.BlockSpec(own.shape, lambda i, seq_ref: (0, 0))
    return call(
        partial(merge_kernel, forward, level),
        after,
        grid=(1,),
        in_specs=[spec, spec],
        out_specs=spec,
        out_shape=jax.ShapeDtypeStruct(own.shape, own.dtype),
        prefetch=1,
    )(seq, own, got, *after)


def stat_add_kernel(a_ref, b_ref, out_ref):
    out_ref[...] = a_ref[...] + b_ref[...]


def stat_add(after, a, b):
    spec = pl.BlockSpec(a.shape, lambda i: (0, 0))
    return call(
        stat_add_kernel,
        after,
        grid=(1,),
        in_specs=[spec, spec],
        out_specs=spec,
        out_shape=jax.ShapeDtypeStruct(a.shape, a.dtype),
    )(a, b, *after)


def scan_forward_kernel(
    dot,
    inner_ref, state_ref, dt_ref, edge_in_ref, edge_st_ref, ker_in_ref, bias_in_ref,
    ker_st_ref, bias_st_ref, step_bias_ref, decay_ref, skip_ref,
    out_ref, kq_ref, step_ref, within_ref, starts_ref, packed_ref,
    scores_ref, turned_ref, ext_ref, ext_st_ref,
):
    pair = pl.program_id(0)
    rows = inner_ref.shape[0]
    chunks = rows // GROUP

    @pl.when(pair == 0)
    def _():
        ext_st_ref[0:EDGE, :] = edge_st_ref[...]
        ext_st_ref[EDGE:, :] = state_ref[...]
        pre = convolve(ext_st_ref, ker_st_ref, bias_st_ref, rows)
        kq_ref[...] = pre * sigmoid(pre)
        steps = softplus(dt_ref[...] + step_bias_ref[...])
        _, within = chunk_sums(steps, decay_ref[...], rows)
        step_ref[...] = steps
        within_ref[...] = within
        turned_ref[...] = within.T
        pack_decay(packed_ref, within_ref, chunks)
        for c in range(chunks):
            at = slice(c * GROUP, (c + 1) * GROUP)
            scores_ref[c] = high_dot(kq_ref[at, NS:], kq_ref[at, :NS], NT)

    ext_ref[0:EDGE, :] = edge_in_ref[...]
    ext_ref[EDGE:, :] = inner_ref[...]
    pre = convolve(ext_ref, ker_in_ref, bias_in_ref, rows)
    values = pre * sigmoid(pre)
    within_cols = [column(within_ref[...], 2 * pair + k) for k in range(2)]
    step_cols = [column(step_ref[...], 2 * pair + k) for k in range(2)]
    shape = (rows, LANES)
    scaled = values * pair_select(step_cols[0], step_cols[1], shape, 1)
    within_wide = pair_select(within_cols[0], within_cols[1], shape, 1)
    causal = iota((GROUP, GROUP), 0) >= iota((GROUP, GROUP), 1)
    state = jnp.zeros((LANES, NS), F32)
    for c in range(chunks):
        at = slice(c * GROUP, (c + 1) * GROUP)
        scaled_low = scaled[at]
        halves = []
        ends = []
        for k in range(2):
            row = turned_ref[pl.ds(2 * pair + k, 1), at]
            decays = jnp.exp(jnp.where(causal, within_cols[k][at] - row, -1e30))
            halves.append(dot(decays * scores_ref[c], scaled_low, NN))
            ends.append(within_cols[k][(c + 1) * GROUP - 1 : (c + 1) * GROUP])
        result = pair_select(halves[0], halves[1], (GROUP, LANES), 1)
        if c > 0:
            result = result + jnp.exp(within_wide[at]) * dot(kq_ref[at, NS:], state, NT)
        out_ref[at, :] = result + skip_ref[...] * values[at]
        starts_ref[c] = state
        end_wide = pair_select(ends[0], ends[1], (1, LANES), 1)
        tail = jnp.exp(end_wide - within_wide[at])
        piece = dot(scaled[at] * tail, kq_ref[at, :NS], TN)
        state = jnp.exp(pair_select(ends[0], ends[1], (LANES, 1), 0)) * state + piece
    packed_ref[pl.ds(pl.multiple_of(pair * LANES, LANES), LANES), :] = state


def scan_forward(after, dot, pre, pre_st, edge, small):
    rows = pre.shape[0]
    width = small["bias_inner"].shape[1]
    pairs = width // LANES
    chunks = rows // GROUP
    taps = small["kernel_inner"].shape[0]
    block = lambda shape, index: pl.BlockSpec(shape, index)
    const2 = lambda p: (0, 0)
    return call(
        partial(scan_forward_kernel, dot),
        after,
        grid=(pairs,),
        in_specs=[
            block((rows, LANES), lambda p: (0, pairs + p)),
            block((rows, 2 * NS), lambda p: (0, 0)),
            block((rows, LANES), lambda p: (0, 2)),
            block((EDGE, LANES), lambda p: (0, p)),
            block((EDGE, 2 * NS), lambda p: (0, pairs // 2)),
            block((taps, LANES), lambda p: (0, p)),
            block((1, LANES), lambda p: (0, p)),
            block((taps, 2 * NS), const2),
            block((1, 2 * NS), const2),
            block((1, LANES), const2),
            block((1, LANES), const2),
            block((1, LANES), lambda p: (0, p)),
        ],
        out_specs=[
            block((rows, LANES), lambda p: (0, p)),
            block((rows, 2 * NS), const2),
            block((rows, LANES), const2),
            block((rows, LANES), const2),
            block((chunks, LANES, NS), lambda p: (0, p, 0)),
            block((width + PACK, NS), const2),
        ],
        out_shape=[
            jax.ShapeDtypeStruct((rows, width), F32),
            jax.ShapeDtypeStruct((rows, 2 * NS), F32),
            jax.ShapeDtypeStruct((rows, LANES), F32),
            jax.ShapeDtypeStruct((rows, LANES), F32),
            jax.ShapeDtypeStruct((chunks, width, NS), F32),
            jax.ShapeDtypeStruct((width + PACK, NS), F32),
        ],
        scratch_shapes=[
            pltpu.VMEM((chunks, GROUP, GROUP), F32),
            pltpu.VMEM((LANES, rows), F32),
            pltpu.VMEM((rows + EDGE, LANES), F32),
            pltpu.VMEM((rows + EDGE, 2 * NS), F32),
        ],
    )(
        pre, pre_st, pre_st, edge, edge, small["kernel_inner"], small["bias_inner"],
        small["kernel_state"], small["bias_state"], small["step_bias"], small["decay_log"],
        small["skip_wide"], *after,
    )


def scan_backward_kernel(
    seq_ref, inner_ref, state_ref, dt_ref, edge_in_ref, edge_st_ref, ker_in_ref, bias_in_ref,
    ker_st_ref, bias_st_ref, step_bias_ref, decay_ref, skip_ref,
    kq_ref, step_ref, within_ref, starts_ref, before_ref, grad_ref, *refs,
):
    arrived = len(refs) - 19
    after_refs, decay_refs, refs = refs[: arrived // 2], refs[arrived // 2 : arrived], refs[arrived:]
    (inner_out, edge_out, small_in_out, state_out, small_st_out, raw_out, small_dt_out,
    scores_ref, turned_ref, ext_ref, ext_st_ref, back_ref, back_st_ref,
    grad_scores, grad_kq, grad_within, grad_turned, grad_steps, grad_ends) = refs
    pair = pl.program_id(0)
    rows = inner_ref.shape[0]
    chunks = rows // GROUP
    taps = ker_in_ref.shape[0]

    @pl.when(pair == 0)
    def _():
        turned_ref[...] = within_ref[...].T
        for c in range(chunks):
            at = slice(c * GROUP, (c + 1) * GROUP)
            scores_ref[c] = high_dot(kq_ref[at, NS:], kq_ref[at, :NS], NT)
        for ref in (grad_scores, grad_kq, grad_within, grad_turned, grad_steps, grad_ends):
            ref[...] = jnp.zeros_like(ref)

    ext_ref[0:EDGE, :] = edge_in_ref[...]
    ext_ref[EDGE:, :] = inner_ref[...]
    pre = convolve(ext_ref, ker_in_ref, bias_in_ref, rows)
    sig = sigmoid(pre)
    values = pre * sig
    shape = (rows, LANES)
    within_cols = [column(within_ref[...], 2 * pair + k) for k in range(2)]
    step_cols = [column(step_ref[...], 2 * pair + k) for k in range(2)]
    step_wide = pair_select(step_cols[0], step_cols[1], shape, 1)
    scaled = values * step_wide
    within_wide = pair_select(within_cols[0], within_cols[1], shape, 1)
    causal = iota((GROUP, GROUP), 0) >= iota((GROUP, GROUP), 1)
    first_half = iota((GROUP, LANES), 1) < P_SIZE
    lanes = iota((1, LANES), 1)
    pick = jnp.where(
        iota((LANES, LANES), 1) == 2 * pair + iota((LANES, LANES), 0) // P_SIZE, 1.0, 0.0
    )
    ends = [
        [within_cols[k][(c + 1) * GROUP - 1 : (c + 1) * GROUP] for k in range(2)]
        for c in range(chunks)
    ]
    passed = [[jnp.zeros((1, 1), F32)] * 2]
    for c in range(chunks - 1):
        passed.append([passed[c][k] + ends[c][k] for k in range(2)])
    state_grad = unpack_states(
        seq_ref[0], False, after_refs, [ref[...] for ref in decay_refs], 2 * pair
    )
    value_grads = [None] * chunks
    for c in reversed(range(chunks)):
        at = slice(c * GROUP, (c + 1) * GROUP)
        start_decay = jnp.exp(pair_select(passed[c][0], passed[c][1], (LANES, 1), 0))
        state = starts_ref[c] + start_decay * before_ref[...]
        grad = grad_ref[at, :]
        grad_low = grad.astype(BF16)
        scaled_low = scaled[at].astype(BF16)
        keys = kq_ref[at, :NS].astype(BF16)
        reads = kq_ref[at, NS:].astype(BF16)
        state_low = state.astype(BF16)
        state_grad_low = state_grad.astype(BF16)
        halves = []
        for k in range(2):
            head = 2 * pair + k
            row = turned_ref[pl.ds(head, 1), at]
            decays = jnp.exp(jnp.where(causal, within_cols[k][at] - row, -1e30))
            weights = decays * scores_ref[c]
            mine = first_half if k == 0 else jnp.logical_not(first_half)
            own = jnp.where(mine, grad, 0.0).astype(BF16)
            weight_grad = lax.dot_general(own, scaled_low, NT, preferred_element_type=F32)
            halves.append(low_dot(weights, grad_low, TN))
            grad_scores[c] += weight_grad * decays
            moved = weight_grad * weights
            grad_within[at, :] += jnp.where(
                lanes == head, jnp.sum(moved, axis=1, keepdims=True), 0.0
            )
            grad_turned[pl.ds(head, 1), at] = jnp.sum(moved, axis=0, keepdims=True)
        scaled_grad = pair_select(halves[0], halves[1], (GROUP, LANES), 1)
        end_wide = pair_select(ends[c][0], ends[c][1], (1, LANES), 1)
        tail = jnp.exp(end_wide - within_wide[at])
        late = tail * lax.dot_general(keys, state_grad_low, NT, preferred_element_type=F32)
        late_sums = high_dot(scaled[at] * late, pick, NN)
        scaled_grad = scaled_grad + late
        grad_kq[at, :NS] += low_dot(scaled[at] * tail, state_grad_low, NN)
        entry = jnp.exp(within_wide[at])
        early = entry * lax.dot_general(reads, state_low, NT, preferred_element_type=F32)
        early_sums = high_dot(grad * early, pick, NN)
        grad_entry = (grad * entry).astype(BF16)
        grad_kq[at, NS:] += lax.dot_general(grad_entry, state_low, NN, preferred_element_type=F32)
        grad_within[at, :] += early_sums - late_sums
        end_decay = jnp.exp(pair_select(ends[c][0], ends[c][1], (LANES, 1), 0))
        kept = end_decay * state_grad * state
        kept_sum = jnp.sum(kept, axis=1, keepdims=True)
        kept_sums = jnp.sum(kept_sum * pick, axis=0, keepdims=True)
        grad_ends[c : c + 1, :] += jnp.sum(late_sums, axis=0, keepdims=True) + kept_sums
        grad_steps[at, :] += high_dot(values[at] * scaled_grad, pick, NN)
        value_grads[c] = step_wide[at] * scaled_grad + skip_ref[...] * grad
        state_grad = end_decay * state_grad + lax.dot_general(
            grad_entry, reads, TN, preferred_element_type=F32
        )
    value_grad = jnp.concatenate(value_grads, axis=0)
    pre_grad = value_grad * sig * (1.0 + pre * (1.0 - sig))
    total, small = convolve_back(back_ref, ext_ref, ker_in_ref, pre_grad, rows)
    edge_out[:, pl.ds(pl.multiple_of(pair * LANES, LANES), LANES)] = total[0:EDGE]
    inner_out[...] = total[EDGE:]
    small.append(jnp.sum(grad_ref[...] * values, axis=0, keepdims=True))
    small.append(jnp.zeros((8 - len(small), LANES), F32))
    small_in_out[...] = jnp.concatenate(small, axis=0)

    @pl.when(pair == pl.num_programs(0) - 1)
    def _():
        upper = jnp.where(iota((GROUP, GROUP), 0) <= iota((GROUP, GROUP), 1), 1.0, 0.0)
        scale = -jnp.exp(decay_ref[...])
        decay_grad = jnp.zeros((1, LANES), F32)
        back = grad_turned[...].T
        for c in range(chunks):
            at = slice(c * GROUP, (c + 1) * GROUP)
            grad_kq[at, NS:] += high_dot(grad_scores[c], kq_ref[at, :NS], NN)
            grad_kq[at, :NS] += high_dot(grad_scores[c], kq_ref[at, NS:], TN)
            rate_grad = high_dot(upper, grad_within[at, :] - back[at], NN) + grad_ends[c : c + 1, :]
            grad_steps[at, :] += rate_grad * scale
            decay_grad += jnp.sum(rate_grad * scale * step_ref[at, :], axis=0, keepdims=True)
        raw = grad_steps[...] * sigmoid(dt_ref[...] + step_bias_ref[...])
        raw_out[...] = raw
        raw_sum = jnp.sum(raw, axis=0, keepdims=True)
        small_dt_out[...] = jnp.concatenate(
            [raw_sum, decay_grad, jnp.zeros((6, LANES), F32)], axis=0
        )
        ext_st_ref[0:EDGE, :] = edge_st_ref[...]
        ext_st_ref[EDGE:, :] = state_ref[...]
        pre_st = convolve(ext_st_ref, ker_st_ref, bias_st_ref, rows)
        sig_st = sigmoid(pre_st)
        pre_st_grad = grad_kq[...] * sig_st * (1.0 + pre_st * (1.0 - sig_st))
        total_st, small_st = convolve_back(back_st_ref, ext_st_ref, ker_st_ref, pre_st_grad, rows)
        edge_out[:, edge_out.shape[1] - 2 * NS :] = total_st[0:EDGE]
        state_out[...] = total_st[EDGE:]
        small_st.append(jnp.zeros((8 - len(small_st), 2 * NS), F32))
        small_st_out[...] = jnp.concatenate(small_st, axis=0)


def scan_backward(after, seq, pre, pre_st, edge, small, kq, steps, within, starts, before, later, grad):
    rows = pre.shape[0]
    width = grad.shape[1]
    pairs = width // LANES
    chunks = rows // GROUP
    taps = small["kernel_inner"].shape[0]
    block = lambda shape, index: pl.BlockSpec(shape, index)
    const2 = lambda p, seq_ref: (0, 0)
    lane2 = lambda p, seq_ref: (0, p)
    return call(
        scan_backward_kernel,
        after,
        grid=(pairs,),
        in_specs=[
            block((rows, LANES), lambda p, seq_ref: (0, pairs + p)),
            block((rows, 2 * NS), lambda p, seq_ref: (0, 0)),
            block((rows, LANES), lambda p, seq_ref: (0, 2)),
            block((EDGE, LANES), lane2),
            block((EDGE, 2 * NS), lambda p, seq_ref: (0, pairs // 2)),
            block((taps, LANES), lane2),
            block((1, LANES), lane2),
            block((taps, 2 * NS), const2),
            block((1, 2 * NS), const2),
            block((1, LANES), const2),
            block((1, LANES), const2),
            block((1, LANES), lane2),
            block((rows, 2 * NS), const2),
            block((rows, LANES), const2),
            block((rows, LANES), const2),
            block((chunks, LANES, NS), lambda p, seq_ref: (0, p, 0)),
            block((LANES, NS), lambda p, seq_ref: (p, 0)),
            block((rows, LANES), lane2),
        ]
        + [block((LANES, NS), lambda p, seq_ref: (p, 0))] * len(later)
        + [block((PACK, NS), lambda p, seq_ref: (width // PACK, 0))] * len(later),
        out_specs=[
            block((rows, LANES), lane2),
            block((EDGE, width + 2 * NS), const2),
            block((8, LANES), lane2),
            block((rows, 2 * NS), const2),
            block((8, 2 * NS), const2),
            block((rows, LANES), const2),
            block((8, LANES), const2),
        ],
        out_shape=[
            jax.ShapeDtypeStruct((rows, width), F32),
            jax.ShapeDtypeStruct((EDGE, width + 2 * NS), F32),
            jax.ShapeDtypeStruct((8, width), F32),
            jax.ShapeDtypeStruct((rows, 2 * NS), F32),
            jax.ShapeDtypeStruct((8, 2 * NS), F32),
            jax.ShapeDtypeStruct((rows, LANES), F32),
            jax.ShapeDtypeStruct((8, LANES), F32),
        ],
        scratch_shapes=[
            pltpu.VMEM((chunks, GROUP, GROUP), F32),
            pltpu.VMEM((LANES, rows), F32),
            pltpu.VMEM((rows + EDGE, LANES), F32),
            pltpu.VMEM((rows + EDGE, 2 * NS), F32),
            pltpu.VMEM((rows + 2 * EDGE, LANES), F32),
            pltpu.VMEM((rows + 2 * EDGE, 2 * NS), F32),
            pltpu.VMEM((chunks, GROUP, GROUP), F32),
            pltpu.VMEM((rows, 2 * NS), F32),
            pltpu.VMEM((rows, LANES), F32),
            pltpu.VMEM((LANES, rows), F32),
            pltpu.VMEM((rows, LANES), F32),
            pltpu.VMEM((8, LANES), F32),
        ],
        prefetch=1,
    )(
        seq, pre, pre_st, pre_st, edge, edge, small["kernel_inner"], small["bias_inner"],
        small["kernel_state"], small["bias_state"], small["step_bias"], small["decay_log"],
        small["skip_wide"], kq, steps, within, starts, before, grad, *later, *later, *after,
    )


def widen(values, width):
    spread = jnp.where(
        iota((LANES, width), 1) // P_SIZE == iota((LANES, width), 0), 1.0, 0.0
    ).astype(BF16)
    high = values.astype(BF16)
    rest = (values - high.astype(F32)).astype(BF16)
    return lax.dot_general(high, spread, NN, preferred_element_type=F32) + lax.dot_general(
        rest, spread, NN, preferred_element_type=F32
    )


def entry_decay(within_ref, chunk, chunks):
    offset = jnp.zeros((1, LANES), F32)
    for c in range(chunks - 1):
        offset = offset + jnp.where(c < chunk, within_ref[(c + 1) * GROUP - 1 : (c + 1) * GROUP, :], 0.0)
    at = pl.multiple_of(chunk * GROUP, GROUP)
    return jnp.exp(within_ref[pl.ds(at, GROUP), :] + offset)


def stat_columns(stat_refs):
    height, length = stat_refs[0].shape
    total = stat_refs[0][...]
    for ref in stat_refs[1:]:
        total = total + ref[...]
    return jnp.concatenate([total, jnp.zeros((LANES - height, length), F32)], axis=0).T


def mix_first_kernel(dot, chunks, arrived, with_grad, seq_ref, *refs):
    local_ref, gate_ref, reads_ref, within_ref, gain_ref = refs[:5]
    arrived_refs = refs[5 : 5 + arrived]
    refs = refs[5 + arrived :]
    if with_grad:
        proj_ref, up_ref, mixer_ref, before_ref, stats_ref, back_ref = refs
    else:
        mixer_ref, before_ref, stats_ref = refs
    width = local_ref.shape[1]
    chunk = pl.program_id(0)

    @pl.when(chunk == 0)
    def _():
        states = [ref.at[0:width, :] for ref in arrived_refs]
        decays = [ref[width:, :] for ref in arrived_refs]
        before_ref[...] = unpack_states(seq_ref[0], True, states, decays, 0)

    entry = widen(entry_decay(within_ref, chunk, chunks), width)
    mixer = local_ref[...] + entry * dot(reads_ref[...], before_ref[...], NT)
    mixer_ref[...] = mixer
    gate = gate_ref[...]
    gated = mixer * gate * sigmoid(gate)
    ones = jnp.ones((8, width), F32)
    stats = high_dot(ones, gated * gated, NT)
    if with_grad:
        back = lax.dot_general(up_ref[...], proj_ref[...], NT, preferred_element_type=F32)
        back_ref[...] = back
        other = high_dot(ones, back * gated * gain_ref[...], NT)
        stats = jnp.where(iota(stats.shape, 0) == 1, other, stats)
    stats_ref[...] = stats


def mix_first(after, seq, dot, local, pre, kq, within, gain, arrived, upstream=None, proj_out=None):
    rows, width = local.shape
    chunks = rows // GROUP
    block = lambda shape, index: pl.BlockSpec(shape, index)
    row2 = lambda c, seq_ref: (c, 0)
    const2 = lambda c, seq_ref: (0, 0)
    with_grad = upstream is not None
    in_specs = [
        block((GROUP, width), row2),
        block((GROUP, width), row2),
        block((GROUP, NS), lambda c, seq_ref: (c, 1)),
        block((rows, LANES), const2),
        block((1, width), const2),
    ] + [block((width + PACK, NS), const2)] * len(arrived)
    out_specs = [
        block((GROUP, width), row2),
        block((width, NS), const2),
        block((8, GROUP), lambda c, seq_ref: (0, c)),
    ]
    out_shape = [
        jax.ShapeDtypeStruct((rows, width), F32),
        jax.ShapeDtypeStruct((width, NS), F32),
        jax.ShapeDtypeStruct((8, rows), F32),
    ]
    args = [local, pre, kq, within, gain, *arrived]
    flops = 4 * rows * width * NS
    if with_grad:
        features = upstream.shape[1]
        in_specs += [block((width, features), const2), block((GROUP, features), row2)]
        out_specs.append(block((GROUP, width), row2))
        out_shape.append(jax.ShapeDtypeStruct((rows, width), F32))
        args += [proj_out, upstream]
        flops += 2 * rows * width * features
    return call(
        partial(mix_first_kernel, dot, chunks, len(arrived), with_grad),
        after,
        grid=(chunks,),
        in_specs=in_specs,
        out_specs=out_specs,
        out_shape=out_shape,
        prefetch=1,
    )(seq, *args, *after)


def project_out_kernel(total_width, count, *refs):
    mixer_ref, gate_ref, gain_ref, proj_ref = refs[:4]
    part_ref, low_ref = refs[4 + count :]
    scale = lax.rsqrt(stat_columns(refs[4 : 4 + count])[:, 0:1] / total_width + EPS)
    gate = gate_ref[...]
    normed = (mixer_ref[...] * gate * sigmoid(gate) * scale * gain_ref[...]).astype(BF16)
    part = lax.dot_general(normed, proj_ref[...], NN, preferred_element_type=F32)
    part_ref[...] = part
    low_ref[...] = part.astype(BF16)


def project_out(after, chunk, mixer, pre, gain, stats, proj_out, total_width):
    width = mixer.shape[1]
    features = proj_out.shape[1]
    block = lambda shape, index: pl.BlockSpec(shape, index)
    const2 = lambda c: (0, 0)
    return call(
        partial(project_out_kernel, total_width, len(stats)),
        after,
        grid=(1,),
        in_specs=[
            block((GROUP, width), lambda c: (chunk, 0)),
            block((GROUP, width), lambda c: (chunk, 0)),
            block((1, width), const2),
            block((width, features), const2),
        ]
        + [block((8, GROUP), lambda c: (0, chunk))] * len(stats),
        out_specs=[block((GROUP, features), const2)] * 2,
        out_shape=[
            jax.ShapeDtypeStruct((GROUP, features), F32),
            jax.ShapeDtypeStruct((GROUP, features), BF16),
        ],
    )(mixer, pre, gain, proj_out, *stats, *after)


def assemble(place_ref, refs, out_ref):
    size = refs[0].shape[0]
    inner = (place_ref[0] == 1) | (place_ref[0] == 2)
    for chunk in range(len(refs) // 2):
        at = slice(chunk * size, (chunk + 1) * size)

        @pl.when(inner)
        def _(chunk=chunk, at=at):
            out_ref[at, :] = refs[2 * chunk][...]

        @pl.when(jnp.logical_not(inner))
        def _(chunk=chunk, at=at):
            out_ref[at, :] = refs[2 * chunk + 1][...]


def join_kernel(place_ref, done_ref, crossed_ref, out_ref):
    half = done_ref.shape[0]

    @pl.when(place_ref[0] < 2)
    def _():
        out_ref[0:half, :] = done_ref[...]
        out_ref[half:, :] = crossed_ref[...]

    @pl.when(place_ref[0] >= 2)
    def _():
        out_ref[0:half, :] = crossed_ref[...]
        out_ref[half:, :] = done_ref[...]


def join(after, place, done, crossed):
    half, features = done.shape
    spec = pl.BlockSpec((half, features), lambda i, place_ref: (0, 0))
    return call(
        join_kernel,
        after,
        grid=(1,),
        in_specs=[spec, spec],
        out_specs=pl.BlockSpec((2 * half, features), lambda i, place_ref: (0, 0)),
        out_shape=jax.ShapeDtypeStruct((2 * half, features), done.dtype),
        prefetch=1,
    )(place, done, crossed, *after)


def project_kernel(assembled, place_ref, *refs):
    if assembled:
        pieces = refs[:assembled]
        gain_ref, wide_ref, bc_ref, dt_ref, normed_ref, scale_ref, pre_ref, state_ref, edge_ref, rows_ref = refs[assembled:]
    else:
        rows_ref, gain_ref, wide_ref, bc_ref, dt_ref, normed_ref, scale_ref, pre_ref, state_ref, edge_ref = refs
    width = wide_ref.shape[1]
    rows = pre_ref.shape[0]

    @pl.when(pl.program_id(0) == 0)
    def _():
        if assembled:
            assemble(place_ref, pieces, rows_ref)
        wide = rows_ref[...].astype(F32)
        scale = lax.rsqrt(jnp.mean(wide * wide, axis=1, keepdims=True) + EPS)
        normed = (wide * scale * gain_ref[...]).astype(BF16)
        normed_ref[...] = normed
        scale_ref[...] = scale
        state = lax.dot_general(normed, bc_ref[...], NN, preferred_element_type=F32)
        state_ref[:, 0 : 2 * NS] = state
        state_ref[:, 2 * NS :] = lax.dot_general(normed, dt_ref[...], NN, preferred_element_type=F32)
        edge_ref[:, width:] = state[rows - EDGE :]

    pre = lax.dot_general(normed_ref[...], wide_ref[...], NN, preferred_element_type=F32)
    pre_ref[...] = pre
    edge_ref[:, 0:width] = pre[rows - EDGE :]


def project(after, place, rows_in, gain, w_wide, w_bc, w_dt):
    assembled = len(rows_in) if isinstance(rows_in, (list, tuple)) else 0
    pieces = list(rows_in) if assembled else [rows_in]
    features = w_wide.shape[0]
    width = w_wide.shape[1] // 2
    rows = pieces[0].shape[0] * (assembled // 2 if assembled else 1)
    block = lambda shape, index: pl.BlockSpec(shape, index)
    const2 = lambda f, place_ref: (0, 0)
    out_specs = [
        block((rows, features), const2),
        block((rows, 1), const2),
        block((rows, width), lambda f, place_ref: (0, f)),
        block((rows, 2 * NS + LANES), const2),
        block((EDGE, width + 2 * NS), const2),
    ]
    out_shape = [
        jax.ShapeDtypeStruct((rows, features), BF16),
        jax.ShapeDtypeStruct((rows, 1), F32),
        jax.ShapeDtypeStruct((rows, 2 * width), F32),
        jax.ShapeDtypeStruct((rows, 2 * NS + LANES), F32),
        jax.ShapeDtypeStruct((EDGE, width + 2 * NS), F32),
    ]
    if assembled:
        out_specs.append(block((rows, features), const2))
        out_shape.append(jax.ShapeDtypeStruct((rows, features), BF16))
    return call(
        partial(project_kernel, assembled),
        after,
        grid=(2,),
        in_specs=[block(piece.shape, const2) for piece in pieces]
        + [
            block((1, features), const2),
            block((features, width), lambda f, place_ref: (0, f)),
            block((features, 2 * NS), const2),
            block((features, LANES), const2),
        ],
        out_specs=out_specs,
        out_shape=out_shape,
        prefetch=1,
    )(place, *pieces, gain, w_wide, w_bc, w_dt, *after)


def input_grad(total_ref, rows_ref, scale_ref, gain_ref, up_ref):
    scale = scale_ref[...]
    unit = rows_ref[...].astype(F32) * scale
    grad_unit = total_ref[...].astype(F32) * gain_ref[...]
    mean = jnp.mean(grad_unit * unit, axis=1, keepdims=True)
    return (up_ref[...].astype(F32) + scale * (grad_unit - unit * mean)).astype(BF16)


def back_first_kernel(
    total_ref, rows_ref, scale_ref, pre_gain_ref, old_ref,
    proj_ref, mixer_ref, gate_ref, gain_ref, up_ref, back_ref, stats_ref,
):
    upstream = input_grad(total_ref, rows_ref, scale_ref, pre_gain_ref, old_ref)
    up_ref[...] = upstream
    back = lax.dot_general(upstream, proj_ref[...], NT, preferred_element_type=F32)
    back_ref[...] = back
    gate = gate_ref[...]
    product = back * mixer_ref[...] * gate * sigmoid(gate) * gain_ref[...]
    stats_ref[...] = high_dot(jnp.ones((8, back.shape[1]), F32), product, NT)


def back_first(after, total, rows_in, scale, pre_gain, old, proj_out, mixer, pre, gain):
    rows, width = mixer.shape
    features = proj_out.shape[1]
    block = lambda shape, index: pl.BlockSpec(shape, index)
    row2 = lambda c: (c, 0)
    const2 = lambda c: (0, 0)
    wide = block((GROUP, features), row2)
    return call(
        back_first_kernel,
        after,
        grid=(rows // GROUP,),
        in_specs=[
            wide,
            wide,
            block((GROUP, 1), row2),
            block((1, features), const2),
            wide,
            block((width, features), const2),
            block((GROUP, width), row2),
            block((GROUP, width), row2),
            block((1, width), const2),
        ],
        out_specs=[wide, block((GROUP, width), row2), block((8, GROUP), lambda c: (0, c))],
        out_shape=[
            jax.ShapeDtypeStruct((rows, features), BF16),
            jax.ShapeDtypeStruct((rows, width), F32),
            jax.ShapeDtypeStruct((8, rows), F32),
        ],
    )(total, rows_in, scale, pre_gain, old, proj_out, mixer, pre, gain, *after)


def end_back_kernel(total_ref, rows_ref, scale_ref, gain_ref, up_ref, out_ref):
    out_ref[...] = input_grad(total_ref, rows_ref, scale_ref, gain_ref, up_ref)


def end_back(after, total, rows_in, scale, gain, upstream):
    rows, features = total.shape
    wide = pl.BlockSpec((GROUP, features), lambda c: (c, 0))
    return call(
        end_back_kernel,
        after,
        grid=(rows // GROUP,),
        in_specs=[
            wide,
            wide,
            pl.BlockSpec((GROUP, 1), lambda c: (c, 0)),
            pl.BlockSpec((1, features), lambda c: (0, 0)),
            wide,
        ],
        out_specs=wide,
        out_shape=jax.ShapeDtypeStruct((rows, features), BF16),
    )(total, rows_in, scale, gain, upstream, *after)


def end_out_kernel(per, *refs):
    for m in range(per):
        refs[2 * per + m][...] = (
            refs[per + m][...].astype(F32) + refs[m][...].astype(F32)
        ).astype(BF16)


def end_out(after, totals, rows_in):
    per = len(totals)
    rows, features = totals[0].shape
    wide = pl.BlockSpec((GROUP, features), lambda c: (c, 0))
    return call(
        partial(end_out_kernel, per),
        after,
        grid=(rows // GROUP,),
        in_specs=[wide] * (2 * per),
        out_specs=[wide] * per,
        out_shape=[jax.ShapeDtypeStruct((rows, features), BF16)] * per,
    )(*totals, *rows_in, *after)


def mix_back_kernel(chunks, total_width, squares, products, *refs):
    back_ref, mixer_ref, gate_ref, reads_ref, within_ref, gain_ref = refs[:6]
    square_refs, product_refs = refs[6 : 6 + squares], refs[6 + squares : 6 + squares + products]
    refs = refs[6 + squares + products :]
    grad_ref, gate_grad_ref, gain_grad_ref, packed_ref, normed_ref, total_ref = refs
    width = mixer_ref.shape[1]
    chunk = pl.program_id(0)
    square = stat_columns(square_refs)
    scale = lax.rsqrt(square[:, 0:1] / total_width + EPS)
    product = (stat_columns(product_refs) if products else square)[:, 1:2] / total_width
    gate = gate_ref[...]
    sig = sigmoid(gate)
    act = gate * sig
    mixer = mixer_ref[...]
    back = back_ref[...]
    gated = mixer * act
    unit = gated * scale
    normed = (unit * gain_ref[...]).astype(BF16)
    normed_ref[...] = normed
    gated_grad = scale * back * gain_ref[...] - gated * (scale * scale * scale * product)
    grad = gated_grad * act
    grad_ref[...] = grad
    gate_grad_ref[...] = (gated_grad * mixer * sig * (1.0 + gate * (1.0 - sig))).astype(BF16)
    entry = widen(entry_decay(within_ref, chunk, chunks), width)
    gain_part = jnp.sum(back * unit, axis=0, keepdims=True)
    state_part = low_dot(grad * entry, reads_ref[...], TN)

    @pl.when(chunk == 0)
    def _():
        gain_grad_ref[...] = gain_part
        total_ref[...] = state_part

    @pl.when(chunk > 0)
    def _():
        gain_grad_ref[...] += gain_part
        total_ref[...] += state_part

    @pl.when(chunk == chunks - 1)
    def _():
        packed_ref[0:width, :] = total_ref[...].astype(BF16)
        pack_decay(packed_ref, within_ref, chunks)


def mix_back(after, back, mixer, pre, kq, within, gain, square, product, total_width):
    rows, width = mixer.shape
    chunks = rows // GROUP
    block = lambda shape, index: pl.BlockSpec(shape, index)
    row2 = lambda c: (c, 0)
    const2 = lambda c: (0, 0)
    in_specs = [
        block((GROUP, width), row2),
        block((GROUP, width), row2),
        block((GROUP, width), row2),
        block((GROUP, NS), lambda c: (c, 1)),
        block((rows, LANES), const2),
        block((1, width), const2),
    ] + [block((8, GROUP), lambda c: (0, c))] * (len(square) + len(product))
    out_specs = [
        block((GROUP, width), row2),
        block((GROUP, width), row2),
        block((1, width), const2),
        block((width + PACK, NS), const2),
        block((GROUP, width), row2),
    ]
    out_shape = [
        jax.ShapeDtypeStruct((rows, width), F32),
        jax.ShapeDtypeStruct((rows, width), BF16),
        jax.ShapeDtypeStruct((1, width), F32),
        jax.ShapeDtypeStruct((width + PACK, NS), BF16),
        jax.ShapeDtypeStruct((rows, width), BF16),
    ]
    args = [back, mixer, pre, kq, within, gain, *square, *product]
    flops = 2 * rows * width * NS
    return call(
        partial(mix_back_kernel, chunks, total_width, len(square), len(product)),
        after,
        grid=(chunks,),
        in_specs=in_specs,
        out_specs=out_specs,
        out_shape=out_shape,
        scratch_shapes=[pltpu.VMEM((width, NS), F32)],
    )(*args, *after)


def late_out_kernel(per, *refs):
    proj_ref = refs[per]
    for m in range(per):
        refs[per + 1 + m][...] = lax.dot_general(
            refs[m][...], proj_ref[...], NN, preferred_element_type=F32
        ).astype(BF16)


def late_out(after, normed_outs, proj_out):
    per = len(normed_outs)
    rows, width = normed_outs[0].shape
    features = proj_out.shape[1]
    return call(
        partial(late_out_kernel, per),
        after,
        grid=(rows // GROUP,),
        in_specs=[pl.BlockSpec((GROUP, width), lambda c: (c, 0))] * per
        + [pl.BlockSpec((width, features), lambda c: (0, 0))],
        out_specs=[pl.BlockSpec((GROUP, features), lambda c: (c, 0))] * per,
        out_shape=[jax.ShapeDtypeStruct((rows, features), BF16)] * per,
    )(*normed_outs, proj_out, *after)


def project_back_kernel(
    gate_ref, inner_ref, state_ref, raw_ref, edge_ref, wide_ref, bc_ref, dt_ref, rows_ref, scale_ref,
    grads_ref, narrow_grads_ref, gain_grad_ref, part_ref,
):
    width = gate_ref.shape[1]
    rows = gate_ref.shape[0]

    @pl.when(pl.program_id(0) == 0)
    def _():
        grads_ref[:, 0:width] = gate_ref[...]
        added = jnp.concatenate(
            [jnp.zeros((EDGE, width), F32), edge_ref[:, 0:width]], axis=0
        )
        grads_ref[0 : rows - PACK, width:] = inner_ref[0 : rows - PACK, :].astype(BF16)
        grads_ref[rows - PACK :, width:] = (inner_ref[rows - PACK :, :] + added).astype(BF16)
        added = jnp.concatenate(
            [jnp.zeros((EDGE, 2 * NS), F32), edge_ref[:, width:]], axis=0
        )
        narrow_grads_ref[0 : rows - PACK, 0 : 2 * NS] = state_ref[0 : rows - PACK, :].astype(BF16)
        narrow_grads_ref[rows - PACK :, 0 : 2 * NS] = (state_ref[rows - PACK :, :] + added).astype(BF16)
        narrow_grads_ref[:, 2 * NS :] = raw_ref[...].astype(BF16)

    part = lax.dot_general(grads_ref[...], wide_ref[...], NT, preferred_element_type=F32)
    part = part + lax.dot_general(
        narrow_grads_ref[:, 0 : 2 * NS], bc_ref[...], NT, preferred_element_type=F32
    )
    part = part + lax.dot_general(
        narrow_grads_ref[:, 2 * NS :], dt_ref[...], NT, preferred_element_type=F32
    )
    unit = rows_ref[...].astype(F32) * scale_ref[...]
    gain_grad_ref[...] = jnp.sum(part * unit, axis=0, keepdims=True)
    part_ref[...] = part.astype(BF16)


def project_back(after, gate_grad, inner, state, raw, edges, w_wide, w_bc, w_dt, rows_in, scale):
    rows, width = gate_grad.shape
    features = w_wide.shape[0]
    size = 512 if features % 512 == 0 else features
    block = lambda shape, index: pl.BlockSpec(shape, index)
    const2 = lambda f: (0, 0)
    narrow = 2 * NS + LANES
    return call(
        project_back_kernel,
        after,
        grid=(features // size,),
        in_specs=[
            block((rows, width), const2),
            block((rows, width), const2),
            block((rows, 2 * NS), const2),
            block((rows, LANES), const2),
            block((EDGE, width + 2 * NS), const2),
            block((size, 2 * width), lambda f: (f, 0)),
            block((size, 2 * NS), lambda f: (f, 0)),
            block((size, LANES), lambda f: (f, 0)),
            block((rows, size), lambda f: (0, f)),
            block((rows, 1), const2),
        ],
        out_specs=[
            block((rows, 2 * width), const2),
            block((rows, narrow), const2),
            block((1, size), lambda f: (0, f)),
            block((rows, size), lambda f: (0, f)),
        ],
        out_shape=[
            jax.ShapeDtypeStruct((rows, 2 * width), BF16),
            jax.ShapeDtypeStruct((rows, narrow), BF16),
            jax.ShapeDtypeStruct((1, features), F32),
            jax.ShapeDtypeStruct((rows, features), BF16),
        ],
    )(gate_grad, inner, state, raw, edges, w_wide, w_bc, w_dt, rows_in, scale, *after)


def add_half_kernel(index_ref, own_ref, first_ref, out_ref):
    out_ref[...] = (own_ref[...].astype(F32) + first_ref[...].astype(F32)).astype(out_ref.dtype)


def add_half(after, index, own, first, kind):
    half = own.shape[0] // 2
    features = own.shape[1]
    pick = pl.BlockSpec((half, features), lambda i, index_ref: (index_ref[0], 0))
    return call(
        add_half_kernel,
        after,
        grid=(1,),
        in_specs=[pick, pick],
        out_specs=pl.BlockSpec((half, features), lambda i, index_ref: (0, 0)),
        out_shape=jax.ShapeDtypeStruct((half, features), kind),
        prefetch=1,
    )(index, own, first, *after)


def finish_out_kernel(index_ref, own_ref, first_ref, second_ref, rows_ref, out_ref):
    total = own_ref[...].astype(F32) + first_ref[...].astype(F32) + second_ref[...].astype(F32)
    out_ref[...] = (rows_ref[...].astype(F32) + total).astype(BF16)


def finish_half(after, index, chunk, own, first, second, rows_in):
    half, features = second.shape
    pick = pl.BlockSpec((half, features), lambda i, index_ref: (index_ref[0], 0))
    whole = pl.BlockSpec((half, features), lambda i, index_ref: (2 * chunk + index_ref[0], 0))
    same = pl.BlockSpec((half, features), lambda i, index_ref: (0, 0))
    one = pl.BlockSpec((1, features), lambda i, index_ref: (0, 0))
    in_specs = [pick, pick, same, whole]
    args = [own, first, second, rows_in]
    return call(
        finish_out_kernel,
        after,
        grid=(1,),
        in_specs=in_specs,
        out_specs=same,
        out_shape=jax.ShapeDtypeStruct((half, features), BF16),
        prefetch=1,
    )(index, *args, *after)


def weight_grads_kernel(per, share, section_ref, *refs):
    kept_ref, given_ref, total_ref = refs[5 * per :]
    at = 0
    for left, right in ((0, 2), (0, 3), (1, 4)):
        width = refs[right].shape[1]
        part = None
        for m in range(per):
            product = lax.dot_general(
                refs[5 * m + left][...], refs[5 * m + right][...], TN, preferred_element_type=F32
            )
            part = product if part is None else part + product
        total_ref[:, at : at + width] = part
        at += width
    half = share // 2
    for i in range(total_ref.shape[0] // share):
        to = slice(i * half, (i + 1) * half)
        mine = pl.multiple_of(i * share + section_ref[0] * half, half)
        theirs = pl.multiple_of(i * share + (1 - section_ref[0]) * half, half)
        kept_ref[to, :] = total_ref[pl.ds(mine, half), :].astype(BF16)
        given_ref[to, :] = total_ref[pl.ds(theirs, half), :].astype(BF16)


def weight_grads(after, section, terms, share):
    rows, features = terms[0][0].shape
    size = 384
    block = lambda shape, index: pl.BlockSpec(shape, index)
    in_specs = []
    args = []
    for normed, up, grads, narrow, normed_out in terms:
        in_specs += [block((rows, size), lambda f, section_ref: (0, f))] * 2
        in_specs += [block(a.shape, lambda f, section_ref: (0, 0)) for a in (grads, narrow, normed_out)]
        args += [normed, up, grads, narrow, normed_out]
    total = sum(a.shape[1] for a in terms[0][2:])
    return call(
        partial(weight_grads_kernel, len(terms), share),
        after,
        grid=(features // size,),
        in_specs=in_specs,
        out_specs=[block((size // 2, total), lambda f, section_ref: (f, 0))] * 2,
        out_shape=[jax.ShapeDtypeStruct((features // 2, total), BF16)] * 2,
        scratch_shapes=[pltpu.VMEM((size, total), F32)],
        prefetch=1,
    )(section, *args, *after)


def place_kernel(per, section_ref, *refs):
    out_ref, buffer, come, go = refs[-4:]
    for section in range(2):

        @pl.when(section_ref[0] == section)
        def _(section=section):
            ins, outs = [], []
            for m in range(2 * per):
                own = m // per == section
                source = refs[(2 * section + (0 if own else 1)) * per + m % per]
                ins.append(pltpu.make_async_copy(source, buffer.at[m], come.at[m]))
                outs.append(pltpu.make_async_copy(buffer.at[m], out_ref.at[m], go.at[m]))
            for copy in ins:
                copy.start()
            for first, second in zip(ins, outs):
                first.wait()
                second.start()
            for copy in outs:
                copy.wait()


def place_layers(after, section, first, first_got, second, second_got):
    count = 2 * len(first)
    rows, features = first[0].shape
    spot = pl.BlockSpec(memory_space=pl.ANY)
    return call(
        partial(place_kernel, len(first)),
        after,
        grid=(1,),
        in_specs=[spot] * (2 * count),
        out_specs=spot,
        out_shape=jax.ShapeDtypeStruct((count, rows, features), BF16),
        scratch_shapes=[
            pltpu.VMEM((count, rows, features), BF16),
            pltpu.SemaphoreType.DMA((count,)),
            pltpu.SemaphoreType.DMA((count,)),
        ],
        prefetch=1,
    )(section, *first, *first_got, *second, *second_got, *after)


def hold_kernel(*refs):
    pass


def hold(after, arrays):
    count = len(arrays)
    spot = pl.BlockSpec(memory_space=pl.ANY)
    return pl.pallas_call(
        hold_kernel,
        in_specs=[spot] * (count + len(after)),
        out_specs=[spot] * count,
        out_shape=[jax.ShapeDtypeStruct(a.shape, a.dtype) for a in arrays],
        input_output_aliases={k: k for k in range(count)},
    )(*arrays, *after)


SMALL_NAMES = (
    "pre_gain", "kernel_inner", "bias_inner", "kernel_state", "bias_state",
    "step_bias", "decay_log", "skip_wide", "norm_gain",
)


def small_layout(features, width, taps):
    shapes = {
        "pre_gain": (1, features),
        "kernel_inner": (taps, width),
        "bias_inner": (1, width),
        "kernel_state": (taps, 2 * NS),
        "bias_state": (1, 2 * NS),
        "step_bias": (1, LANES),
        "decay_log": (1, LANES),
        "skip_wide": (1, width),
        "norm_gain": (1, width),
    }
    places, row = {}, 0
    for name in SMALL_NAMES:
        places[name] = (row, *shapes[name])
        row += shapes[name][0]
    return places, -(-row // 8) * 8


def pack_kernel(places, pre_ref, ker_in_ref, bias_in_ref, ker_st_ref, bias_st_ref, step_ref, decay_ref, skip_ref, norm_ref, out_ref):
    out_ref[...] = jnp.zeros_like(out_ref)
    heads = step_ref.shape[1]
    width = norm_ref.shape[1]
    spread = jnp.where(iota((heads, width), 1) // P_SIZE == iota((heads, width), 0), 1.0, 0.0)
    values = {
        "pre_gain": pre_ref[...],
        "kernel_inner": ker_in_ref[0],
        "bias_inner": bias_in_ref[...],
        "kernel_state": ker_st_ref[0],
        "bias_state": bias_st_ref[...],
        "step_bias": step_ref[...],
        "decay_log": decay_ref[...],
        "skip_wide": high_dot(skip_ref[...], spread, NN),
        "norm_gain": norm_ref[...],
    }
    for name, value in values.items():
        row = places[name][0]
        out_ref[row : row + value.shape[0], 0 : value.shape[1]] = value


def pack(pre_gain, kernel_inner, *rest):
    features = pre_gain.shape[1]
    places, height = small_layout(features, kernel_inner.shape[2], kernel_inner.shape[1])
    args = (pre_gain, kernel_inner, *rest)
    return call(
        partial(pack_kernel, places),
        (),
        grid=(1,),
        in_specs=[pl.BlockSpec(a.shape, lambda i, n=a.ndim: (0,) * n) for a in args],
        out_specs=pl.BlockSpec((height, features), lambda i: (0, 0)),
        out_shape=jax.ShapeDtypeStruct((height, features), F32),
    )(*args)


def choose_kernel(index, places, section_ref, *refs):
    count = 5
    own, other, outs = refs[:count], refs[count : 2 * count], refs[2 * count :]
    for mine in (True, False):

        @pl.when((section_ref[0] == index) == mine)
        def _(source=own if mine else other):
            for k in range(count - 1):
                outs[k][...] = source[k][...]

            @pl.when(pl.program_id(0) == 0)
            def _():
                for name, out in zip(SMALL_NAMES, outs[count - 1 :]):
                    row, high, wide = places[name]
                    out[...] = source[count - 1][row : row + high, 0:wide]


def choose(after, section, index, own, other, width, taps):
    steps = 4
    features = own[0].shape[0]
    places, _ = small_layout(features, width, taps)

    def specs(mine):
        result = []
        for array in own[:-1]:
            shape = (array.shape[0] // steps, array.shape[1])

            def at(i, section_ref):
                used = (section_ref[0] == index) == mine
                return jnp.where(used, i, 0), 0

            result.append(pl.BlockSpec(shape, at))
        result.append(pl.BlockSpec(own[-1].shape, lambda i, section_ref: (0, 0)))
        return result

    out_specs = [
        pl.BlockSpec((a.shape[0] // steps, a.shape[1]), lambda i, section_ref: (i, 0)) for a in own[:-1]
    ]
    out_shape = [jax.ShapeDtypeStruct(a.shape, a.dtype) for a in own[:-1]]
    for name in SMALL_NAMES:
        shape = places[name][1:]
        out_specs.append(pl.BlockSpec(shape, lambda i, section_ref: (0, 0)))
        out_shape.append(jax.ShapeDtypeStruct(shape, F32))
    return call(
        partial(choose_kernel, index, places),
        after,
        grid=(steps,),
        in_specs=[*specs(True), *specs(False)],
        out_specs=out_specs,
        out_shape=out_shape,
        prefetch=1,
    )(section, *own, *other, *after)


def pick_kernel(section_ref, array_ref, *out_refs):
    for m, out_ref in enumerate(out_refs):

        @pl.when(pl.program_id(0) == m)
        def _(out_ref=out_ref):
            out_ref[...] = array_ref[0]


def pick(after, section, array, per):
    _, rows, features = array.shape
    return call(
        pick_kernel,
        after,
        grid=(per,),
        in_specs=[pl.BlockSpec((1, rows, features), lambda i, section_ref: (section_ref[0] * per + i, 0, 0))],
        out_specs=[pl.BlockSpec((rows, features), lambda i, section_ref: (0, 0))] * per,
        out_shape=[jax.ShapeDtypeStruct((rows, features), array.dtype)] * per,
        prefetch=1,
    )(section, array, *after)


def add_kernel(a_ref, b_ref, out_ref):
    out_ref[...] = (a_ref[...].astype(F32) + b_ref[...].astype(F32)).astype(out_ref.dtype)


def add(after, a, b):
    rows, width = a.shape
    steps = 4 if rows % 64 == 0 else 1
    spec = pl.BlockSpec((rows // steps, width), lambda i: (i, 0))
    return call(
        add_kernel,
        after,
        grid=(steps,),
        in_specs=[spec, spec],
        out_specs=spec,
        out_shape=jax.ShapeDtypeStruct(a.shape, a.dtype),
    )(a, b, *after)


def neighbor(array, axis, by):
    length = lax.axis_size(axis)
    pairs = [(i, i + by) for i in range(length) if 0 <= i + by < length]
    return lax.ppermute(array, axis, pairs)


def swap(array):
    return lax.ppermute(array, SECTION, [(0, 1), (1, 0)])


def whole_sum(array, axis):
    length = lax.axis_size(axis)
    by = 1
    while by < length:
        array = array + lax.ppermute(array, axis, [(i, i ^ by) for i in range(length)])
        by *= 2
    return array


class Order:
    def __init__(self):
        self.after = ()

    def wait(self, *arrays):
        self.after = (*self.after, *arrays)

    def __call__(self, result):
        self.after = (result[0] if isinstance(result, (list, tuple)) else result,)
        return result


def shards(
    layer_input, cotangent, pre_gain, proj_zx, proj_bc, proj_dt, kernel_inner, bias_inner,
    kernel_state, bias_state, step_bias, decay_log, skip_gain, norm_gain, proj_out,
):
    section = lax.axis_index(SECTION)
    sections = lax.axis_size(SECTION)
    micro, rows, features = layer_input.shape
    per = micro // sections
    width = norm_gain.shape[1]
    heads = step_bias.shape[1]
    total_width = width * lax.axis_size(HEAD)
    taps = kernel_inner.shape[1]
    chunks = rows // GROUP
    assert lax.axis_size(HEAD) == 4
    place = lax.axis_index(HEAD)
    inner_place = (place == 1) | (place == 2)
    lower = place < 2
    keep = jnp.where(lower, 0, 1).astype(jnp.int32)[None]
    give = 1 - keep
    across = [(1, 2), (2, 1)]
    outward = [(1, 0), (2, 3)]
    order = Order()

    at_place = place.astype(jnp.int32)[None]
    at_seq = lax.axis_index(SEQ).astype(jnp.int32)[None]
    seqs = lax.axis_size(SEQ)
    at_section = section.astype(jnp.int32)[None]

    packed = pack(
        pre_gain, kernel_inner, bias_inner, kernel_state, bias_state, step_bias, decay_log, skip_gain, norm_gain
    )
    own = (
        proj_zx[0].reshape(features, 2 * width),
        proj_bc[0],
        jnp.pad(proj_dt[0], ((0, 0), (0, LANES - heads))),
        proj_out[0],
        packed,
    )
    other = tuple(swap(array) for array in own)

    def layer_weights(index):
        w_wide, w_bc, w_dt, w_out, *rest = order(
            choose(order.after, at_section, index, own, other, width, taps)
        )
        return w_wide, w_bc, w_dt, w_out, dict(zip(SMALL_NAMES, rest))

    span = range(per)
    mine_in = order(pick(order.after, at_section, layer_input, per))

    class Micro:
        pass

    def enter(rows_in, layer):
        t = Micro()
        w_wide, w_bc, w_dt, t.w_out, t.small = layer
        t.layer, t.rows_in = layer, rows_in
        t.gain = t.small["norm_gain"]
        t.normed, t.scale, t.pre, t.pre_st, edge, *rest = order(
            project(order.after, at_place, rows_in, t.small["pre_gain"], w_wide, w_bc, w_dt)
        )
        if rest:
            t.rows_in = rest[0]
        t.edge = neighbor(edge, SEQ, 1)
        return t

    def scan(t, dot):
        t.local, t.kq, t.steps, t.within, t.starts, packed = order(
            scan_forward(order.after, dot, t.pre, t.pre_st, t.edge, t.small)
        )
        t.packed, t.forward = packed, True
        t.arrived = [flip(packed, SEQ, 0)]

    def flip(array, axis, level):
        length = lax.axis_size(axis)
        return lax.ppermute(array, axis, [(i, i ^ (1 << level)) for i in range(length)])

    def pass_on(t):
        level = len(t.arrived)
        if (1 << level) < seqs:
            t.packed = order(
                merge(order.after, at_seq, t.forward, level - 1, t.packed, t.arrived[-1])
            )
            t.arrived.append(flip(t.packed, SEQ, level))
            if (2 << level) < seqs:
                pass_on(t)

    def stats_on(t, name):
        array, got = getattr(t, name)
        total = order(stat_add(order.after, array, got))
        setattr(t, name, [total, flip(total, HEAD, 1)])

    def mix(t, dot, upstream=None):
        args = () if upstream is None else (upstream, t.w_out)
        t.mixer, t.before, stats, *back = order(
            mix_first(order.after, at_seq, dot, t.local, t.pre, t.kq, t.within, t.gain, t.arrived, *args)
        )
        t.back = back[0] if back else None
        t.stats = [stats, flip(stats, HEAD, 0)]

    def out(t, c):
        if c == 0:
            t.owns, t.firsts = [], []
        own, low = order(
            project_out(order.after, c, t.mixer, t.pre, t.gain, t.stats, t.w_out, total_width)
        )
        t.owns.append(own)
        t.firsts.append(lax.ppermute(low, HEAD, [(0, 1), (3, 2)]))

    def pass_half(t, c, kind=BF16):
        if c == 0:
            t.seconds = []
        given = order(add_half(order.after, give, t.owns[c], t.firsts[c], kind))
        t.seconds.append(lax.ppermute(given, HEAD, across))

    def finish(t, c):
        if c == 0:
            t.pieces, t.halves = [], []
        done = order(
            finish_half(order.after, keep, c, t.owns[c], t.firsts[c], t.seconds[c], t.rows_in)
        )
        t.halves.append((done, lax.ppermute(done, HEAD, across)))

    def spread(t, c):
        joined = order(join(order.after, at_place, *t.halves[c]))
        t.pieces += [joined, lax.ppermute(joined, HEAD, outward)]

    def mix_up(t, products):
        t.grad, t.gate_grad, t.gain_grad, packed, t.normed_out = order(
            mix_back(
                order.after, t.back, t.mixer, t.pre, t.kq, t.within, t.gain, t.stats, products, total_width
            )
        )
        t.packed, t.forward = packed, False
        t.arrived = t.later = [flip(packed, SEQ, 0)]

    def back_start(t, above, total, old):
        t.upstream, t.back, product = order(
            back_first(
                order.after, total, above.rows_in, above.scale, above.small["pre_gain"], old,
                t.w_out, t.mixer, t.pre, t.gain,
            )
        )
        t.products = [product, flip(product, HEAD, 0)]

    def scan_back(t):
        t.inner, edge, t.small_in, t.state, t.small_st, t.raw, t.small_dt = order(
            scan_backward(
                order.after, at_seq, t.pre, t.pre_st, t.edge, t.small, t.kq, t.steps, t.within, t.starts, t.before, t.later, t.grad
            )
        )
        t.edges = neighbor(edge, SEQ, -1)

    def back_out(t, upstream):
        grads, narrow, t.pre_gain_grad, part = order(
            project_back(
                order.after, t.gate_grad, t.inner, t.state, t.raw, t.edges, *t.layer[:3], t.rows_in, t.scale
            )
        )
        t.weights = (t.normed, upstream, grads, narrow, t.normed_out)
        return part

    def scatter_rows(array, axis, ordered=False):
        count = array.shape[0]
        length = lax.axis_size(axis)
        level = length // 2
        while level >= 1:
            high = (lax.axis_index(axis) & level) > 0
            count //= 2
            mine = jnp.where(high, count, 0)
            given = lax.dynamic_slice_in_dim(array, count - mine, count, 0)
            got = lax.ppermute(given, axis, [(i, i ^ level) for i in range(length)])
            own = lax.dynamic_slice_in_dim(array, mine, count, 0)
            array = order(add(order.after, own, got)) if ordered else own + got
            level //= 2
        return array

    dot0, dot1 = split_dot, low_dot
    a, b = span
    share = features // seqs

    layer0 = layer_weights(0)
    f0 = [enter(mine_in[m], layer0) for m in span]
    scan(f0[a], dot0)
    scan(f0[b], dot0)
    pass_on(f0[a])
    mine_back = order(pick(order.after, at_section, cotangent, per))
    pass_on(f0[b])
    mix(f0[a], dot0)
    mix(f0[b], dot0)
    stats_on(f0[a], "stats")
    stats_on(f0[b], "stats")
    order.wait(*f0[a].stats, *f0[b].stats)
    for t in f0:
        for c in range(chunks):
            out(t, c)
    layer1 = layer_weights(1)
    jobs = [(t, c) for t in f0 for c in range(chunks)]
    for k in range(len(jobs) + 2):
        if k < len(jobs):
            pass_half(*jobs[k], WIRE)
        if 0 < k <= len(jobs):
            finish(*jobs[k - 1])
        if k > 1:
            spread(*jobs[k - 2])

    f1 = [enter(f0[a].pieces, layer1)]
    scan(f1[a], dot1)
    f1.append(enter(f0[b].pieces, layer1))
    pass_on(f1[a])
    scan(f1[b], dot1)
    mix(f1[a], dot1, mine_back[a])
    pass_on(f1[b])
    stats_on(f1[a], "stats")
    mix(f1[b], dot1, mine_back[b])
    mix_up(f1[a], ())
    stats_on(f1[b], "stats")
    pass_on(f1[a])
    mix_up(f1[b], ())
    scan_back(f1[a])
    pass_on(f1[b])
    scan_back(f1[b])
    parts = [back_out(f1[m], mine_back[m]) for m in span]
    totals = lax.psum(tuple(parts), HEAD)
    kept1, given1 = order(
        weight_grads(order.after, at_section, [t.weights for t in f1], share)
    )
    parts = order(late_out(order.after, [t.normed_out for t in f1], f1[a].w_out))
    summed1 = order(add(order.after, kept1, swap(given1)))
    reduced1 = lax.psum_scatter(summed1, SEQ, scatter_dimension=0, tiled=True)
    parts = order(hold((*order.after, *totals), parts))
    for m in span:
        back_start(f0[m], f1[m], totals[m], mine_back[m])
    totals1 = lax.psum(tuple(parts), HEAD)
    stats_on(f0[a], "products")
    stats_on(f0[b], "products")
    mix_up(f0[a], f0[a].products)
    mix_up(f0[b], f0[b].products)
    pass_on(f0[a])
    pass_on(f0[b])
    scan_back(f0[a])
    scan_back(f0[b])
    parts = [back_out(f0[m], f0[m].upstream) for m in span]
    kept0, given0 = order(
        weight_grads(order.after, at_section, [t.weights for t in f0], share)
    )
    parts = order(hold((*order.after, *totals1), parts))
    totals = lax.psum(tuple(parts), HEAD)
    given0 = swap(given0)
    outs1 = order(end_out(order.after, totals1, [t.rows_in for t in f1]))
    reduced0 = scatter_rows(order(add(order.after, kept0, given0)), SEQ, True)
    outs0 = [t.rows_in for t in f1]
    sents1 = [t.upstream for t in f0]

    def exchange(first, second):
        got_first = [lax.ppermute(x, SECTION, [(1, 0)]) for x in first]
        got_second = [lax.ppermute(x, SECTION, [(0, 1)]) for x in second]
        return got_first, got_second

    order.wait(reduced1)
    sents0 = [
        order(
            end_back(
                order.after, totals[m], f0[m].rows_in, f0[m].scale, f0[m].small["pre_gain"], f0[m].upstream
            )
        )
        for m in span
    ]
    got2, got3 = exchange(outs0, outs1)
    got0, got1 = exchange(sents0, sents1)
    layer_out = order(
        place_layers(order.after, at_section, outs0, got2, outs1, got3)
    )
    reduced = [reduced0, reduced1]
    kept = jnp.where(section == 0, reduced[0], reduced[1])
    moved = swap(jnp.where(section == 0, reduced[1], reduced[0]))
    weights = jnp.where(
        section == 0,
        jnp.concatenate([kept, moved], axis=0),
        jnp.concatenate([moved, kept], axis=0),
    ).astype(F32)
    grad_zx = weights[:, : 2 * width].reshape(share, 2, width)
    grad_bc = scatter_rows(weights[:, 2 * width : 2 * width + 2 * NS], HEAD)
    grad_dt = weights[:, 2 * width + 2 * NS : 2 * width + 2 * NS + heads]
    grad_out = weights[:, 2 * width + 2 * NS + LANES :].T

    def collect_smalls(tasks):
        names = ("small_in", "gain_grad", "small_dt", "small_st", "pre_gain_grad")
        return jnp.concatenate(
            [sum(getattr(t, name) for t in tasks).reshape(-1, LANES) for name in names], axis=0
        )

    joined = [collect_smalls(f0), collect_smalls(f1)]
    smalls = jnp.where(section == 0, joined[0], joined[1]) + swap(
        jnp.where(section == 0, joined[1], joined[0])
    )
    smalls = whole_sum(smalls, SEQ)
    inner_rows = 8 * width // LANES
    gain_rows = width // LANES
    at = 0
    small_in = smalls[at : at + inner_rows].reshape(8, width)
    at += inner_rows
    gain_grad = smalls[at : at + gain_rows].reshape(width)
    at += gain_rows
    small_dt = smalls[at : at + 8]
    at += 8
    shared = whole_sum(smalls[at:], HEAD)
    small_st = shared[: 8 * 2 * NS // LANES].reshape(8, 2 * NS)
    grad_pre = shared[8 * 2 * NS // LANES :].reshape(features)
    grad_pre = lax.dynamic_slice_in_dim(grad_pre, lax.axis_index(SEQ) * share, share, 0)
    parts = seqs * lax.axis_size(HEAD)
    st_width = 2 * NS // parts
    st_at = (lax.axis_index(SEQ) * lax.axis_size(HEAD) + lax.axis_index(HEAD)) * st_width
    small_st = lax.dynamic_slice_in_dim(small_st, st_at, st_width, 1)
    grads = [
        grad_pre[None],
        grad_zx[None],
        grad_bc[None],
        grad_dt[None],
        small_in[None, :taps],
        small_in[None, taps],
        small_st[None, :taps],
        small_st[None, taps],
        small_dt[None, 0, :heads],
        small_dt[None, 1, :heads],
        small_in[None, taps + 1].reshape(1, heads, P_SIZE).sum(axis=2),
        gain_grad[None],
        grad_out[None],
    ]
    order.wait(grad_bc)
    layer_grad = order(
        place_layers(order.after, at_section, sents0, got0, sents1, got1)
    )

    return (layer_out[None], layer_grad[None], *grads)


def solution(mesh):
    return jax.shard_map(
        shards,
        mesh=mesh,
        in_specs=(
            P(None, SEQ, None),
            P(None, SEQ, None),
            P(SECTION, None),
            P(SECTION, None, None, HEAD),
            P(SECTION, None, None),
            P(SECTION, None, HEAD),
            P(SECTION, None, HEAD),
            P(SECTION, HEAD),
            P(SECTION, None, None),
            P(SECTION, None),
            P(SECTION, HEAD),
            P(SECTION, HEAD),
            P(SECTION, HEAD),
            P(SECTION, HEAD),
            P(SECTION, HEAD, None),
        ),
        out_specs=(
            P(SECTION, None, SEQ, None),
            P(SECTION, None, SEQ, None),
            P(SECTION, SEQ),
            P(SECTION, SEQ, None, HEAD),
            P(SECTION, (SEQ, HEAD), None),
            P(SECTION, SEQ, HEAD),
            P(SECTION, None, HEAD),
            P(SECTION, HEAD),
            P(SECTION, None, (SEQ, HEAD)),
            P(SECTION, (SEQ, HEAD)),
            P(SECTION, HEAD),
            P(SECTION, HEAD),
            P(SECTION, HEAD),
            P(SECTION, HEAD),
            P(SECTION, HEAD, SEQ),
        ),
        check_vma=False,
    )
```

```python
from functools import partial

import jax
import jax.numpy as jnp
from jax import lax
from jax.experimental import pallas as pl
from jax.experimental.pallas import tpu as pltpu
from jax.sharding import PartitionSpec as P

P_SIZE = 64
NS = 128
GROUP = 256
LANES = 128
EDGE = 8
PACK = 16
BLOCK = 256

EPS = 1e-05
HIGH = lax.Precision.HIGHEST
F32 = jnp.float32
BF16 = jnp.bfloat16
VMEM_LIMIT = 60 * 1024 * 1024
HEAD, SEQ, SECTION = "head", "seq", "section"
WIRE = F32

NN = (((1,), (0,)), ((), ()))
NT = (((1,), (1,)), ((), ()))
TN = (((0,), (0,)), ((), ()))


def call(kernel, after, grid, in_specs, out_specs, out_shape, scratch_shapes=(), prefetch=0):
    count = prefetch + len(in_specs)

    def body(*refs):
        kernel(*refs[:count], *refs[count + len(after) :])

    return pl.pallas_call(
        body,
        grid_spec=pltpu.PrefetchScalarGridSpec(
            num_scalar_prefetch=prefetch,
            grid=grid,
            in_specs=[*in_specs, *[pl.BlockSpec(memory_space=pl.ANY)] * len(after)],
            out_specs=out_specs,
            scratch_shapes=scratch_shapes,
        ),
        out_shape=out_shape,
        compiler_params=pltpu.CompilerParams(vmem_limit_bytes=VMEM_LIMIT),
        name=getattr(kernel, "func", kernel).__name__,
    )


def low_dot(a, b, dims):
    return lax.dot_general(a.astype(BF16), b.astype(BF16), dims, preferred_element_type=F32)


def high_dot(a, b, dims):
    return lax.dot_general(a, b, dims, precision=HIGH, preferred_element_type=F32)


def split_dot(a, b, dims):
    a_high, b_high = a.astype(BF16), b.astype(BF16)
    a_low = (a - a_high.astype(F32)).astype(BF16)
    b_low = (b - b_high.astype(F32)).astype(BF16)
    dot = partial(lax.dot_general, dimension_numbers=dims, preferred_element_type=F32)
    return dot(a_high, b_high) + (dot(a_high, b_low) + dot(a_low, b_high))


def iota(shape, dim):
    return lax.broadcasted_iota(jnp.int32, shape, dim)


def softplus(v):
    return jnp.maximum(v, 0.0) + jnp.log1p(jnp.exp(-jnp.abs(v)))


def sigmoid(v):
    return 1.0 / (1.0 + jnp.exp(-v))


def column(values, lane):
    return jnp.sum(jnp.where(iota(values.shape, 1) == lane, values, 0.0), axis=1, keepdims=True)


def convolve(ext_ref, kernel_ref, bias_ref, rows):
    taps = kernel_ref.shape[0]
    total = bias_ref[...] + kernel_ref[0:1, :] * ext_ref[EDGE - taps + 1 : EDGE - taps + 1 + rows, :]
    for k in range(1, taps):
        at = EDGE - taps + 1 + k
        total = total + kernel_ref[k : k + 1, :] * ext_ref[at : at + rows, :]
    return total


def convolve_back(grad_ref, ext_ref, kernel_ref, grad, rows):
    taps = kernel_ref.shape[0]
    width = grad.shape[1]
    grad_ref[0:EDGE, :] = jnp.zeros((EDGE, width), F32)
    grad_ref[EDGE : EDGE + rows, :] = grad
    grad_ref[EDGE + rows :, :] = jnp.zeros((EDGE, width), F32)
    total = kernel_ref[0:1, :] * grad_ref[taps - 1 : taps - 1 + rows + EDGE, :]
    for k in range(1, taps):
        at = taps - 1 - k
        total = total + kernel_ref[k : k + 1, :] * grad_ref[at : at + rows + EDGE, :]
    small = []
    for k in range(taps):
        at = EDGE - taps + 1 + k
        small.append(jnp.sum(grad * ext_ref[at : at + rows, :], axis=0, keepdims=True))
    small.append(jnp.sum(grad, axis=0, keepdims=True))
    return total, small


def chunk_sums(steps, decay_log, rows):
    rates = -steps * jnp.exp(decay_log)
    lower = jnp.where(iota((GROUP, GROUP), 0) >= iota((GROUP, GROUP), 1), 1.0, 0.0)
    parts = [high_dot(lower, rates[at : at + GROUP], NN) for at in range(0, rows, GROUP)]
    return rates, jnp.concatenate(parts, axis=0)


def pair_select(first, second, shape, dim):
    return jnp.where(iota(shape, dim) < P_SIZE, first, second)


def pack_decay(packed_ref, within_ref, chunks):
    total = within_ref[GROUP - 1 : GROUP, :]
    for c in range(1, chunks):
        total = total + within_ref[(c + 1) * GROUP - 1 : (c + 1) * GROUP, :]
    decay = jnp.exp(total)
    kind = packed_ref.dtype
    high = decay.astype(kind)
    rest = (decay - high.astype(F32)).astype(kind)
    packed_ref[packed_ref.shape[0] - PACK :, :] = jnp.concatenate(
        [high, rest, jnp.zeros((PACK - 2, LANES), kind)], axis=0
    )


def head_factors(decay, count, first_head):
    owner = iota((count, LANES), 0) // P_SIZE + first_head
    return jnp.sum(jnp.where(iota((count, LANES), 1) == owner, decay, 0.0), axis=1, keepdims=True)


def decay_of(rows):
    return rows[0:1, :].astype(F32) + rows[1:2, :].astype(F32)


def unpack_states(seq, forward, state_refs, decay_rows, first_head):
    count = state_refs[0].shape[0]
    total = jnp.zeros((count, NS), F32)
    passed = jnp.ones((1, LANES), F32)
    for level, (ref, rows) in enumerate(zip(state_refs, decay_rows)):
        used = (lax.shift_right_logical(seq, level) & 1) == (1 if forward else 0)
        part = head_factors(passed, count, first_head) * ref[...].astype(F32)
        total = total + jnp.where(used, part, 0.0)
        passed = jnp.where(used, passed * decay_of(rows), passed)
    return total


def merge_kernel(forward, level, seq_ref, own_ref, got_ref, out_ref):
    width = own_ref.shape[0] - PACK
    right = (lax.shift_right_logical(seq_ref[0], level) & 1) == 1
    own_late = right if forward else jnp.logical_not(right)
    own, got = own_ref[0:width, :].astype(F32), got_ref[0:width, :].astype(F32)
    own_decay, got_decay = decay_of(own_ref[width:, :]), decay_of(got_ref[width:, :])
    decay = jnp.where(own_late, own_decay, got_decay)
    factors = head_factors(decay, width, 0)
    out_ref[0:width, :] = (
        factors * jnp.where(own_late, got, own) + jnp.where(own_late, own, got)
    ).astype(out_ref.dtype)
    both = own_decay * got_decay
    high = both.astype(out_ref.dtype)
    rest = (both - high.astype(F32)).astype(out_ref.dtype)
    out_ref[width:, :] = jnp.concatenate(
        [high, rest, jnp.zeros((PACK - 2, LANES), out_ref.dtype)], axis=0
    )


def merge(after, seq, forward, level, own, got):
    spec = pl.BlockSpec(own.shape, lambda i, seq_ref: (0, 0))
    return call(
        partial(merge_kernel, forward, level),
        after,
        grid=(1,),
        in_specs=[spec, spec],
        out_specs=spec,
        out_shape=jax.ShapeDtypeStruct(own.shape, own.dtype),
        prefetch=1,
    )(seq, own, got, *after)


def stat_add_kernel(a_ref, b_ref, out_ref):
    out_ref[...] = a_ref[...] + b_ref[...]


def stat_add(after, a, b):
    spec = pl.BlockSpec(a.shape, lambda i: (0, 0))
    return call(
        stat_add_kernel,
        after,
        grid=(1,),
        in_specs=[spec, spec],
        out_specs=spec,
        out_shape=jax.ShapeDtypeStruct(a.shape, a.dtype),
    )(a, b, *after)


def scan_forward_kernel(
    dot,
    inner_ref, state_ref, dt_ref, edge_in_ref, edge_st_ref, ker_in_ref, bias_in_ref,
    ker_st_ref, bias_st_ref, step_bias_ref, decay_ref, skip_ref,
    out_ref, kq_ref, step_ref, within_ref, starts_ref, packed_ref,
    scores_ref, turned_ref, ext_ref, ext_st_ref,
):
    pair = pl.program_id(0)
    rows = inner_ref.shape[0]
    chunks = rows // GROUP

    @pl.when(pair == 0)
    def _():
        ext_st_ref[0:EDGE, :] = edge_st_ref[...]
        ext_st_ref[EDGE:, :] = state_ref[...]
        pre = convolve(ext_st_ref, ker_st_ref, bias_st_ref, rows)
        kq_ref[...] = pre * sigmoid(pre)
        steps = softplus(dt_ref[...] + step_bias_ref[...])
        _, within = chunk_sums(steps, decay_ref[...], rows)
        step_ref[...] = steps
        within_ref[...] = within
        turned_ref[...] = within.T
        pack_decay(packed_ref, within_ref, chunks)
        for c in range(chunks):
            at = slice(c * GROUP, (c + 1) * GROUP)
            scores_ref[c] = high_dot(kq_ref[at, NS:], kq_ref[at, :NS], NT)

    ext_ref[0:EDGE, :] = edge_in_ref[...]
    ext_ref[EDGE:, :] = inner_ref[...]
    pre = convolve(ext_ref, ker_in_ref, bias_in_ref, rows)
    values = pre * sigmoid(pre)
    within_cols = [column(within_ref[...], 2 * pair + k) for k in range(2)]
    step_cols = [column(step_ref[...], 2 * pair + k) for k in range(2)]
    shape = (rows, LANES)
    scaled = values * pair_select(step_cols[0], step_cols[1], shape, 1)
    within_wide = pair_select(within_cols[0], within_cols[1], shape, 1)
    causal = iota((GROUP, GROUP), 0) >= iota((GROUP, GROUP), 1)
    state = jnp.zeros((LANES, NS), F32)
    for c in range(chunks):
        at = slice(c * GROUP, (c + 1) * GROUP)
        scaled_low = scaled[at]
        halves = []
        ends = []
        for k in range(2):
            row = turned_ref[pl.ds(2 * pair + k, 1), at]
            decays = jnp.exp(jnp.where(causal, within_cols[k][at] - row, -1e30))
            halves.append(dot(decays * scores_ref[c], scaled_low, NN))
            ends.append(within_cols[k][(c + 1) * GROUP - 1 : (c + 1) * GROUP])
        result = pair_select(halves[0], halves[1], (GROUP, LANES), 1)
        if c > 0:
            result = result + jnp.exp(within_wide[at]) * dot(kq_ref[at, NS:], state, NT)
        out_ref[at, :] = result + skip_ref[...] * values[at]
        starts_ref[c] = state
        end_wide = pair_select(ends[0], ends[1], (1, LANES), 1)
        tail = jnp.exp(end_wide - within_wide[at])
        piece = dot(scaled[at] * tail, kq_ref[at, :NS], TN)
        state = jnp.exp(pair_select(ends[0], ends[1], (LANES, 1), 0)) * state + piece
    packed_ref[pl.ds(pl.multiple_of(pair * LANES, LANES), LANES), :] = state


def scan_forward(after, dot, pre, pre_st, edge, small):
    rows = pre.shape[0]
    width = small["bias_inner"].shape[1]
    pairs = width // LANES
    chunks = rows // GROUP
    taps = small["kernel_inner"].shape[0]
    block = lambda shape, index: pl.BlockSpec(shape, index)
    const2 = lambda p: (0, 0)
    return call(
        partial(scan_forward_kernel, dot),
        after,
        grid=(pairs,),
        in_specs=[
            block((rows, LANES), lambda p: (0, pairs + p)),
            block((rows, 2 * NS), lambda p: (0, 0)),
            block((rows, LANES), lambda p: (0, 2)),
            block((EDGE, LANES), lambda p: (0, p)),
            block((EDGE, 2 * NS), lambda p: (0, pairs // 2)),
            block((taps, LANES), lambda p: (0, p)),
            block((1, LANES), lambda p: (0, p)),
            block((taps, 2 * NS), const2),
            block((1, 2 * NS), const2),
            block((1, LANES), const2),
            block((1, LANES), const2),
            block((1, LANES), lambda p: (0, p)),
        ],
        out_specs=[
            block((rows, LANES), lambda p: (0, p)),
            block((rows, 2 * NS), const2),
            block((rows, LANES), const2),
            block((rows, LANES), const2),
            block((chunks, LANES, NS), lambda p: (0, p, 0)),
            block((width + PACK, NS), const2),
        ],
        out_shape=[
            jax.ShapeDtypeStruct((rows, width), F32),
            jax.ShapeDtypeStruct((rows, 2 * NS), F32),
            jax.ShapeDtypeStruct((rows, LANES), F32),
            jax.ShapeDtypeStruct((rows, LANES), F32),
            jax.ShapeDtypeStruct((chunks, width, NS), F32),
            jax.ShapeDtypeStruct((width + PACK, NS), F32),
        ],
        scratch_shapes=[
            pltpu.VMEM((chunks, GROUP, GROUP), F32),
            pltpu.VMEM((LANES, rows), F32),
            pltpu.VMEM((rows + EDGE, LANES), F32),
            pltpu.VMEM((rows + EDGE, 2 * NS), F32),
        ],
    )(
        pre, pre_st, pre_st, edge, edge, small["kernel_inner"], small["bias_inner"],
        small["kernel_state"], small["bias_state"], small["step_bias"], small["decay_log"],
        small["skip_wide"], *after,
    )


def scan_backward_kernel(
    seq_ref, inner_ref, state_ref, dt_ref, edge_in_ref, edge_st_ref, ker_in_ref, bias_in_ref,
    ker_st_ref, bias_st_ref, step_bias_ref, decay_ref, skip_ref,
    kq_ref, step_ref, within_ref, starts_ref, before_ref, grad_ref, *refs,
):
    arrived = len(refs) - 19
    after_refs, decay_refs, refs = refs[: arrived // 2], refs[arrived // 2 : arrived], refs[arrived:]
    (inner_out, edge_out, small_in_out, state_out, small_st_out, raw_out, small_dt_out,
    scores_ref, turned_ref, ext_ref, ext_st_ref, back_ref, back_st_ref,
    grad_scores, grad_kq, grad_within, grad_turned, grad_steps, grad_ends) = refs
    pair = pl.program_id(0)
    rows = inner_ref.shape[0]
    chunks = rows // GROUP
    taps = ker_in_ref.shape[0]

    @pl.when(pair == 0)
    def _():
        turned_ref[...] = within_ref[...].T
        for c in range(chunks):
            at = slice(c * GROUP, (c + 1) * GROUP)
            scores_ref[c] = high_dot(kq_ref[at, NS:], kq_ref[at, :NS], NT)
        for ref in (grad_scores, grad_kq, grad_within, grad_turned, grad_steps, grad_ends):
            ref[...] = jnp.zeros_like(ref)

    ext_ref[0:EDGE, :] = edge_in_ref[...]
    ext_ref[EDGE:, :] = inner_ref[...]
    pre = convolve(ext_ref, ker_in_ref, bias_in_ref, rows)
    sig = sigmoid(pre)
    values = pre * sig
    shape = (rows, LANES)
    within_cols = [column(within_ref[...], 2 * pair + k) for k in range(2)]
    step_cols = [column(step_ref[...], 2 * pair + k) for k in range(2)]
    step_wide = pair_select(step_cols[0], step_cols[1], shape, 1)
    scaled = values * step_wide
    within_wide = pair_select(within_cols[0], within_cols[1], shape, 1)
    causal = iota((GROUP, GROUP), 0) >= iota((GROUP, GROUP), 1)
    first_half = iota((GROUP, LANES), 1) < P_SIZE
    lanes = iota((1, LANES), 1)
    pick = jnp.where(
        iota((LANES, LANES), 1) == 2 * pair + iota((LANES, LANES), 0) // P_SIZE, 1.0, 0.0
    )
    ends = [
        [within_cols[k][(c + 1) * GROUP - 1 : (c + 1) * GROUP] for k in range(2)]
        for c in range(chunks)
    ]
    passed = [[jnp.zeros((1, 1), F32)] * 2]
    for c in range(chunks - 1):
        passed.append([passed[c][k] + ends[c][k] for k in range(2)])
    state_grad = unpack_states(
        seq_ref[0], False, after_refs, [ref[...] for ref in decay_refs], 2 * pair
    )
    value_grads = [None] * chunks
    for c in reversed(range(chunks)):
        at = slice(c * GROUP, (c + 1) * GROUP)
        start_decay = jnp.exp(pair_select(passed[c][0], passed[c][1], (LANES, 1), 0))
        state = starts_ref[c] + start_decay * before_ref[...]
        grad = grad_ref[at, :]
        grad_low = grad.astype(BF16)
        scaled_low = scaled[at].astype(BF16)
        keys = kq_ref[at, :NS].astype(BF16)
        reads = kq_ref[at, NS:].astype(BF16)
        state_low = state.astype(BF16)
        state_grad_low = state_grad.astype(BF16)
        halves = []
        for k in range(2):
            head = 2 * pair + k
            row = turned_ref[pl.ds(head, 1), at]
            decays = jnp.exp(jnp.where(causal, within_cols[k][at] - row, -1e30))
            weights = decays * scores_ref[c]
            mine = first_half if k == 0 else jnp.logical_not(first_half)
            own = jnp.where(mine, grad, 0.0).astype(BF16)
            weight_grad = lax.dot_general(own, scaled_low, NT, preferred_element_type=F32)
            halves.append(low_dot(weights, grad_low, TN))
            grad_scores[c] += weight_grad * decays
            moved = weight_grad * weights
            grad_within[at, :] += jnp.where(
                lanes == head, jnp.sum(moved, axis=1, keepdims=True), 0.0
            )
            grad_turned[pl.ds(head, 1), at] = jnp.sum(moved, axis=0, keepdims=True)
        scaled_grad = pair_select(halves[0], halves[1], (GROUP, LANES), 1)
        end_wide = pair_select(ends[c][0], ends[c][1], (1, LANES), 1)
        tail = jnp.exp(end_wide - within_wide[at])
        late = tail * lax.dot_general(keys, state_grad_low, NT, preferred_element_type=F32)
        late_sums = high_dot(scaled[at] * late, pick, NN)
        scaled_grad = scaled_grad + late
        grad_kq[at, :NS] += low_dot(scaled[at] * tail, state_grad_low, NN)
        entry = jnp.exp(within_wide[at])
        early = entry * lax.dot_general(reads, state_low, NT, preferred_element_type=F32)
        early_sums = high_dot(grad * early, pick, NN)
        grad_entry = (grad * entry).astype(BF16)
        grad_kq[at, NS:] += lax.dot_general(grad_entry, state_low, NN, preferred_element_type=F32)
        grad_within[at, :] += early_sums - late_sums
        end_decay = jnp.exp(pair_select(ends[c][0], ends[c][1], (LANES, 1), 0))
        kept = end_decay * state_grad * state
        kept_sum = jnp.sum(kept, axis=1, keepdims=True)
        kept_sums = jnp.sum(kept_sum * pick, axis=0, keepdims=True)
        grad_ends[c : c + 1, :] += jnp.sum(late_sums, axis=0, keepdims=True) + kept_sums
        grad_steps[at, :] += high_dot(values[at] * scaled_grad, pick, NN)
        value_grads[c] = step_wide[at] * scaled_grad + skip_ref[...] * grad
        state_grad = end_decay * state_grad + lax.dot_general(
            grad_entry, reads, TN, preferred_element_type=F32
        )
    value_grad = jnp.concatenate(value_grads, axis=0)
    pre_grad = value_grad * sig * (1.0 + pre * (1.0 - sig))
    total, small = convolve_back(back_ref, ext_ref, ker_in_ref, pre_grad, rows)
    edge_out[:, pl.ds(pl.multiple_of(pair * LANES, LANES), LANES)] = total[0:EDGE]
    inner_out[...] = total[EDGE:]
    small.append(jnp.sum(grad_ref[...] * values, axis=0, keepdims=True))
    small.append(jnp.zeros((8 - len(small), LANES), F32))
    small_in_out[...] = jnp.concatenate(small, axis=0)

    @pl.when(pair == pl.num_programs(0) - 1)
    def _():
        upper = jnp.where(iota((GROUP, GROUP), 0) <= iota((GROUP, GROUP), 1), 1.0, 0.0)
        scale = -jnp.exp(decay_ref[...])
        decay_grad = jnp.zeros((1, LANES), F32)
        back = grad_turned[...].T
        for c in range(chunks):
            at = slice(c * GROUP, (c + 1) * GROUP)
            grad_kq[at, NS:] += high_dot(grad_scores[c], kq_ref[at, :NS], NN)
            grad_kq[at, :NS] += high_dot(grad_scores[c], kq_ref[at, NS:], TN)
            rate_grad = high_dot(upper, grad_within[at, :] - back[at], NN) + grad_ends[c : c + 1, :]
            grad_steps[at, :] += rate_grad * scale
            decay_grad += jnp.sum(rate_grad * scale * step_ref[at, :], axis=0, keepdims=True)
        raw = grad_steps[...] * sigmoid(dt_ref[...] + step_bias_ref[...])
        raw_out[...] = raw
        raw_sum = jnp.sum(raw, axis=0, keepdims=True)
        small_dt_out[...] = jnp.concatenate(
            [raw_sum, decay_grad, jnp.zeros((6, LANES), F32)], axis=0
        )
        ext_st_ref[0:EDGE, :] = edge_st_ref[...]
        ext_st_ref[EDGE:, :] = state_ref[...]
        pre_st = convolve(ext_st_ref, ker_st_ref, bias_st_ref, rows)
        sig_st = sigmoid(pre_st)
        pre_st_grad = grad_kq[...] * sig_st * (1.0 + pre_st * (1.0 - sig_st))
        total_st, small_st = convolve_back(back_st_ref, ext_st_ref, ker_st_ref, pre_st_grad, rows)
        edge_out[:, edge_out.shape[1] - 2 * NS :] = total_st[0:EDGE]
        state_out[...] = total_st[EDGE:]
        small_st.append(jnp.zeros((8 - len(small_st), 2 * NS), F32))
        small_st_out[...] = jnp.concatenate(small_st, axis=0)


def scan_backward(after, seq, pre, pre_st, edge, small, kq, steps, within, starts, before, later, grad):
    rows = pre.shape[0]
    width = grad.shape[1]
    pairs = width // LANES
    chunks = rows // GROUP
    taps = small["kernel_inner"].shape[0]
    block = lambda shape, index: pl.BlockSpec(shape, index)
    const2 = lambda p, seq_ref: (0, 0)
    lane2 = lambda p, seq_ref: (0, p)
    return call(
        scan_backward_kernel,
        after,
        grid=(pairs,),
        in_specs=[
            block((rows, LANES), lambda p, seq_ref: (0, pairs + p)),
            block((rows, 2 * NS), lambda p, seq_ref: (0, 0)),
            block((rows, LANES), lambda p, seq_ref: (0, 2)),
            block((EDGE, LANES), lane2),
            block((EDGE, 2 * NS), lambda p, seq_ref: (0, pairs // 2)),
            block((taps, LANES), lane2),
            block((1, LANES), lane2),
            block((taps, 2 * NS), const2),
            block((1, 2 * NS), const2),
            block((1, LANES), const2),
            block((1, LANES), const2),
            block((1, LANES), lane2),
            block((rows, 2 * NS), const2),
            block((rows, LANES), const2),
            block((rows, LANES), const2),
            block((chunks, LANES, NS), lambda p, seq_ref: (0, p, 0)),
            block((LANES, NS), lambda p, seq_ref: (p, 0)),
            block((rows, LANES), lane2),
        ]
        + [block((LANES, NS), lambda p, seq_ref: (p, 0))] * len(later)
        + [block((PACK, NS), lambda p, seq_ref: (width // PACK, 0))] * len(later),
        out_specs=[
            block((rows, LANES), lane2),
            block((EDGE, width + 2 * NS), const2),
            block((8, LANES), lane2),
            block((rows, 2 * NS), const2),
            block((8, 2 * NS), const2),
            block((rows, LANES), const2),
            block((8, LANES), const2),
        ],
        out_shape=[
            jax.ShapeDtypeStruct((rows, width), F32),
            jax.ShapeDtypeStruct((EDGE, width + 2 * NS), F32),
            jax.ShapeDtypeStruct((8, width), F32),
            jax.ShapeDtypeStruct((rows, 2 * NS), F32),
            jax.ShapeDtypeStruct((8, 2 * NS), F32),
            jax.ShapeDtypeStruct((rows, LANES), F32),
            jax.ShapeDtypeStruct((8, LANES), F32),
        ],
        scratch_shapes=[
            pltpu.VMEM((chunks, GROUP, GROUP), F32),
            pltpu.VMEM((LANES, rows), F32),
            pltpu.VMEM((rows + EDGE, LANES), F32),
            pltpu.VMEM((rows + EDGE, 2 * NS), F32),
            pltpu.VMEM((rows + 2 * EDGE, LANES), F32),
            pltpu.VMEM((rows + 2 * EDGE, 2 * NS), F32),
            pltpu.VMEM((chunks, GROUP, GROUP), F32),
            pltpu.VMEM((rows, 2 * NS), F32),
            pltpu.VMEM((rows, LANES), F32),
            pltpu.VMEM((LANES, rows), F32),
            pltpu.VMEM((rows, LANES), F32),
            pltpu.VMEM((8, LANES), F32),
        ],
        prefetch=1,
    )(
        seq, pre, pre_st, pre_st, edge, edge, small["kernel_inner"], small["bias_inner"],
        small["kernel_state"], small["bias_state"], small["step_bias"], small["decay_log"],
        small["skip_wide"], kq, steps, within, starts, before, grad, *later, *later, *after,
    )


def widen(values, width):
    spread = jnp.where(
        iota((LANES, width), 1) // P_SIZE == iota((LANES, width), 0), 1.0, 0.0
    ).astype(BF16)
    high = values.astype(BF16)
    rest = (values - high.astype(F32)).astype(BF16)
    return lax.dot_general(high, spread, NN, preferred_element_type=F32) + lax.dot_general(
        rest, spread, NN, preferred_element_type=F32
    )


def entry_decay(within_ref, chunk, chunks):
    offset = jnp.zeros((1, LANES), F32)
    for c in range(chunks - 1):
        offset = offset + jnp.where(c < chunk, within_ref[(c + 1) * GROUP - 1 : (c + 1) * GROUP, :], 0.0)
    at = pl.multiple_of(chunk * GROUP, GROUP)
    return jnp.exp(within_ref[pl.ds(at, GROUP), :] + offset)


def stat_columns(stat_refs):
    height, length = stat_refs[0].shape
    total = stat_refs[0][...]
    for ref in stat_refs[1:]:
        total = total + ref[...]
    return jnp.concatenate([total, jnp.zeros((LANES - height, length), F32)], axis=0).T


def mix_first_kernel(dot, chunks, arrived, with_grad, seq_ref, *refs):
    local_ref, gate_ref, reads_ref, within_ref, gain_ref = refs[:5]
    arrived_refs = refs[5 : 5 + arrived]
    refs = refs[5 + arrived :]
    if with_grad:
        proj_ref, up_ref, mixer_ref, before_ref, stats_ref, back_ref = refs
    else:
        mixer_ref, before_ref, stats_ref = refs
    width = local_ref.shape[1]
    chunk = pl.program_id(0)

    @pl.when(chunk == 0)
    def _():
        states = [ref.at[0:width, :] for ref in arrived_refs]
        decays = [ref[width:, :] for ref in arrived_refs]
        before_ref[...] = unpack_states(seq_ref[0], True, states, decays, 0)

    entry = widen(entry_decay(within_ref, chunk, chunks), width)
    mixer = local_ref[...] + entry * dot(reads_ref[...], before_ref[...], NT)
    mixer_ref[...] = mixer
    gate = gate_ref[...]
    gated = mixer * gate * sigmoid(gate)
    ones = jnp.ones((8, width), F32)
    stats = high_dot(ones, gated * gated, NT)
    if with_grad:
        back = lax.dot_general(up_ref[...], proj_ref[...], NT, preferred_element_type=F32)
        back_ref[...] = back
        other = high_dot(ones, back * gated * gain_ref[...], NT)
        stats = jnp.where(iota(stats.shape, 0) == 1, other, stats)
    stats_ref[...] = stats


def mix_first(after, seq, dot, local, pre, kq, within, gain, arrived, upstream=None, proj_out=None):
    rows, width = local.shape
    chunks = rows // GROUP
    block = lambda shape, index: pl.BlockSpec(shape, index)
    row2 = lambda c, seq_ref: (c, 0)
    const2 = lambda c, seq_ref: (0, 0)
    with_grad = upstream is not None
    in_specs = [
        block((GROUP, width), row2),
        block((GROUP, width), row2),
        block((GROUP, NS), lambda c, seq_ref: (c, 1)),
        block((rows, LANES), const2),
        block((1, width), const2),
    ] + [block((width + PACK, NS), const2)] * len(arrived)
    out_specs = [
        block((GROUP, width), row2),
        block((width, NS), const2),
        block((8, GROUP), lambda c, seq_ref: (0, c)),
    ]
    out_shape = [
        jax.ShapeDtypeStruct((rows, width), F32),
        jax.ShapeDtypeStruct((width, NS), F32),
        jax.ShapeDtypeStruct((8, rows), F32),
    ]
    args = [local, pre, kq, within, gain, *arrived]
    flops = 4 * rows * width * NS
    if with_grad:
        features = upstream.shape[1]
        in_specs += [block((width, features), const2), block((GROUP, features), row2)]
        out_specs.append(block((GROUP, width), row2))
        out_shape.append(jax.ShapeDtypeStruct((rows, width), F32))
        args += [proj_out, upstream]
        flops += 2 * rows * width * features
    return call(
        partial(mix_first_kernel, dot, chunks, len(arrived), with_grad),
        after,
        grid=(chunks,),
        in_specs=in_specs,
        out_specs=out_specs,
        out_shape=out_shape,
        prefetch=1,
    )(seq, *args, *after)


def project_out_kernel(total_width, count, *refs):
    mixer_ref, gate_ref, gain_ref, proj_ref = refs[:4]
    part_ref = refs[4 + count]
    scale = lax.rsqrt(stat_columns(refs[4 : 4 + count])[:, 0:1] / total_width + EPS)
    gate = gate_ref[...]
    normed = (mixer_ref[...] * gate * sigmoid(gate) * scale * gain_ref[...]).astype(BF16)
    part_ref[...] = lax.dot_general(normed, proj_ref[...], NN, preferred_element_type=F32)


def project_out(after, chunk, mixer, pre, gain, stats, proj_out, total_width):
    width = mixer.shape[1]
    features = proj_out.shape[1]
    block = lambda shape, index: pl.BlockSpec(shape, index)
    const2 = lambda c: (0, 0)
    return call(
        partial(project_out_kernel, total_width, len(stats)),
        after,
        grid=(1,),
        in_specs=[
            block((GROUP, width), lambda c: (chunk, 0)),
            block((GROUP, width), lambda c: (chunk, 0)),
            block((1, width), const2),
            block((width, features), const2),
        ]
        + [block((8, GROUP), lambda c: (0, chunk))] * len(stats),
        out_specs=block((GROUP, features), const2),
        out_shape=jax.ShapeDtypeStruct((GROUP, features), F32),
    )(mixer, pre, gain, proj_out, *stats, *after)


def assemble(place_ref, refs, out_ref):
    size = refs[0].shape[0]
    inner = (place_ref[0] == 1) | (place_ref[0] == 2)
    for chunk in range(len(refs) // 2):
        at = slice(chunk * size, (chunk + 1) * size)

        @pl.when(inner)
        def _(chunk=chunk, at=at):
            out_ref[at, :] = refs[2 * chunk][...]

        @pl.when(jnp.logical_not(inner))
        def _(chunk=chunk, at=at):
            out_ref[at, :] = refs[2 * chunk + 1][...]


def join_kernel(place_ref, done_ref, crossed_ref, out_ref):
    half = done_ref.shape[0]

    @pl.when(place_ref[0] < 2)
    def _():
        out_ref[0:half, :] = done_ref[...]
        out_ref[half:, :] = crossed_ref[...]

    @pl.when(place_ref[0] >= 2)
    def _():
        out_ref[0:half, :] = crossed_ref[...]
        out_ref[half:, :] = done_ref[...]


def join(after, place, done, crossed):
    half, features = done.shape
    spec = pl.BlockSpec((half, features), lambda i, place_ref: (0, 0))
    return call(
        join_kernel,
        after,
        grid=(1,),
        in_specs=[spec, spec],
        out_specs=pl.BlockSpec((2 * half, features), lambda i, place_ref: (0, 0)),
        out_shape=jax.ShapeDtypeStruct((2 * half, features), done.dtype),
        prefetch=1,
    )(place, done, crossed, *after)


def project_kernel(assembled, place_ref, *refs):
    if assembled:
        pieces = refs[:assembled]
        gain_ref, wide_ref, bc_ref, dt_ref, normed_ref, scale_ref, pre_ref, state_ref, edge_ref, rows_ref = refs[assembled:]
    else:
        rows_ref, gain_ref, wide_ref, bc_ref, dt_ref, normed_ref, scale_ref, pre_ref, state_ref, edge_ref = refs
    width = wide_ref.shape[1]
    rows = pre_ref.shape[0]

    @pl.when(pl.program_id(0) == 0)
    def _():
        if assembled:
            assemble(place_ref, pieces, rows_ref)
        wide = rows_ref[...].astype(F32)
        scale = lax.rsqrt(jnp.mean(wide * wide, axis=1, keepdims=True) + EPS)
        normed = (wide * scale * gain_ref[...]).astype(BF16)
        normed_ref[...] = normed
        scale_ref[...] = scale
        state = lax.dot_general(normed, bc_ref[...], NN, preferred_element_type=F32)
        state_ref[:, 0 : 2 * NS] = state
        state_ref[:, 2 * NS :] = lax.dot_general(normed, dt_ref[...], NN, preferred_element_type=F32)
        edge_ref[:, width:] = state[rows - EDGE :]

    pre = lax.dot_general(normed_ref[...], wide_ref[...], NN, preferred_element_type=F32)
    pre_ref[...] = pre
    edge_ref[:, 0:width] = pre[rows - EDGE :]


def project(after, place, rows_in, gain, w_wide, w_bc, w_dt):
    assembled = len(rows_in) if isinstance(rows_in, (list, tuple)) else 0
    pieces = list(rows_in) if assembled else [rows_in]
    features = w_wide.shape[0]
    width = w_wide.shape[1] // 2
    rows = pieces[0].shape[0] * (assembled // 2 if assembled else 1)
    block = lambda shape, index: pl.BlockSpec(shape, index)
    const2 = lambda f, place_ref: (0, 0)
    out_specs = [
        block((rows, features), const2),
        block((rows, 1), const2),
        block((rows, width), lambda f, place_ref: (0, f)),
        block((rows, 2 * NS + LANES), const2),
        block((EDGE, width + 2 * NS), const2),
    ]
    out_shape = [
        jax.ShapeDtypeStruct((rows, features), BF16),
        jax.ShapeDtypeStruct((rows, 1), F32),
        jax.ShapeDtypeStruct((rows, 2 * width), F32),
        jax.ShapeDtypeStruct((rows, 2 * NS + LANES), F32),
        jax.ShapeDtypeStruct((EDGE, width + 2 * NS), F32),
    ]
    if assembled:
        out_specs.append(block((rows, features), const2))
        out_shape.append(jax.ShapeDtypeStruct((rows, features), BF16))
    return call(
        partial(project_kernel, assembled),
        after,
        grid=(2,),
        in_specs=[block(piece.shape, const2) for piece in pieces]
        + [
            block((1, features), const2),
            block((features, width), lambda f, place_ref: (0, f)),
            block((features, 2 * NS), const2),
            block((features, LANES), const2),
        ],
        out_specs=out_specs,
        out_shape=out_shape,
        prefetch=1,
    )(place, *pieces, gain, w_wide, w_bc, w_dt, *after)


def input_grad(total_ref, rows_ref, scale_ref, gain_ref, up_ref):
    scale = scale_ref[...]
    unit = rows_ref[...].astype(F32) * scale
    grad_unit = total_ref[...].astype(F32) * gain_ref[...]
    mean = jnp.mean(grad_unit * unit, axis=1, keepdims=True)
    return (up_ref[...].astype(F32) + scale * (grad_unit - unit * mean)).astype(BF16)


def back_first_kernel(
    total_ref, rows_ref, scale_ref, pre_gain_ref, old_ref,
    proj_ref, mixer_ref, gate_ref, gain_ref, up_ref, back_ref, stats_ref,
):
    upstream = input_grad(total_ref, rows_ref, scale_ref, pre_gain_ref, old_ref)
    up_ref[...] = upstream
    back = lax.dot_general(upstream, proj_ref[...], NT, preferred_element_type=F32)
    back_ref[...] = back
    gate = gate_ref[...]
    product = back * mixer_ref[...] * gate * sigmoid(gate) * gain_ref[...]
    stats_ref[...] = high_dot(jnp.ones((8, back.shape[1]), F32), product, NT)


def back_first(after, total, rows_in, scale, pre_gain, old, proj_out, mixer, pre, gain):
    rows, width = mixer.shape
    features = proj_out.shape[1]
    block = lambda shape, index: pl.BlockSpec(shape, index)
    row2 = lambda c: (c, 0)
    const2 = lambda c: (0, 0)
    wide = block((GROUP, features), row2)
    return call(
        back_first_kernel,
        after,
        grid=(rows // GROUP,),
        in_specs=[
            wide,
            wide,
            block((GROUP, 1), row2),
            block((1, features), const2),
            wide,
            block((width, features), const2),
            block((GROUP, width), row2),
            block((GROUP, width), row2),
            block((1, width), const2),
        ],
        out_specs=[wide, block((GROUP, width), row2), block((8, GROUP), lambda c: (0, c))],
        out_shape=[
            jax.ShapeDtypeStruct((rows, features), BF16),
            jax.ShapeDtypeStruct((rows, width), F32),
            jax.ShapeDtypeStruct((8, rows), F32),
        ],
    )(total, rows_in, scale, pre_gain, old, proj_out, mixer, pre, gain, *after)


def end_back_kernel(total_ref, rows_ref, scale_ref, gain_ref, up_ref, out_ref):
    out_ref[...] = input_grad(total_ref, rows_ref, scale_ref, gain_ref, up_ref)


def end_back(after, total, rows_in, scale, gain, upstream):
    rows, features = total.shape
    wide = pl.BlockSpec((GROUP, features), lambda c: (c, 0))
    return call(
        end_back_kernel,
        after,
        grid=(rows // GROUP,),
        in_specs=[
            wide,
            wide,
            pl.BlockSpec((GROUP, 1), lambda c: (c, 0)),
            pl.BlockSpec((1, features), lambda c: (0, 0)),
            wide,
        ],
        out_specs=wide,
        out_shape=jax.ShapeDtypeStruct((rows, features), BF16),
    )(total, rows_in, scale, gain, upstream, *after)


def end_out_kernel(per, *refs):
    for m in range(per):
        refs[2 * per + m][...] = (
            refs[per + m][...].astype(F32) + refs[m][...].astype(F32)
        ).astype(BF16)


def end_out(after, totals, rows_in):
    per = len(totals)
    rows, features = totals[0].shape
    wide = pl.BlockSpec((GROUP, features), lambda c: (c, 0))
    return call(
        partial(end_out_kernel, per),
        after,
        grid=(rows // GROUP,),
        in_specs=[wide] * (2 * per),
        out_specs=[wide] * per,
        out_shape=[jax.ShapeDtypeStruct((rows, features), BF16)] * per,
    )(*totals, *rows_in, *after)


def mix_back_kernel(chunks, total_width, squares, products, *refs):
    back_ref, mixer_ref, gate_ref, reads_ref, within_ref, gain_ref = refs[:6]
    square_refs, product_refs = refs[6 : 6 + squares], refs[6 + squares : 6 + squares + products]
    refs = refs[6 + squares + products :]
    grad_ref, gate_grad_ref, gain_grad_ref, packed_ref, normed_ref, total_ref = refs
    width = mixer_ref.shape[1]
    chunk = pl.program_id(0)
    square = stat_columns(square_refs)
    scale = lax.rsqrt(square[:, 0:1] / total_width + EPS)
    product = (stat_columns(product_refs) if products else square)[:, 1:2] / total_width
    gate = gate_ref[...]
    sig = sigmoid(gate)
    act = gate * sig
    mixer = mixer_ref[...]
    back = back_ref[...]
    gated = mixer * act
    unit = gated * scale
    normed = (unit * gain_ref[...]).astype(BF16)
    normed_ref[...] = normed
    gated_grad = scale * back * gain_ref[...] - gated * (scale * scale * scale * product)
    grad = gated_grad * act
    grad_ref[...] = grad
    gate_grad_ref[...] = (gated_grad * mixer * sig * (1.0 + gate * (1.0 - sig))).astype(BF16)
    entry = widen(entry_decay(within_ref, chunk, chunks), width)
    gain_part = jnp.sum(back * unit, axis=0, keepdims=True)
    state_part = low_dot(grad * entry, reads_ref[...], TN)

    @pl.when(chunk == 0)
    def _():
        gain_grad_ref[...] = gain_part
        total_ref[...] = state_part

    @pl.when(chunk > 0)
    def _():
        gain_grad_ref[...] += gain_part
        total_ref[...] += state_part

    @pl.when(chunk == chunks - 1)
    def _():
        packed_ref[0:width, :] = total_ref[...].astype(BF16)
        pack_decay(packed_ref, within_ref, chunks)


def mix_back(after, back, mixer, pre, kq, within, gain, square, product, total_width):
    rows, width = mixer.shape
    chunks = rows // GROUP
    block = lambda shape, index: pl.BlockSpec(shape, index)
    row2 = lambda c: (c, 0)
    const2 = lambda c: (0, 0)
    in_specs = [
        block((GROUP, width), row2),
        block((GROUP, width), row2),
        block((GROUP, width), row2),
        block((GROUP, NS), lambda c: (c, 1)),
        block((rows, LANES), const2),
        block((1, width), const2),
    ] + [block((8, GROUP), lambda c: (0, c))] * (len(square) + len(product))
    out_specs = [
        block((GROUP, width), row2),
        block((GROUP, width), row2),
        block((1, width), const2),
        block((width + PACK, NS), const2),
        block((GROUP, width), row2),
    ]
    out_shape = [
        jax.ShapeDtypeStruct((rows, width), F32),
        jax.ShapeDtypeStruct((rows, width), BF16),
        jax.ShapeDtypeStruct((1, width), F32),
        jax.ShapeDtypeStruct((width + PACK, NS), BF16),
        jax.ShapeDtypeStruct((rows, width), BF16),
    ]
    args = [back, mixer, pre, kq, within, gain, *square, *product]
    flops = 2 * rows * width * NS
    return call(
        partial(mix_back_kernel, chunks, total_width, len(square), len(product)),
        after,
        grid=(chunks,),
        in_specs=in_specs,
        out_specs=out_specs,
        out_shape=out_shape,
        scratch_shapes=[pltpu.VMEM((width, NS), F32)],
    )(*args, *after)


def late_out_kernel(per, *refs):
    proj_ref = refs[per]
    for m in range(per):
        refs[per + 1 + m][...] = lax.dot_general(
            refs[m][...], proj_ref[...], NN, preferred_element_type=F32
        ).astype(BF16)


def late_out(after, normed_outs, proj_out):
    per = len(normed_outs)
    rows, width = normed_outs[0].shape
    features = proj_out.shape[1]
    return call(
        partial(late_out_kernel, per),
        after,
        grid=(rows // GROUP,),
        in_specs=[pl.BlockSpec((GROUP, width), lambda c: (c, 0))] * per
        + [pl.BlockSpec((width, features), lambda c: (0, 0))],
        out_specs=[pl.BlockSpec((GROUP, features), lambda c: (c, 0))] * per,
        out_shape=[jax.ShapeDtypeStruct((rows, features), BF16)] * per,
    )(*normed_outs, proj_out, *after)


def project_back_kernel(
    gate_ref, inner_ref, state_ref, raw_ref, edge_ref, wide_ref, bc_ref, dt_ref, rows_ref, scale_ref,
    grads_ref, narrow_grads_ref, gain_grad_ref, part_ref,
):
    width = gate_ref.shape[1]
    rows = gate_ref.shape[0]

    @pl.when(pl.program_id(0) == 0)
    def _():
        grads_ref[:, 0:width] = gate_ref[...]
        added = jnp.concatenate(
            [jnp.zeros((EDGE, width), F32), edge_ref[:, 0:width]], axis=0
        )
        grads_ref[0 : rows - PACK, width:] = inner_ref[0 : rows - PACK, :].astype(BF16)
        grads_ref[rows - PACK :, width:] = (inner_ref[rows - PACK :, :] + added).astype(BF16)
        added = jnp.concatenate(
            [jnp.zeros((EDGE, 2 * NS), F32), edge_ref[:, width:]], axis=0
        )
        narrow_grads_ref[0 : rows - PACK, 0 : 2 * NS] = state_ref[0 : rows - PACK, :].astype(BF16)
        narrow_grads_ref[rows - PACK :, 0 : 2 * NS] = (state_ref[rows - PACK :, :] + added).astype(BF16)
        narrow_grads_ref[:, 2 * NS :] = raw_ref[...].astype(BF16)

    part = lax.dot_general(grads_ref[...], wide_ref[...], NT, preferred_element_type=F32)
    part = part + lax.dot_general(
        narrow_grads_ref[:, 0 : 2 * NS], bc_ref[...], NT, preferred_element_type=F32
    )
    part = part + lax.dot_general(
        narrow_grads_ref[:, 2 * NS :], dt_ref[...], NT, preferred_element_type=F32
    )
    unit = rows_ref[...].astype(F32) * scale_ref[...]
    gain_grad_ref[...] = jnp.sum(part * unit, axis=0, keepdims=True)
    part_ref[...] = part.astype(BF16)


def project_back(after, gate_grad, inner, state, raw, edges, w_wide, w_bc, w_dt, rows_in, scale):
    rows, width = gate_grad.shape
    features = w_wide.shape[0]
    size = 512 if features % 512 == 0 else features
    block = lambda shape, index: pl.BlockSpec(shape, index)
    const2 = lambda f: (0, 0)
    narrow = 2 * NS + LANES
    return call(
        project_back_kernel,
        after,
        grid=(features // size,),
        in_specs=[
            block((rows, width), const2),
            block((rows, width), const2),
            block((rows, 2 * NS), const2),
            block((rows, LANES), const2),
            block((EDGE, width + 2 * NS), const2),
            block((size, 2 * width), lambda f: (f, 0)),
            block((size, 2 * NS), lambda f: (f, 0)),
            block((size, LANES), lambda f: (f, 0)),
            block((rows, size), lambda f: (0, f)),
            block((rows, 1), const2),
        ],
        out_specs=[
            block((rows, 2 * width), const2),
            block((rows, narrow), const2),
            block((1, size), lambda f: (0, f)),
            block((rows, size), lambda f: (0, f)),
        ],
        out_shape=[
            jax.ShapeDtypeStruct((rows, 2 * width), BF16),
            jax.ShapeDtypeStruct((rows, narrow), BF16),
            jax.ShapeDtypeStruct((1, features), F32),
            jax.ShapeDtypeStruct((rows, features), BF16),
        ],
    )(gate_grad, inner, state, raw, edges, w_wide, w_bc, w_dt, rows_in, scale, *after)


def add_half_kernel(index_ref, own_ref, first_ref, out_ref):
    out_ref[...] = (own_ref[...].astype(F32) + first_ref[...].astype(F32)).astype(out_ref.dtype)


def add_half(after, index, own, first, kind):
    half = own.shape[0] // 2
    features = own.shape[1]
    pick = pl.BlockSpec((half, features), lambda i, index_ref: (index_ref[0], 0))
    return call(
        add_half_kernel,
        after,
        grid=(1,),
        in_specs=[pick, pick],
        out_specs=pl.BlockSpec((half, features), lambda i, index_ref: (0, 0)),
        out_shape=jax.ShapeDtypeStruct((half, features), kind),
        prefetch=1,
    )(index, own, first, *after)


def finish_out_kernel(index_ref, own_ref, first_ref, second_ref, rows_ref, out_ref):
    total = own_ref[...].astype(F32) + first_ref[...].astype(F32) + second_ref[...].astype(F32)
    out_ref[...] = (rows_ref[...].astype(F32) + total).astype(BF16)


def finish_half(after, index, chunk, own, first, second, rows_in):
    half, features = second.shape
    pick = pl.BlockSpec((half, features), lambda i, index_ref: (index_ref[0], 0))
    whole = pl.BlockSpec((half, features), lambda i, index_ref: (2 * chunk + index_ref[0], 0))
    same = pl.BlockSpec((half, features), lambda i, index_ref: (0, 0))
    one = pl.BlockSpec((1, features), lambda i, index_ref: (0, 0))
    in_specs = [pick, pick, same, whole]
    args = [own, first, second, rows_in]
    return call(
        finish_out_kernel,
        after,
        grid=(1,),
        in_specs=in_specs,
        out_specs=same,
        out_shape=jax.ShapeDtypeStruct((half, features), BF16),
        prefetch=1,
    )(index, *args, *after)


def weight_grads_kernel(per, share, section_ref, *refs):
    kept_ref, given_ref, total_ref = refs[5 * per :]
    at = 0
    for left, right in ((0, 2), (0, 3), (1, 4)):
        width = refs[right].shape[1]
        part = None
        for m in range(per):
            product = lax.dot_general(
                refs[5 * m + left][...], refs[5 * m + right][...], TN, preferred_element_type=F32
            )
            part = product if part is None else part + product
        total_ref[:, at : at + width] = part
        at += width
    half = share // 2
    for i in range(total_ref.shape[0] // share):
        to = slice(i * half, (i + 1) * half)
        mine = pl.multiple_of(i * share + section_ref[0] * half, half)
        theirs = pl.multiple_of(i * share + (1 - section_ref[0]) * half, half)
        kept_ref[to, :] = total_ref[pl.ds(mine, half), :].astype(BF16)
        given_ref[to, :] = total_ref[pl.ds(theirs, half), :].astype(BF16)


def weight_grads(after, section, terms, share):
    rows, features = terms[0][0].shape
    size = 384
    block = lambda shape, index: pl.BlockSpec(shape, index)
    in_specs = []
    args = []
    for normed, up, grads, narrow, normed_out in terms:
        in_specs += [block((rows, size), lambda f, section_ref: (0, f))] * 2
        in_specs += [block(a.shape, lambda f, section_ref: (0, 0)) for a in (grads, narrow, normed_out)]
        args += [normed, up, grads, narrow, normed_out]
    total = sum(a.shape[1] for a in terms[0][2:])
    return call(
        partial(weight_grads_kernel, len(terms), share),
        after,
        grid=(features // size,),
        in_specs=in_specs,
        out_specs=[block((size // 2, total), lambda f, section_ref: (f, 0))] * 2,
        out_shape=[jax.ShapeDtypeStruct((features // 2, total), BF16)] * 2,
        scratch_shapes=[pltpu.VMEM((size, total), F32)],
        prefetch=1,
    )(section, *args, *after)


def place_kernel(per, section_ref, *refs):
    out_ref, buffer, come, go = refs[-4:]
    for section in range(2):

        @pl.when(section_ref[0] == section)
        def _(section=section):
            ins, outs = [], []
            for m in range(2 * per):
                own = m // per == section
                source = refs[(2 * section + (0 if own else 1)) * per + m % per]
                ins.append(pltpu.make_async_copy(source, buffer.at[m], come.at[m]))
                outs.append(pltpu.make_async_copy(buffer.at[m], out_ref.at[m], go.at[m]))
            for copy in ins:
                copy.start()
            for first, second in zip(ins, outs):
                first.wait()
                second.start()
            for copy in outs:
                copy.wait()


def place_layers(after, section, first, first_got, second, second_got):
    count = 2 * len(first)
    rows, features = first[0].shape
    spot = pl.BlockSpec(memory_space=pl.ANY)
    return call(
        partial(place_kernel, len(first)),
        after,
        grid=(1,),
        in_specs=[spot] * (2 * count),
        out_specs=spot,
        out_shape=jax.ShapeDtypeStruct((count, rows, features), BF16),
        scratch_shapes=[
            pltpu.VMEM((count, rows, features), BF16),
            pltpu.SemaphoreType.DMA((count,)),
            pltpu.SemaphoreType.DMA((count,)),
        ],
        prefetch=1,
    )(section, *first, *first_got, *second, *second_got, *after)


def hold_kernel(*refs):
    pass


def hold(after, arrays):
    count = len(arrays)
    spot = pl.BlockSpec(memory_space=pl.ANY)
    return pl.pallas_call(
        hold_kernel,
        in_specs=[spot] * (count + len(after)),
        out_specs=[spot] * count,
        out_shape=[jax.ShapeDtypeStruct(a.shape, a.dtype) for a in arrays],
        input_output_aliases={k: k for k in range(count)},
    )(*arrays, *after)


SMALL_NAMES = (
    "pre_gain", "kernel_inner", "bias_inner", "kernel_state", "bias_state",
    "step_bias", "decay_log", "skip_wide", "norm_gain",
)


def small_layout(features, width, taps):
    shapes = {
        "pre_gain": (1, features),
        "kernel_inner": (taps, width),
        "bias_inner": (1, width),
        "kernel_state": (taps, 2 * NS),
        "bias_state": (1, 2 * NS),
        "step_bias": (1, LANES),
        "decay_log": (1, LANES),
        "skip_wide": (1, width),
        "norm_gain": (1, width),
    }
    places, row = {}, 0
    for name in SMALL_NAMES:
        places[name] = (row, *shapes[name])
        row += shapes[name][0]
    return places, -(-row // 8) * 8


def pack_kernel(places, pre_ref, ker_in_ref, bias_in_ref, ker_st_ref, bias_st_ref, step_ref, decay_ref, skip_ref, norm_ref, out_ref):
    out_ref[...] = jnp.zeros_like(out_ref)
    heads = step_ref.shape[1]
    width = norm_ref.shape[1]
    spread = jnp.where(iota((heads, width), 1) // P_SIZE == iota((heads, width), 0), 1.0, 0.0)
    values = {
        "pre_gain": pre_ref[...],
        "kernel_inner": ker_in_ref[0],
        "bias_inner": bias_in_ref[...],
        "kernel_state": ker_st_ref[0],
        "bias_state": bias_st_ref[...],
        "step_bias": step_ref[...],
        "decay_log": decay_ref[...],
        "skip_wide": high_dot(skip_ref[...], spread, NN),
        "norm_gain": norm_ref[...],
    }
    for name, value in values.items():
        row = places[name][0]
        out_ref[row : row + value.shape[0], 0 : value.shape[1]] = value


def pack(pre_gain, kernel_inner, *rest):
    features = pre_gain.shape[1]
    places, height = small_layout(features, kernel_inner.shape[2], kernel_inner.shape[1])
    args = (pre_gain, kernel_inner, *rest)
    return call(
        partial(pack_kernel, places),
        (),
        grid=(1,),
        in_specs=[pl.BlockSpec(a.shape, lambda i, n=a.ndim: (0,) * n) for a in args],
        out_specs=pl.BlockSpec((height, features), lambda i: (0, 0)),
        out_shape=jax.ShapeDtypeStruct((height, features), F32),
    )(*args)


def choose_kernel(index, places, section_ref, *refs):
    count = 5
    own, other, outs = refs[:count], refs[count : 2 * count], refs[2 * count :]
    for mine in (True, False):

        @pl.when((section_ref[0] == index) == mine)
        def _(source=own if mine else other):
            for k in range(count - 1):
                outs[k][...] = source[k][...]

            @pl.when(pl.program_id(0) == 0)
            def _():
                for name, out in zip(SMALL_NAMES, outs[count - 1 :]):
                    row, high, wide = places[name]
                    out[...] = source[count - 1][row : row + high, 0:wide]


def choose(after, section, index, own, other, width, taps):
    steps = 4
    features = own[0].shape[0]
    places, _ = small_layout(features, width, taps)

    def specs(mine):
        result = []
        for array in own[:-1]:
            shape = (array.shape[0] // steps, array.shape[1])

            def at(i, section_ref):
                used = (section_ref[0] == index) == mine
                return jnp.where(used, i, 0), 0

            result.append(pl.BlockSpec(shape, at))
        result.append(pl.BlockSpec(own[-1].shape, lambda i, section_ref: (0, 0)))
        return result

    out_specs = [
        pl.BlockSpec((a.shape[0] // steps, a.shape[1]), lambda i, section_ref: (i, 0)) for a in own[:-1]
    ]
    out_shape = [jax.ShapeDtypeStruct(a.shape, a.dtype) for a in own[:-1]]
    for name in SMALL_NAMES:
        shape = places[name][1:]
        out_specs.append(pl.BlockSpec(shape, lambda i, section_ref: (0, 0)))
        out_shape.append(jax.ShapeDtypeStruct(shape, F32))
    return call(
        partial(choose_kernel, index, places),
        after,
        grid=(steps,),
        in_specs=[*specs(True), *specs(False)],
        out_specs=out_specs,
        out_shape=out_shape,
        prefetch=1,
    )(section, *own, *other, *after)


def pick_kernel(section_ref, array_ref, *out_refs):
    for m, out_ref in enumerate(out_refs):

        @pl.when(pl.program_id(0) == m)
        def _(out_ref=out_ref):
            out_ref[...] = array_ref[0]


def pick(after, section, array, per):
    _, rows, features = array.shape
    return call(
        pick_kernel,
        after,
        grid=(per,),
        in_specs=[pl.BlockSpec((1, rows, features), lambda i, section_ref: (section_ref[0] * per + i, 0, 0))],
        out_specs=[pl.BlockSpec((rows, features), lambda i, section_ref: (0, 0))] * per,
        out_shape=[jax.ShapeDtypeStruct((rows, features), array.dtype)] * per,
        prefetch=1,
    )(section, array, *after)


def add_kernel(a_ref, b_ref, out_ref):
    out_ref[...] = (a_ref[...].astype(F32) + b_ref[...].astype(F32)).astype(out_ref.dtype)


def add(after, a, b):
    rows, width = a.shape
    steps = 4 if rows % 64 == 0 else 1
    spec = pl.BlockSpec((rows // steps, width), lambda i: (i, 0))
    return call(
        add_kernel,
        after,
        grid=(steps,),
        in_specs=[spec, spec],
        out_specs=spec,
        out_shape=jax.ShapeDtypeStruct(a.shape, a.dtype),
    )(a, b, *after)


def neighbor(array, axis, by):
    length = lax.axis_size(axis)
    pairs = [(i, i + by) for i in range(length) if 0 <= i + by < length]
    return lax.ppermute(array, axis, pairs)


def swap(array):
    return lax.ppermute(array, SECTION, [(0, 1), (1, 0)])


def whole_sum(array, axis):
    length = lax.axis_size(axis)
    by = 1
    while by < length:
        array = array + lax.ppermute(array, axis, [(i, i ^ by) for i in range(length)])
        by *= 2
    return array


class Order:
    def __init__(self):
        self.after = ()

    def wait(self, *arrays):
        self.after = (*self.after, *arrays)

    def __call__(self, result):
        self.after = (result[0] if isinstance(result, (list, tuple)) else result,)
        return result


def shards(
    layer_input, cotangent, pre_gain, proj_zx, proj_bc, proj_dt, kernel_inner, bias_inner,
    kernel_state, bias_state, step_bias, decay_log, skip_gain, norm_gain, proj_out,
):
    section = lax.axis_index(SECTION)
    sections = lax.axis_size(SECTION)
    micro, rows, features = layer_input.shape
    per = micro // sections
    width = norm_gain.shape[1]
    heads = step_bias.shape[1]
    total_width = width * lax.axis_size(HEAD)
    taps = kernel_inner.shape[1]
    chunks = rows // GROUP
    assert lax.axis_size(HEAD) == 4
    place = lax.axis_index(HEAD)
    inner_place = (place == 1) | (place == 2)
    lower = place < 2
    keep = jnp.where(lower, 0, 1).astype(jnp.int32)[None]
    give = 1 - keep
    across = [(1, 2), (2, 1)]
    outward = [(1, 0), (2, 3)]
    order = Order()

    at_place = place.astype(jnp.int32)[None]
    at_seq = lax.axis_index(SEQ).astype(jnp.int32)[None]
    seqs = lax.axis_size(SEQ)
    at_section = section.astype(jnp.int32)[None]

    packed = pack(
        pre_gain, kernel_inner, bias_inner, kernel_state, bias_state, step_bias, decay_log, skip_gain, norm_gain
    )
    own = (
        proj_zx[0].reshape(features, 2 * width),
        proj_bc[0],
        jnp.pad(proj_dt[0], ((0, 0), (0, LANES - heads))),
        proj_out[0],
        packed,
    )
    other = tuple(swap(array) for array in own)

    def layer_weights(index):
        w_wide, w_bc, w_dt, w_out, *rest = order(
            choose(order.after, at_section, index, own, other, width, taps)
        )
        return w_wide, w_bc, w_dt, w_out, dict(zip(SMALL_NAMES, rest))

    span = range(per)
    mine_in = order(pick(order.after, at_section, layer_input, per))

    class Micro:
        pass

    def enter(rows_in, layer):
        t = Micro()
        w_wide, w_bc, w_dt, t.w_out, t.small = layer
        t.layer, t.rows_in = layer, rows_in
        t.gain = t.small["norm_gain"]
        t.normed, t.scale, t.pre, t.pre_st, edge, *rest = order(
            project(order.after, at_place, rows_in, t.small["pre_gain"], w_wide, w_bc, w_dt)
        )
        if rest:
            t.rows_in = rest[0]
        t.edge = neighbor(edge, SEQ, 1)
        return t

    def scan(t, dot):
        t.local, t.kq, t.steps, t.within, t.starts, packed = order(
            scan_forward(order.after, dot, t.pre, t.pre_st, t.edge, t.small)
        )
        t.packed, t.forward = packed, True
        t.arrived = [flip(packed, SEQ, 0)]

    def flip(array, axis, level):
        length = lax.axis_size(axis)
        return lax.ppermute(array, axis, [(i, i ^ (1 << level)) for i in range(length)])

    def pass_on(t):
        level = len(t.arrived)
        if (1 << level) < seqs:
            t.packed = order(
                merge(order.after, at_seq, t.forward, level - 1, t.packed, t.arrived[-1])
            )
            t.arrived.append(flip(t.packed, SEQ, level))
            if (2 << level) < seqs:
                pass_on(t)

    def stats_on(t, name):
        array, got = getattr(t, name)
        total = order(stat_add(order.after, array, got))
        setattr(t, name, [total, flip(total, HEAD, 1)])

    def mix(t, dot, upstream=None):
        args = () if upstream is None else (upstream, t.w_out)
        t.mixer, t.before, stats, *back = order(
            mix_first(order.after, at_seq, dot, t.local, t.pre, t.kq, t.within, t.gain, t.arrived, *args)
        )
        t.back = back[0] if back else None
        t.stats = [stats, flip(stats, HEAD, 0)]

    def out(t, c):
        if c == 0:
            t.owns, t.firsts = [], []
        own = order(
            project_out(order.after, c, t.mixer, t.pre, t.gain, t.stats, t.w_out, total_width)
        )
        t.owns.append(own)
        t.firsts.append(lax.ppermute(own, HEAD, [(0, 1), (3, 2)]))

    def pass_half(t, c, kind=BF16):
        if c == 0:
            t.seconds = []
        given = order(add_half(order.after, give, t.owns[c], t.firsts[c], kind))
        t.seconds.append(lax.ppermute(given, HEAD, across))

    def finish(t, c):
        if c == 0:
            t.pieces, t.halves = [], []
        done = order(
            finish_half(order.after, keep, c, t.owns[c], t.firsts[c], t.seconds[c], t.rows_in)
        )
        t.halves.append((done, lax.ppermute(done, HEAD, across)))

    def spread(t, c):
        joined = order(join(order.after, at_place, *t.halves[c]))
        t.pieces += [joined, lax.ppermute(joined, HEAD, outward)]

    def mix_up(t, products):
        t.grad, t.gate_grad, t.gain_grad, packed, t.normed_out = order(
            mix_back(
                order.after, t.back, t.mixer, t.pre, t.kq, t.within, t.gain, t.stats, products, total_width
            )
        )
        t.packed, t.forward = packed, False
        t.arrived = t.later = [flip(packed, SEQ, 0)]

    def back_start(t, above, total, old):
        t.upstream, t.back, product = order(
            back_first(
                order.after, total, above.rows_in, above.scale, above.small["pre_gain"], old,
                t.w_out, t.mixer, t.pre, t.gain,
            )
        )
        t.products = [product, flip(product, HEAD, 0)]

    def scan_back(t):
        t.inner, edge, t.small_in, t.state, t.small_st, t.raw, t.small_dt = order(
            scan_backward(
                order.after, at_seq, t.pre, t.pre_st, t.edge, t.small, t.kq, t.steps, t.within, t.starts, t.before, t.later, t.grad
            )
        )
        t.edges = neighbor(edge, SEQ, -1)

    def back_out(t, upstream):
        grads, narrow, t.pre_gain_grad, part = order(
            project_back(
                order.after, t.gate_grad, t.inner, t.state, t.raw, t.edges, *t.layer[:3], t.rows_in, t.scale
            )
        )
        t.weights = (t.normed, upstream, grads, narrow, t.normed_out)
        return part

    def scatter_rows(array, axis, ordered=False):
        count = array.shape[0]
        length = lax.axis_size(axis)
        level = length // 2
        while level >= 1:
            high = (lax.axis_index(axis) & level) > 0
            count //= 2
            mine = jnp.where(high, count, 0)
            given = lax.dynamic_slice_in_dim(array, count - mine, count, 0)
            got = lax.ppermute(given, axis, [(i, i ^ level) for i in range(length)])
            own = lax.dynamic_slice_in_dim(array, mine, count, 0)
            array = order(add(order.after, own, got)) if ordered else own + got
            level //= 2
        return array

    dot0, dot1 = split_dot, low_dot
    a, b = span
    share = features // seqs

    layer0 = layer_weights(0)
    f0 = [enter(mine_in[m], layer0) for m in span]
    scan(f0[a], dot0)
    scan(f0[b], dot0)
    pass_on(f0[a])
    mine_back = order(pick(order.after, at_section, cotangent, per))
    pass_on(f0[b])
    mix(f0[a], dot0)
    mix(f0[b], dot0)
    stats_on(f0[a], "stats")
    stats_on(f0[b], "stats")
    order.wait(*f0[a].stats, *f0[b].stats)
    for t in f0:
        for c in range(chunks):
            out(t, c)
    layer1 = layer_weights(1)
    jobs = [(t, c) for t in f0 for c in range(chunks)]
    for k in range(len(jobs) + 2):
        if k < len(jobs):
            pass_half(*jobs[k], WIRE)
        if 0 < k <= len(jobs):
            finish(*jobs[k - 1])
        if k > 1:
            spread(*jobs[k - 2])

    f1 = [enter(f0[a].pieces, layer1)]
    scan(f1[a], dot1)
    f1.append(enter(f0[b].pieces, layer1))
    pass_on(f1[a])
    scan(f1[b], dot1)
    mix(f1[a], dot1, mine_back[a])
    pass_on(f1[b])
    stats_on(f1[a], "stats")
    mix(f1[b], dot1, mine_back[b])
    mix_up(f1[a], ())
    stats_on(f1[b], "stats")
    pass_on(f1[a])
    mix_up(f1[b], ())
    scan_back(f1[a])
    pass_on(f1[b])
    scan_back(f1[b])
    parts = [back_out(f1[m], mine_back[m]) for m in span]
    totals = lax.psum(tuple(parts), HEAD)
    kept1, given1 = order(
        weight_grads(order.after, at_section, [t.weights for t in f1], share)
    )
    parts = order(late_out(order.after, [t.normed_out for t in f1], f1[a].w_out))
    summed1 = order(add(order.after, kept1, swap(given1)))
    reduced1 = lax.psum_scatter(summed1, SEQ, scatter_dimension=0, tiled=True)
    parts = order(hold((*order.after, *totals), parts))
    for m in span:
        back_start(f0[m], f1[m], totals[m], mine_back[m])
    totals1 = lax.psum(tuple(parts), HEAD)
    stats_on(f0[a], "products")
    stats_on(f0[b], "products")
    mix_up(f0[a], f0[a].products)
    mix_up(f0[b], f0[b].products)
    pass_on(f0[a])
    pass_on(f0[b])
    scan_back(f0[a])
    scan_back(f0[b])
    parts = [back_out(f0[m], f0[m].upstream) for m in span]
    kept0, given0 = order(
        weight_grads(order.after, at_section, [t.weights for t in f0], share)
    )
    parts = order(hold((*order.after, *totals1), parts))
    totals = lax.psum(tuple(parts), HEAD)
    given0 = swap(given0)
    outs1 = order(end_out(order.after, totals1, [t.rows_in for t in f1]))
    reduced0 = scatter_rows(order(add(order.after, kept0, given0)), SEQ, True)
    outs0 = [t.rows_in for t in f1]
    sents1 = [t.upstream for t in f0]

    def exchange(first, second):
        got_first = [lax.ppermute(x, SECTION, [(1, 0)]) for x in first]
        got_second = [lax.ppermute(x, SECTION, [(0, 1)]) for x in second]
        return got_first, got_second

    sents0 = [
        order(
            end_back(
                order.after, totals[m], f0[m].rows_in, f0[m].scale, f0[m].small["pre_gain"], f0[m].upstream
            )
        )
        for m in span
    ]
    got2, got3 = exchange(outs0, outs1)
    got0, got1 = exchange(sents0, sents1)
    layer_out = order(
        place_layers(order.after, at_section, outs0, got2, outs1, got3)
    )
    reduced = [reduced0, reduced1]
    kept = jnp.where(section == 0, reduced[0], reduced[1])
    moved = swap(jnp.where(section == 0, reduced[1], reduced[0]))
    weights = jnp.where(
        section == 0,
        jnp.concatenate([kept, moved], axis=0),
        jnp.concatenate([moved, kept], axis=0),
    ).astype(F32)
    grad_zx = weights[:, : 2 * width].reshape(share, 2, width)
    grad_bc = scatter_rows(weights[:, 2 * width : 2 * width + 2 * NS], HEAD)
    grad_dt = weights[:, 2 * width + 2 * NS : 2 * width + 2 * NS + heads]
    grad_out = weights[:, 2 * width + 2 * NS + LANES :].T

    def collect_smalls(tasks):
        names = ("small_in", "gain_grad", "small_dt", "small_st", "pre_gain_grad")
        return jnp.concatenate(
            [sum(getattr(t, name) for t in tasks).reshape(-1, LANES) for name in names], axis=0
        )

    joined = [collect_smalls(f0), collect_smalls(f1)]
    smalls = jnp.where(section == 0, joined[0], joined[1]) + swap(
        jnp.where(section == 0, joined[1], joined[0])
    )
    smalls = whole_sum(smalls, SEQ)
    inner_rows = 8 * width // LANES
    gain_rows = width // LANES
    at = 0
    small_in = smalls[at : at + inner_rows].reshape(8, width)
    at += inner_rows
    gain_grad = smalls[at : at + gain_rows].reshape(width)
    at += gain_rows
    small_dt = smalls[at : at + 8]
    at += 8
    shared = whole_sum(smalls[at:], HEAD)
    small_st = shared[: 8 * 2 * NS // LANES].reshape(8, 2 * NS)
    grad_pre = shared[8 * 2 * NS // LANES :].reshape(features)
    grad_pre = lax.dynamic_slice_in_dim(grad_pre, lax.axis_index(SEQ) * share, share, 0)
    parts = seqs * lax.axis_size(HEAD)
    st_width = 2 * NS // parts
    st_at = (lax.axis_index(SEQ) * lax.axis_size(HEAD) + lax.axis_index(HEAD)) * st_width
    small_st = lax.dynamic_slice_in_dim(small_st, st_at, st_width, 1)
    grads = [
        grad_pre[None],
        grad_zx[None],
        grad_bc[None],
        grad_dt[None],
        small_in[None, :taps],
        small_in[None, taps],
        small_st[None, :taps],
        small_st[None, taps],
        small_dt[None, 0, :heads],
        small_dt[None, 1, :heads],
        small_in[None, taps + 1].reshape(1, heads, P_SIZE).sum(axis=2),
        gain_grad[None],
        grad_out[None],
    ]
    order.wait(grad_bc)
    layer_grad = order(
        place_layers(order.after, at_section, sents0, got0, sents1, got1)
    )

    return (layer_out[None], layer_grad[None], *grads)


def solution(mesh):
    return jax.shard_map(
        shards,
        mesh=mesh,
        in_specs=(
            P(None, SEQ, None),
            P(None, SEQ, None),
            P(SECTION, None),
            P(SECTION, None, None, HEAD),
            P(SECTION, None, None),
            P(SECTION, None, HEAD),
            P(SECTION, None, HEAD),
            P(SECTION, HEAD),
            P(SECTION, None, None),
            P(SECTION, None),
            P(SECTION, HEAD),
            P(SECTION, HEAD),
            P(SECTION, HEAD),
            P(SECTION, HEAD),
            P(SECTION, HEAD, None),
        ),
        out_specs=(
            P(SECTION, None, SEQ, None),
            P(SECTION, None, SEQ, None),
            P(SECTION, SEQ),
            P(SECTION, SEQ, None, HEAD),
            P(SECTION, (SEQ, HEAD), None),
            P(SECTION, SEQ, HEAD),
            P(SECTION, None, HEAD),
            P(SECTION, HEAD),
            P(SECTION, None, (SEQ, HEAD)),
            P(SECTION, (SEQ, HEAD)),
            P(SECTION, HEAD),
            P(SECTION, HEAD),
            P(SECTION, HEAD),
            P(SECTION, HEAD),
            P(SECTION, HEAD, SEQ),
        ),
        check_vma=False,
    )
```
